32 devices in a mesh: narrow: 4 (over y, x), wide: 8 (over z, core).
Axes of the slice: x: 2, y: 2, z: 4, core: 2. Of those that a mesh axis runs over, the one named last changes fastest.
Arguments:
- tokens: bfloat16 [8, 2, 1024, 768], P('wide', None, 'narrow'), may hold values from -6 to 6
- lengths: int32 [8], P('wide'), may hold values from 128 to 1024, as said below
- w_qkv: bfloat16 [2, 768, 2304], P(None, 'narrow'), may hold values from -0.21875 to 0.21875
- w_out: bfloat16 [2, 768, 768], P(None, 'narrow'), may hold values from -1.5 to 1.5
- w_up: bfloat16 [2, 768, 3072], P(None, 'narrow'), may hold values from -0.21875 to 0.21875
- w_down: bfloat16 [2, 3072, 768], P(None, 'narrow'), may hold values from -0.109375 to 0.109375
- norm_gains: bfloat16 [2, 2, 768], P(None, None, 'narrow'), may hold values from 0.099609375 to 1.8984375
- norm_biases: bfloat16 [2, 2, 768], P(None, None, 'narrow'), may hold values from -2 to 2
- cotangent: bfloat16 [8, 2, 1024, 768], P('wide', None, 'narrow'), may hold values from -6 to 6
Outputs:
- result: bfloat16 [8, 2, 1024, 768], P('wide', None, 'narrow')
- grad_tokens: bfloat16 [8, 2, 1024, 768], P('wide', None, 'narrow')
- grad_qkv: float32 [2, 768, 2304], P(None, 'narrow')
- grad_out: float32 [2, 768, 768], P(None, 'narrow')
- grad_up: float32 [2, 768, 3072], P(None, 'narrow')
- grad_down: float32 [2, 3072, 768], P(None, 'narrow')
- grad_gains: float32 [2, 2, 768], P(None, None, 'narrow')
- biases_first: float32 [2, 768], P(None, 'narrow')
- biases_second: float32 [2, 768], P(None, 'narrow')
The draws below stay inside these ranges and needn't reach their ends.
Inputs may be any that keep to these rules, and one draw needn't show every extreme that they name: `lengths`: each length is a multiple of 16; some row has exactly 1024 and some exactly 128.
All inputs are finite; a program needn't handle non-finite values.
Results may differ from the reference program's by a relative error of at most 0.019.
Values may be sent and summed in bfloat16 or wider, within the bound.
A program may use at most 256 MiB of HBM per device.

```python
import jax
import jax.numpy as jnp
from jax import lax

D = 768
H = 12
HD = 64
FF = 3072
LMAX = 1024
LMIN = 128
BLOCK = 16
LAYERS = 2
ROWS = 8


def draw_lengths(key, part):
    first, second = jax.random.split(key)
    blocks = jax.random.randint(first, (ROWS,), LMIN // BLOCK, LMAX // BLOCK + 1)
    picks = jax.random.permutation(second, ROWS)
    lengths = blocks * BLOCK
    lengths = lengths.at[picks[0]].set(LMAX)
    lengths = lengths.at[picks[1]].set(LMIN)
    return lengths.astype(jnp.int32)


def level_of(stream_key, shape, cuts, least, largest):
    level = 1.0
    for dim, shards_of in cuts:
        steps = jax.random.uniform(jax.random.fold_in(jax.random.fold_in(stream_key, 6), dim), (shards_of,), jnp.float32, least / len(cuts), largest / len(cuts))
        level = level * jnp.repeat(jnp.exp(steps), shape[dim] // shards_of).reshape((-1,) + (1,) * (len(shape) - 1 - dim))
    return level


def bell_draw(key, dims, scale, reach, pieces=(), held_as=jnp.bfloat16):
    entries = scale * jax.random.normal(key, dims, jnp.float32)
    if pieces:
        entries = entries * level_of(key, dims, pieces, -0.22, 0.18)
    return jnp.clip(entries, -reach, reach).astype(held_as)


def setup_inputs(seed: int = 0) -> dict:
    splits = jax.random.split(jax.random.key(seed), 10)
    tokens = bell_draw(splits[0], (ROWS, 2, LMAX, D), 1.0, 6.0, ((0, 8), (2, 4)))
    lengths = draw_lengths(jax.random.fold_in(splits[9], 71), 0)
    w_qkv = bell_draw(splits[2], (LAYERS, D, 3 * D), D ** -0.5, 0.21875, ((1, 4),))
    w_out = bell_draw(splits[3], (LAYERS, D, D), (max(D // 48, 1)) ** -0.5, 1.5, ((1, 4),))
    w_up = bell_draw(splits[4], (LAYERS, D, FF), D ** -0.5, 0.21875, ((1, 4),))
    w_down = bell_draw(splits[5], (LAYERS, FF, D), FF ** -0.5, 0.109375, ((1, 4),))
    norm_gains = jnp.clip(1.0 + 0.18 * jax.random.normal(splits[6], (LAYERS, 2, D), jnp.float32), 0.099609375, 1.8984375).astype(jnp.bfloat16)
    norm_biases = bell_draw(splits[7], (LAYERS, 2, D), 0.3, 2.0, ((2, 4),))
    cotangent = bell_draw(splits[8], (ROWS, 2, LMAX, D), 1.0, 6.0, ((0, 8), (2, 4)))
    return {"tokens": tokens, "lengths": lengths, "w_qkv": w_qkv, "w_out": w_out, "w_up": w_up, "w_down": w_down, "norm_gains": norm_gains, "norm_biases": norm_biases, "cotangent": cotangent}


@jax.custom_vjp
def low(v):
    return lax.optimization_barrier(v.astype(jnp.bfloat16)).astype(jnp.float32)

@jax.custom_vjp
def low_back(v):
    return v

def low_keep(v):
    return (low(v), None)

def low_pass(kept, grad):
    return (grad,)

def back_keep(v):
    return (v, None)

def back_low(kept, grad):
    return (low(grad),)
low.defvjp(low_keep, low_pass)
low_back.defvjp(back_keep, back_low)

def norm_rows(hidden, gain, bias):
    mean = lax.optimization_barrier(jnp.mean(hidden, axis=-1, keepdims=True))
    centred = hidden - mean
    variance = lax.optimization_barrier(jnp.mean(centred * centred, axis=-1, keepdims=True))
    return centred * lax.rsqrt(variance + 1e-05) * gain + bias

def rotate(values, positions):
    half = values.shape[-1] // 2
    freq = jnp.exp(-jnp.log(10000.0) * jnp.arange(half, dtype=jnp.float32) * 2.0 / values.shape[-1])
    angle = positions.astype(jnp.float32)[:, None] * freq[None, :]
    cosine = jnp.cos(angle)[:, None, :]
    sine = jnp.sin(angle)[:, None, :]
    first = values[..., :half]
    second = values[..., half:]
    return jnp.concatenate([first * cosine - second * sine, second * cosine + first * sine], axis=-1)

def allowed(query_index, key_index):
    query_clean = (query_index >= LMAX)[:, None]
    key_clean = (key_index >= LMAX)[None, :]
    query_block = (query_index % LMAX // BLOCK)[:, None]
    key_block = (key_index % LMAX // BLOCK)[None, :]
    noisy_rule = jnp.where(key_clean, key_block < query_block, key_block == query_block)
    clean_rule = key_clean & (key_block <= query_block)
    return jnp.where(query_clean, clean_rule, noisy_rule)

def row_forward(hidden, w_qkv, w_out, w_up, w_down, gains, biases):
    highest = lax.Precision.HIGHEST
    total = 2 * LMAX
    positions = jnp.arange(total, dtype=jnp.int32) % LMAX
    block_rows = min(512, total)
    scale = HD ** (-0.5)
    key_index = jnp.arange(total, dtype=jnp.int32)
    for layer in range(LAYERS):
        first = low(norm_rows(hidden, gains[layer, 0], biases[layer, 0]))
        mixed = low_back(jnp.dot(first, w_qkv[layer], precision=highest)).reshape(total, 3, H, HD)
        query = low(rotate(mixed[:, 0], positions))
        key = low(rotate(mixed[:, 1], positions))
        value = low(mixed[:, 2])

        def one_block(query_part, start):
            rows_here = start + jnp.arange(block_rows, dtype=jnp.int32)
            score = low_back(jnp.einsum('qhd,khd->hqk', query_part, key, precision=highest) * scale)
            score = jnp.where(allowed(rows_here, key_index)[None], score, -jnp.inf)
            probs = low(jax.nn.softmax(score, axis=-1))
            return jnp.einsum('hqk,khd->qhd', probs, value, precision=highest)
        checked = jax.checkpoint(one_block)
        starts = jnp.arange(0, total, block_rows, dtype=jnp.int32)
        blocks = lax.map(lambda pair: checked(pair[0], pair[1]), (query.reshape(total // block_rows, block_rows, H, HD), starts))
        context = low(low_back(blocks.reshape(total, D)))
        hidden = hidden + low_back(jnp.dot(context, w_out[layer], precision=highest))
        second = low(norm_rows(hidden, gains[layer, 1], biases[layer, 1]))
        upper = low_back(jnp.dot(second, w_up[layer], precision=highest))
        active = low(jax.nn.gelu(upper, approximate=True))
        hidden = hidden + low_back(jnp.dot(active, w_down[layer], precision=highest))
    return hidden

def reference(tokens, lengths, w_qkv, w_out, w_up, w_down, norm_gains, norm_biases, cotangent):
    weights = (w_qkv.astype(jnp.float32), w_out.astype(jnp.float32), w_up.astype(jnp.float32), w_down.astype(jnp.float32), norm_gains.astype(jnp.float32), norm_biases.astype(jnp.float32))
    total = 2 * LMAX

    def one_row(carry, item):
        row_tokens, row_cot, length = item
        inputs = row_tokens.reshape(total, D).astype(jnp.float32)
        valid = (jnp.arange(total, dtype=jnp.int32) % LMAX < length).astype(jnp.float32)
        out_grad = row_cot.reshape(total, D).astype(jnp.float32) * valid[:, None]
        output, pull = jax.vjp(row_forward, inputs, *weights)
        grads = pull(out_grad)
        summed = tuple((c + g for c, g in zip(carry, grads[1:])))
        return (summed, (output.astype(jnp.bfloat16), grads[0].astype(jnp.bfloat16)))
    start = tuple((jnp.zeros(w.shape, jnp.float32) for w in weights))
    sums, (outputs, input_grads) = lax.scan(one_row, start, (tokens, cotangent, lengths))
    return (outputs.reshape(tokens.shape), input_grads.reshape(tokens.shape), sums[0], sums[1], sums[2], sums[3], sums[4], sums[5][:, 0], sums[5][:, 1])
```

```python
from functools import partial

import jax
import jax.numpy as jnp
from jax import lax
from jax.experimental import pallas as pl
from jax.experimental.pallas import tpu as pltpu
from jax.sharding import PartitionSpec as P

H = 12
BLOCK = 16
NEG = -1e30
EPS = 1e-05
MESH = pl.DeviceIdType.MESH
F32 = jnp.float32
BF16 = jnp.bfloat16
GELU_C = 0.7978845608028654
GELU_A = 0.044715


def dot(a, b):
    return jnp.dot(a, b, preferred_element_type=F32)


def dot_nt(a, b):
    return lax.dot_general(a, b, (((1,), (1,)), ((), ())), preferred_element_type=F32)


def dot_tn(a, b):
    return lax.dot_general(a, b, (((0,), (0,)), ((), ())), preferred_element_type=F32)


def tile_at(index, size):
    return pl.ds(pl.multiple_of(index * size, size), size)


def loop(count, body):
    lax.fori_loop(0, count, lambda i, _: (body(i), None)[1], None)


def swap_halves(x, first):
    return jnp.where(first, pltpu.roll(x, 96, 1), pltpu.roll(x, 32, 1))


def lane_masks(rows):
    lane = lax.broadcasted_iota(jnp.int32, (rows, 128), 1)
    return lane % 64 < 32


def head_masks():
    lane = lax.broadcasted_iota(jnp.int32, (1, 128), 1)
    low = (lane < 64).astype(F32)
    return low, 1.0 - low


def norm_into(src, dst, gain, bias, rows):
    step = 32

    def body(i):
        at = tile_at(i, step)
        x = src[at, :].astype(F32)
        c = x - jnp.mean(x, axis=-1, keepdims=True)
        inv = lax.rsqrt(jnp.mean(c * c, axis=-1, keepdims=True) + EPS)
        dst[at, :] = (c * inv * gain + bias).astype(BF16)

    loop(rows // step, body)


class Gather:
    def __init__(self, here, shard, full, send, recv, base, lsem):
        self.n, self.w = here
        self.core = lax.rem(self.w, 2)
        self.shard, self.full, self.send, self.recv, self.base, self.lsem = (
            shard, full, send, recv, base, lsem)
        self.rows = shard.shape[0]
        self.half = self.rows // 2
        self.quarter = self.rows // 4
        self.x, self.y, self.d, self.s = (
            (self.n ^ 1, self.w), (self.n ^ 2, self.w), (self.n ^ 3, self.w), (self.n, self.w ^ 1))

    def region(self, owner, core, quarter=None):
        start = owner * self.rows + core * self.half
        if quarter is None:
            return self.full.at[pl.ds(pl.multiple_of(start, 16), self.half)]
        return self.full.at[pl.ds(pl.multiple_of(start + quarter * self.quarter, 16), self.quarter)]

    def copy(self, slot, src, dst, device):
        k = self.base + slot
        return pltpu.make_async_remote_copy(
            src_ref=src, dst_ref=dst, send_sem=self.send.at[k], recv_sem=self.recv.at[k],
            device_id=device, device_id_type=MESH)

    def own(self):
        return pltpu.make_async_copy(
            self.shard, self.full.at[pl.ds(pl.multiple_of(self.n * self.rows, 16), self.rows)], self.lsem)

    def plain(self, slot, region, device):
        return self.copy(slot, region, region, device)

    def issue(self):
        src = self.shard.at[pl.ds(pl.multiple_of(self.core * self.half, 16), self.half)]
        dst = self.region(self.n, self.core)
        self.copy(0, src, dst, self.x).start()
        self.copy(1, src, dst, self.y).start()
        self.own().start()

    def forward(self):
        nx, ny = self.x[0], self.y[0]
        self.plain(0, self.region(nx, self.core), self.x).wait_recv()
        self.plain(2, self.region(nx, self.core, 0), self.y).start()
        self.plain(4, self.region(nx, self.core), self.s).start()
        self.plain(1, self.region(ny, self.core), self.y).wait_recv()
        self.plain(3, self.region(ny, self.core, 1), self.x).start()
        self.plain(5, self.region(ny, self.core), self.s).start()

    def finish(self):
        nd = self.d[0]
        self.plain(2, self.region(nd, self.core, 0), self.y).wait_recv()
        self.plain(3, self.region(nd, self.core, 1), self.x).wait_recv()
        self.plain(6, self.region(nd, self.core), self.s).start()

    def use(self):
        other = 1 - self.core
        for slot, who in ((4, self.x), (5, self.y), (6, self.d)):
            self.plain(slot, self.region(who[0], other), self.s).wait_recv()
        self.own().wait()

    def drain(self):
        src = self.shard.at[pl.ds(pl.multiple_of(self.core * self.half, 16), self.half)]
        dst = self.region(self.n, self.core)
        self.copy(0, src, dst, self.x).wait_send()
        self.copy(1, src, dst, self.y).wait_send()
        nx, ny, nd = self.x[0], self.y[0], self.d[0]
        self.plain(2, self.region(nx, self.core, 0), self.y).wait_send()
        self.plain(3, self.region(ny, self.core, 1), self.x).wait_send()
        self.plain(4, self.region(nx, self.core), self.s).wait_send()
        self.plain(5, self.region(ny, self.core), self.s).wait_send()
        self.plain(6, self.region(nd, self.core), self.s).wait_send()


def forward_kernel(
    layers,
    tok, prm, cosr, sinr, bias_c, bias_n, wq, wo, wu, wd,
    result, fq, fo, fu, fd, prm_out, h_out, q_out, nkv_out, kv_out, lse_out, ctx_out, mid_out, u_out,
    gq, go, gu, gd, prm_buf, par, hid, a, q, nkv, kv, score, top, lse, ctx, mid, u, act,
    send, recv, lsem, psend, precv, ksend, krecv, ssem,
):
    n = lax.axis_index("narrow")
    w = lax.axis_index("wide")
    rows, width = tok.shape
    share = rows // 2
    group = share
    pairs = width // 128
    ff = wu.shape[2]
    peers = ((n ^ 1, w), (n ^ 2, w), (n ^ 3, w))

    barrier = pltpu.get_barrier_semaphore()
    for device in peers + ((n, w ^ 1),):
        pl.semaphore_signal(barrier, inc=1, device_id=device, device_id_type=MESH)
    pl.semaphore_wait(barrier, 4)

    tensors = []
    for layer in range(layers):
        for kind, (shard, full) in enumerate(((wq, gq), (wo, go), (wu, gu), (wd, gd))):
            k = layer * 4 + kind
            tensors.append(Gather((n, w), shard.at[layer], full.at[layer], send, recv, 7 * k, lsem.at[k]))

    def params(i):
        return pltpu.make_async_remote_copy(
            src_ref=prm, dst_ref=prm_buf.at[i], send_sem=psend.at[i], recv_sem=precv.at[i],
            device_id=peers[i], device_id_type=MESH)

    def share_kv(layer, i):
        region = kv.at[layer, tile_at(n, share)]
        return pltpu.make_async_remote_copy(
            src_ref=region, dst_ref=region, send_sem=ksend.at[3 * layer + i],
            recv_sem=krecv.at[3 * layer + i], device_id=peers[i], device_id_type=MESH)

    def recv_kv(layer, i):
        region = kv.at[layer, tile_at(peers[i][0], share)]
        return pltpu.make_async_remote_copy(
            src_ref=region, dst_ref=region, send_sem=ksend.at[3 * layer + i],
            recv_sem=krecv.at[3 * layer + i], device_id=peers[i], device_id_type=MESH)

    gives = (n % 2 == 0, n < 2, n < 2)
    takes = (n % 2 == 1, n >= 2, n >= 2)

    for i in range(3):
        params(i).start()
    tensors[0].issue()
    tensors[1].issue()

    def saves(layer):
        pieces = [
            (q, q_out.at[layer]), (nkv, nkv_out.at[layer]), (kv.at[layer], kv_out.at[layer]),
            (lse, lse_out.at[layer]), (ctx, ctx_out.at[layer]), (mid, mid_out.at[layer]), (u, u_out.at[layer]),
            (hid, h_out.at[layer]),
        ]
        return [pltpu.make_async_copy(s, d, ssem.at[layer * 8 + k]) for k, (s, d) in enumerate(pieces)]

    def weight_saves():
        pieces = ((gq, fq), (go, fo), (gu, fu), (gd, fd))
        out = []
        for layer in range(layers):
            for kind, (s, d) in enumerate(pieces):
                k = layer * 4 + kind
                out.append(pltpu.make_async_copy(s.at[layer], d.at[layer], ssem.at[8 * layers + k]))
        return out

    for i in range(3):
        params(i).wait_recv()
    par[...] = prm[...] + prm_buf[0] + prm_buf[1] + prm_buf[2]
    prm_out[...] = par[...]

    first = lane_masks(rows)
    masks = head_masks()
    lanes = lax.broadcasted_iota(jnp.int32, (rows, 128), 1)

    for layer in range(layers):
        t_qkv, t_out, t_up, t_down = tensors[4 * layer:4 * layer + 4]
        later = tensors[4 * layer + 4:]
        gain1, gain2 = par[2 * layer:2 * layer + 1, :], par[2 * layer + 1:2 * layer + 2, :]
        at = 2 * layers + 2 * layer
        bias1, bias2 = par[at:at + 1, :], par[at + 1:at + 2, :]
        saved = saves(layer)
        before = saves(layer - 1) if layer else None
        if layer == 0:
            norm_into(tok, a, gain1, bias1, rows)
        else:
            norm_into(hid, a, gain1, bias1, rows)
        if layer == 0:
            t_qkv.forward()
        t_qkv.finish()
        t_qkv.use()
        if before:
            before[0].wait()
            before[1].wait()

        wqkv = gq.at[layer]

        def query_tile(j):
            x = dot(a[...], wqkv[:, tile_at(j, 256)])
            for part in range(2):
                v = x[:, 128 * part:128 * part + 128]
                v = v * cosr[...] + swap_halves(v, first) * sinr[...]
                q[:, tile_at(2 * j + part, 128)] = (v.astype(BF16).astype(F32) * 0.125).astype(BF16)

        def key_tile(j):
            x = dot(a[...], wqkv[:, tile_at(j + 3, 256)])
            for part in range(2):
                v = x[:, 128 * part:128 * part + 128]
                v = (v * cosr[...] + swap_halves(v, first) * sinr[...]).astype(BF16)
                nkv[:, tile_at(2 * j + part, 128)] = v[:share]
                kv[layer, tile_at(n, share), tile_at(2 * j + part, 128)] = v[share:]

        def value_tile(j):
            v = dot(a[...], wqkv[:, tile_at(j + 6, 256)]).astype(BF16)
            nkv[:, tile_at(j + 3, 256)] = v[:share]
            kv[layer, tile_at(n, share), tile_at(j + 3, 256)] = v[share:]

        loop(3, key_tile)
        loop(3, value_tile)
        for i in range(3):
            @pl.when(gives[i])
            def _():
                share_kv(layer, i).start()
        loop(3, query_tile)
        saved[0].start()
        saved[1].start()
        t_out.forward()
        t_up.issue()
        t_down.issue()
        for i in range(3):
            @pl.when(takes[i])
            def _():
                recv_kv(layer, i).wait_recv()
        saved[2].start()
        if before:
            before[3].wait()
            before[4].wait()

        def pair_step(pair):
            at_pair = tile_at(pair, 128)
            at_value = tile_at(pair + pairs, 128)
            q2 = q[:, at_pair].astype(F32)
            outs = []
            for h in range(2):
                qm = (q2 * masks[h]).astype(BF16)
                s = dot_nt(qm, kv[layer, tile_at(n, group), at_pair]) + bias_c[...]
                score[:, tile_at(n, group)] = s
                top[...] = jnp.maximum(s[:, :128], s[:, 128:])
                s = dot_nt(qm[:share], nkv[:, at_pair]) + bias_n[...]
                score[:share, 4 * group:5 * group] = s
                top[:share] = jnp.maximum(top[:share], jnp.maximum(s[:, :128], s[:, 128:]))

                def scores_of(g):
                    s = dot_nt(qm, kv[layer, tile_at(g, group), at_pair])
                    score[:, tile_at(g, group)] = s
                    top[...] = jnp.maximum(top[...], jnp.maximum(s[:, :128], s[:, 128:]))

                loop(n, scores_of)
                most = jnp.max(top[...], axis=-1, keepdims=True)
                p = jnp.exp(score[:share, 4 * group:5 * group] - most[:share])
                part = p[:, :128] + p[:, 128:]
                add = dot(p.astype(BF16), nkv[:, at_value])
                zeros = jnp.zeros((share, 128), F32)

                def probs_of(g, carry):
                    total, out = carry
                    p = jnp.exp(score[:, tile_at(g, group)] - most)
                    total = total + p[:, :128] + p[:, 128:]
                    out = out + dot(p.astype(BF16), kv[layer, tile_at(g, group), at_value])
                    return total, out

                total, out = lax.fori_loop(
                    0, n + 1, probs_of,
                    (jnp.concatenate([part, zeros], axis=0), jnp.concatenate([add, zeros], axis=0)))
                total = jnp.sum(total, axis=-1, keepdims=True)
                outs.append(out * (masks[h] / total))
                lse[...] = jnp.where(lanes == 2 * pair + h, most + jnp.log(total), lse[...])
            ctx[:, at_pair] = (outs[0] + outs[1]).astype(BF16)

        loop(pairs, pair_step)
        saved[3].start()
        saved[4].start()
        t_out.finish()
        t_out.use()
        t_up.forward()
        if later:
            later[0].issue()
            later[1].issue()
        if before:
            before[5].wait()
            before[6].wait()
            before[7].wait()

        def out_tile(j):
            at = tile_at(j, 256)
            base = (tok if layer == 0 else hid)[:, at].astype(F32)
            mid[:, at] = base + dot(ctx[...], go[layer, :, at])

        loop(width // 256, out_tile)
        saved[5].start()
        norm_into(mid, a, gain2, bias2, rows)
        t_up.finish()
        t_up.use()

        def up_tile(j):
            at = tile_at(j, 256)
            x = dot(a[...], gu[layer, :, at])
            u[:, at] = x
            t = jnp.tanh(GELU_C * (x + GELU_A * (x * x * x)))
            act[:, at] = (0.5 * x * (1.0 + t)).astype(BF16)

        loop(ff // 256, up_tile)
        saved[6].start()
        t_down.forward()
        if later:
            later[0].forward()
        t_down.finish()
        t_down.use()

        def down_tile(j):
            at = tile_at(j, 256)
            out = mid[:, at] + dot(act[...], gd[layer, :, at])
            hid[:, at] = out
            if layer == layers - 1:
                result[:, at] = out.astype(BF16)

        loop(width // 256, down_tile)
        saved[7].start()

    for c in weight_saves():
        c.start()
    for c in saves(layers - 1):
        c.wait()
    for layer in range(layers - 1):
        saves(layer)[2].wait()
    for c in weight_saves():
        c.wait()
    for t in tensors:
        t.drain()
    for i in range(3):
        params(i).wait_send()
        for layer in range(layers):
            @pl.when(gives[i])
            def _():
                share_kv(layer, i).wait_send()


def forward(tokens, prm, cosr, sinr, bias_c, bias_n, w_qkv, w_out, w_up, w_down):
    rows, width = tokens.shape
    share = rows // 2
    layers = w_qkv.shape[0]
    seq = share * 4
    qw, ff = w_qkv.shape[2], w_up.shape[2]
    full = [
        jax.ShapeDtypeStruct((layers, width, qw), BF16),
        jax.ShapeDtypeStruct((layers, width, width), BF16),
        jax.ShapeDtypeStruct((layers, width, ff), BF16),
        jax.ShapeDtypeStruct((layers, ff, width), BF16),
    ]
    hbm = pl.BlockSpec(memory_space=pltpu.HBM)
    vmem = pl.BlockSpec(memory_space=pltpu.VMEM)
    shape = jax.ShapeDtypeStruct
    kept = [
        shape((layers, rows, width), F32),
        shape((layers, rows, width), BF16),
        shape((layers, share, 2 * width), BF16),
        shape((layers, seq, 2 * width), BF16),
        shape((layers, rows, 128), F32),
        shape((layers, rows, width), BF16),
        shape((layers, rows, width), F32),
        shape((layers, rows, ff), F32),
    ]
    dma, count = pltpu.SemaphoreType.DMA, 7 * 4 * layers
    return pl.pallas_call(
        partial(forward_kernel, layers),
        out_shape=[shape((rows, width), BF16)] + full + [shape(prm.shape, F32)] + kept,
        in_specs=[vmem] * 6 + [hbm] * 4,
        out_specs=[vmem] + [hbm] * 4 + [vmem] + [hbm] * 8,
        scratch_shapes=[pltpu.VMEM(f.shape, BF16) for f in full] + [
            pltpu.VMEM((3,) + prm.shape, F32),
            pltpu.VMEM(prm.shape, F32),
            pltpu.VMEM((rows, width), F32),
            pltpu.VMEM((rows, width), BF16),
            pltpu.VMEM((rows, width), BF16),
            pltpu.VMEM((share, 2 * width), BF16),
            pltpu.VMEM((layers, seq, 2 * width), BF16),
            pltpu.VMEM((rows, seq + share), F32),
            pltpu.VMEM((rows, 128), F32),
            pltpu.VMEM((rows, 128), F32),
            pltpu.VMEM((rows, width), BF16),
            pltpu.VMEM((rows, width), F32),
            pltpu.VMEM((rows, ff), F32),
            pltpu.VMEM((rows, ff), BF16),
            dma((count,)), dma((count,)), dma((4 * layers,)),
            dma((3,)), dma((3,)), dma((3 * layers,)), dma((3 * layers,)),
            dma((8 * layers + 4 * layers,)),
        ],
        compiler_params=pltpu.CompilerParams(
            collective_id=0, has_side_effects=True, vmem_limit_bytes=62 * 2**20),
        cost_estimate=pl.CostEstimate(flops=20 * 10**9, bytes_accessed=10**8, transcendentals=10**7),
        name="forward",
    )(tokens, prm, cosr, sinr, bias_c, bias_n, w_qkv, w_out, w_up, w_down)


def shared_params(norm_gains, norm_biases):
    layers, _, part = norm_gains.shape
    mine = jnp.concatenate([norm_gains.reshape(2 * layers, part), norm_biases.reshape(2 * layers, part)]).astype(F32)
    parts = lax.axis_size("narrow")
    owner = jnp.arange(parts) == lax.axis_index("narrow")
    return jnp.where(owner[None, :, None], mine[:, None, :], 0.0).reshape(4 * layers, parts * part)


def attend_tables(share, head_dim):
    local = lax.axis_index("narrow") * share + jnp.arange(share, dtype=jnp.int32)
    half = head_dim // 2
    freq = jnp.exp(-jnp.log(10000.0) * jnp.arange(half, dtype=F32) * 2.0 / head_dim)
    angle = local.astype(F32)[:, None] * freq[None, :]
    cosine, sine = jnp.cos(angle), jnp.sin(angle)
    cosr = jnp.tile(jnp.concatenate([cosine, cosine], axis=1), (2, 2))
    sinr = jnp.tile(jnp.concatenate([-sine, sine], axis=1), (2, 2))
    block = jnp.arange(share, dtype=jnp.int32) // BLOCK
    same = block[:, None] == block[None, :]
    below = block[None, :] < block[:, None]
    bias = lambda allow: jnp.where(allow, 0.0, NEG).astype(F32)
    return cosr, sinr, jnp.concatenate([bias(below), bias(below | same)]), bias(same)


def norm_rows(hidden, gain, bias):
    mean = jnp.mean(hidden, axis=-1, keepdims=True)
    centred = hidden - mean
    inverse = lax.rsqrt(jnp.mean(centred * centred, axis=-1, keepdims=True) + 1e-05)
    return (centred * inverse * gain + bias, centred * inverse, inverse)


def norm_back(grad, normed, inverse, gain):
    scaled = grad * gain
    inner = (
        scaled
        - jnp.mean(scaled, axis=-1, keepdims=True)
        - normed * jnp.mean(scaled * normed, axis=-1, keepdims=True)
    )
    return (inverse * inner, jnp.sum(grad * normed, axis=0), jnp.sum(grad, axis=0))


def tables(positions, width):
    half = width // 2
    freq = jnp.exp(-jnp.log(10000.0) * jnp.arange(half, dtype=jnp.float32) * 2.0 / width)
    angle = positions.astype(jnp.float32)[:, None] * freq[None, :]
    return (jnp.cos(angle)[:, None, :], jnp.sin(angle)[:, None, :])


def rotate(values, cosine, sine):
    half = values.shape[-1] // 2
    first = values[..., :half]
    second = values[..., half:]
    return jnp.concatenate(
        [first * cosine - second * sine, second * cosine + first * sine], axis=-1
    )


def rotate_back(values, cosine, sine):
    half = values.shape[-1] // 2
    first = values[..., :half]
    second = values[..., half:]
    return jnp.concatenate(
        [first * cosine + second * sine, second * cosine - first * sine], axis=-1
    )


def outer_sum(left, right):
    return lax.dot_general(
        left, right, (((0,), (0,)), ((), ())), preferred_element_type=jnp.float32
    )


def times_back(left, weight):
    return lax.dot_general(
        left, weight, (((1,), (1,)), ((), ())), preferred_element_type=jnp.float32
    )


def safe_top(values):
    return jnp.where(jnp.isfinite(values), values, 0.0)


def on_device(tokens, lengths, w_qkv, w_out, w_up, w_down, norm_gains, norm_biases, cotangent):
    rows, _, share, width = tokens.shape
    parts = lax.axis_size("narrow")
    here = lax.axis_index("narrow")
    seq = share * parts
    layers = w_qkv.shape[0]
    heads = H
    head_dim = width // heads
    count = rows * 2 * share
    scale = head_dim ** (-0.5)
    tile = min(128, share)
    tiles = share // tile
    local = here * share + jnp.arange(share, dtype=jnp.int32)
    cosine, sine = tables(local, head_dim)
    query_block = (jnp.concatenate([local, local]) // BLOCK)[:, None]
    query_clean = jnp.concatenate([jnp.zeros((share,), bool), jnp.ones((share,), bool)])[:, None]
    key_offsets = jnp.arange(share, dtype=jnp.int32)
    tile_block = jnp.arange(tile, dtype=jnp.int32) // BLOCK
    same_block = tile_block[:, None] == tile_block[None, :]
    stop = here + 1

    def group_scores(query, keys_all, group):
        keys = lax.dynamic_slice_in_dim(keys_all, group * share, share, 1)
        score = (
            jnp.einsum("rqhd,rkhd->rhqk", query, keys, preferred_element_type=jnp.float32) * scale
        )
        key_block = ((group * share + key_offsets) // BLOCK)[None, :]
        allow = jnp.where(query_clean, key_block <= query_block, key_block < query_block)
        return jnp.where(allow[None, None], score, -jnp.inf)

    def as_tiles(values):
        return values.reshape(rows, tiles, tile, heads, head_dim)

    def to_rows(values):
        return values.transpose(0, 2, 1, 3).reshape(rows, heads, share)

    def to_tiles(values):
        return values.reshape(rows, heads, tiles, tile).transpose(0, 2, 1, 3)[..., None]

    def noisy_scores(query_noisy, key_noisy):
        score = (
            jnp.einsum(
                "rtqhd,rtkhd->rthqk",
                as_tiles(query_noisy),
                as_tiles(key_noisy),
                preferred_element_type=jnp.float32,
            )
            * scale
        )
        return jnp.where(same_block[None, None, None], score, -jnp.inf)

    def attend_backward(query, clean_k, clean_v, noisy_k, noisy_v, grad_ctx, logsum):
        local_score = noisy_scores(query[:, :share], noisy_k)
        local_probs = jnp.exp(local_score - to_tiles(logsum[:, :, :share]))
        grad_tiles = as_tiles(grad_ctx[:, :share])
        local_dp = jnp.einsum(
            "rtqhd,rtkhd->rthqk", grad_tiles, as_tiles(noisy_v), preferred_element_type=jnp.float32
        )
        delta_start = jnp.concatenate(
            [
                to_rows(jnp.sum(local_dp * local_probs, axis=-1)),
                jnp.zeros((rows, heads, share), jnp.float32),
            ],
            axis=2,
        )

        def delta_step(group, delta):
            probs = jnp.exp(group_scores(query, clean_k, group) - logsum[..., None])
            values = lax.dynamic_slice_in_dim(clean_v, group * share, share, 1)
            grad_probs = jnp.einsum(
                "rqhd,rkhd->rhqk", grad_ctx, values, preferred_element_type=jnp.float32
            )
            return delta + jnp.sum(grad_probs * probs, axis=-1)

        delta = lax.fori_loop(0, stop, delta_step, delta_start)
        local_ds = (local_probs * (local_dp - to_tiles(delta[:, :, :share]))).astype(jnp.bfloat16)
        local_dq = (
            jnp.einsum(
                "rthqk,rtkhd->rtqhd",
                local_ds,
                as_tiles(noisy_k),
                preferred_element_type=jnp.float32,
            )
            * scale
        )
        noisy_gk = (
            jnp.einsum(
                "rthqk,rtqhd->rtkhd",
                local_ds,
                as_tiles(query[:, :share]),
                preferred_element_type=jnp.float32,
            )
            * scale
        ).reshape(rows, share, heads, head_dim)
        noisy_gv = jnp.einsum(
            "rthqk,rtqhd->rtkhd",
            local_probs.astype(jnp.bfloat16),
            grad_tiles,
            preferred_element_type=jnp.float32,
        ).reshape(rows, share, heads, head_dim)
        dq_start = jnp.concatenate(
            [
                local_dq.reshape(rows, share, heads, head_dim),
                jnp.zeros((rows, share, heads, head_dim), jnp.float32),
            ],
            axis=1,
        )
        empty = jnp.zeros((rows, seq, heads, head_dim), jnp.float32)

        def grad_step(group, carry):
            grad_query, grad_key, grad_value = carry
            probs = jnp.exp(group_scores(query, clean_k, group) - logsum[..., None])
            keys = lax.dynamic_slice_in_dim(clean_k, group * share, share, 1)
            values = lax.dynamic_slice_in_dim(clean_v, group * share, share, 1)
            grad_probs = jnp.einsum(
                "rqhd,rkhd->rhqk", grad_ctx, values, preferred_element_type=jnp.float32
            )
            grad_score = (probs * (grad_probs - delta[..., None])).astype(jnp.bfloat16)
            grad_query = (
                grad_query
                + jnp.einsum(
                    "rhqk,rkhd->rqhd", grad_score, keys, preferred_element_type=jnp.float32
                )
                * scale
            )
            key_part = (
                jnp.einsum("rhqk,rqhd->rkhd", grad_score, query, preferred_element_type=jnp.float32)
                * scale
            )
            value_part = jnp.einsum(
                "rhqk,rqhd->rkhd",
                probs.astype(jnp.bfloat16),
                grad_ctx,
                preferred_element_type=jnp.float32,
            )
            grad_key = lax.dynamic_update_slice_in_dim(grad_key, key_part, group * share, 1)
            grad_value = lax.dynamic_update_slice_in_dim(grad_value, value_part, group * share, 1)
            return (grad_query, grad_key, grad_value)

        grad_query, clean_gk, clean_gv = lax.fori_loop(0, stop, grad_step, (dq_start, empty, empty))
        return (grad_query, clean_gk, clean_gv, noisy_gk, noisy_gv)

    prm = shared_params(norm_gains, norm_biases)
    cosr, sinr, bias_c, bias_n = attend_tables(share, head_dim)
    (result, fq, fo, fu, fd, prm, h_out, q_out, nkv_out, kv_out, lse_out, ctx_out, mid_out, u_out) = forward(
        tokens.reshape(count, width), prm, cosr, sinr, bias_c, bias_n, w_qkv, w_out, w_up, w_down)
    saved = []
    for layer in range(layers):
        h_in = tokens.astype(jnp.float32).reshape(count, width) if layer == 0 else h_out[layer - 1]
        o, n1, i1 = norm_rows(h_in, prm[2 * layer], prm[2 * layers + 2 * layer])
        f = o.astype(BF16)
        o, n2, i2 = norm_rows(mid_out[layer], prm[2 * layer + 1], prm[2 * layers + 2 * layer + 1])
        s = o.astype(BF16)
        act = jax.nn.gelu(u_out[layer], approximate=True).astype(BF16)
        mixed = jnp.dot(f, fq[layer], preferred_element_type=F32).reshape(rows, 2, share, 3, heads, head_dim)
        query = rotate(mixed[:, :, :, 0], cosine, sine).astype(BF16)
        key = rotate(mixed[:, :, :, 1], cosine, sine).astype(BF16)
        value = mixed[:, :, :, 2].astype(BF16)
        items = (query.reshape(rows, 2 * share, heads, head_dim),
                 lax.all_gather(key[:, 1], "narrow", axis=1, tiled=True),
                 lax.all_gather(value[:, 1], "narrow", axis=1, tiled=True), key[:, 0], value[:, 0])
        ls = lse_out[layer][:, :heads].T[None]
        saved.append((None, n1, i1, f, items, ls, ctx_out[layer], n2, i2, s, u_out[layer], act))
    hidden = result
    result = hidden.reshape(tokens.shape).astype(jnp.bfloat16)
    valid = (local[None, :] < lengths[:, None]).astype(jnp.float32)
    grad = (cotangent.astype(jnp.float32) * valid[:, None, :, None]).reshape(count, width)
    grad_list = [None] * layers
    for layer in reversed(range(layers)):
        (
            stash,
            normed_one,
            inverse_one,
            first,
            head_items,
            logsum,
            context,
            normed_two,
            inverse_two,
            second,
            upper,
            active,
        ) = saved[layer]
        qkv_w, out_w, up_w, down_w = fq[layer], fo[layer], fu[layer], fd[layer]
        gains = prm[2 * layer:2 * layer + 2]
        branch = grad.astype(jnp.bfloat16)
        grad_down = outer_sum(active, branch)
        grad_active = times_back(branch, down_w)
        _, gelu_pull = jax.vjp(partial(jax.nn.gelu, approximate=True), upper)
        grad_upper = gelu_pull(grad_active)[0].astype(jnp.bfloat16)
        grad_up = outer_sum(second, grad_upper)
        grad_second = times_back(grad_upper, up_w)
        grad_norm, gain_two, bias_two = norm_back(
            grad_second, normed_two, inverse_two, gains[1].astype(jnp.float32)
        )
        grad_mid = grad + grad_norm
        branch = grad_mid.astype(jnp.bfloat16)
        grad_out = outer_sum(context, branch)
        grad_ctx = times_back(branch, out_w).astype(jnp.bfloat16)
        head_g = grad_ctx.reshape(rows, 2 * share, heads, head_dim)
        grad_q, clean_k_grad, clean_v_grad, noisy_k_grad, noisy_v_grad = attend_backward(
            *head_items + (head_g, logsum)
        )
        clean_gk, clean_gv = (
            lax.psum_scatter(
                clean_k_grad.astype(jnp.bfloat16), "narrow", scatter_dimension=1, tiled=True
            ).astype(jnp.float32),
            lax.psum_scatter(
                clean_v_grad.astype(jnp.bfloat16), "narrow", scatter_dimension=1, tiled=True
            ).astype(jnp.float32),
        )
        key_grad = jnp.stack([noisy_k_grad, clean_gk], axis=1)
        value_grad = jnp.stack([noisy_v_grad, clean_gv], axis=1)
        query_grad = grad_q.reshape(rows, 2, share, heads, head_dim)
        mixed_grad = jnp.stack(
            [
                rotate_back(query_grad, cosine, sine),
                rotate_back(key_grad, cosine, sine),
                value_grad,
            ],
            axis=3,
        )
        mixed_grad = mixed_grad.reshape(count, 3 * width).astype(jnp.bfloat16)
        grad_qkv = outer_sum(first, mixed_grad)
        grad_first = times_back(mixed_grad, qkv_w)
        grad_in, gain_one, bias_one = norm_back(
            grad_first, normed_one, inverse_one, gains[0].astype(jnp.float32)
        )
        grad = grad_mid + grad_in
        shards = (
            lax.psum_scatter(
                grad_qkv.astype(jnp.bfloat16), "narrow", scatter_dimension=0, tiled=True
            ).astype(jnp.float32),
            lax.psum_scatter(
                grad_out.astype(jnp.bfloat16), "narrow", scatter_dimension=0, tiled=True
            ).astype(jnp.float32),
            lax.psum_scatter(
                grad_up.astype(jnp.bfloat16), "narrow", scatter_dimension=0, tiled=True
            ).astype(jnp.float32),
            lax.psum_scatter(
                grad_down.astype(jnp.bfloat16), "narrow", scatter_dimension=0, tiled=True
            ).astype(jnp.float32),
            lax.psum_scatter(
                jnp.stack([gain_one, gain_two]).astype(jnp.bfloat16),
                "narrow",
                scatter_dimension=1,
                tiled=True,
            ).astype(jnp.float32),
            lax.psum_scatter(
                jnp.stack([bias_one, bias_two]).astype(jnp.bfloat16),
                "narrow",
                scatter_dimension=1,
                tiled=True,
            ).astype(jnp.float32),
        )
        shards = lax.psum(
            (shards[0], shards[1], shards[2], shards[3], shards[4], shards[5]), "wide"
        )
        grad_list[layer] = shards
    stacked = tuple(
        (jnp.stack([grad_list[layer][kind] for layer in range(layers)]) for kind in range(6))
    )
    grad_tokens = grad.reshape(tokens.shape).astype(jnp.bfloat16)
    return (
        result,
        grad_tokens,
        stacked[0],
        stacked[1],
        stacked[2],
        stacked[3],
        stacked[4],
        stacked[5][:, 0],
        stacked[5][:, 1],
    )


def solution(mesh):
    return jax.shard_map(
        on_device,
        mesh=mesh,
        in_specs=(
            P("wide", None, "narrow", None),
            P("wide"),
            P(None, "narrow", None),
            P(None, "narrow", None),
            P(None, "narrow", None),
            P(None, "narrow", None),
            P(None, None, "narrow"),
            P(None, None, "narrow"),
            P("wide", None, "narrow", None),
        ),
        out_specs=(
            P("wide", None, "narrow", None),
            P("wide", None, "narrow", None),
            P(None, "narrow", None),
            P(None, "narrow", None),
            P(None, "narrow", None),
            P(None, "narrow", None),
            P(None, None, "narrow"),
            P(None, "narrow"),
            P(None, "narrow"),
        ),
        check_vma=False,
    )
```

```python
from functools import partial

import jax
import jax.numpy as jnp
from jax import lax
from jax.experimental import pallas as pl
from jax.experimental.pallas import tpu as pltpu
from jax.sharding import PartitionSpec as P

H = 12
BLOCK = 16
NEG = -1e30
EPS = 1e-05
MESH = pl.DeviceIdType.MESH
F32 = jnp.float32
BF16 = jnp.bfloat16
GELU_C = 0.7978845608028654
GELU_A = 0.044715


def dot(a, b):
    return jnp.dot(a, b, preferred_element_type=F32)


def dot_nt(a, b):
    return lax.dot_general(a, b, (((1,), (1,)), ((), ())), preferred_element_type=F32)


def dot_tn(a, b):
    return lax.dot_general(a, b, (((0,), (0,)), ((), ())), preferred_element_type=F32)


def tile_at(index, size):
    return pl.ds(pl.multiple_of(index * size, size), size)


def loop(count, body):
    lax.fori_loop(0, count, lambda i, _: (body(i), None)[1], None)


def swap_halves(x, first):
    return jnp.where(first, pltpu.roll(x, 96, 1), pltpu.roll(x, 32, 1))


def lane_masks(rows):
    lane = lax.broadcasted_iota(jnp.int32, (rows, 128), 1)
    return lane % 64 < 32


def head_masks():
    lane = lax.broadcasted_iota(jnp.int32, (1, 128), 1)
    low = (lane < 64).astype(F32)
    return low, 1.0 - low


def norm_into(src, dst, gain, bias, rows):
    step = 32

    def body(i):
        at = tile_at(i, step)
        x = src[at, :].astype(F32)
        c = x - jnp.mean(x, axis=-1, keepdims=True)
        inv = lax.rsqrt(jnp.mean(c * c, axis=-1, keepdims=True) + EPS)
        dst[at, :] = (c * inv * gain + bias).astype(BF16)

    loop(rows // step, body)


class Gather:
    def __init__(self, here, shard, full, send, recv, base, lsem):
        self.n, self.w = here
        self.core = lax.rem(self.w, 2)
        self.shard, self.full, self.send, self.recv, self.base, self.lsem = (
            shard, full, send, recv, base, lsem)
        self.rows = shard.shape[0]
        self.half = self.rows // 2
        self.quarter = self.rows // 4
        self.x, self.y, self.d, self.s = (
            (self.n ^ 1, self.w), (self.n ^ 2, self.w), (self.n ^ 3, self.w), (self.n, self.w ^ 1))

    def region(self, owner, core, quarter=None):
        start = owner * self.rows + core * self.half
        if quarter is None:
            return self.full.at[pl.ds(pl.multiple_of(start, 16), self.half)]
        return self.full.at[pl.ds(pl.multiple_of(start + quarter * self.quarter, 16), self.quarter)]

    def copy(self, slot, src, dst, device):
        k = self.base + slot
        return pltpu.make_async_remote_copy(
            src_ref=src, dst_ref=dst, send_sem=self.send.at[k], recv_sem=self.recv.at[k],
            device_id=device, device_id_type=MESH)

    def own(self):
        return pltpu.make_async_copy(
            self.shard, self.full.at[pl.ds(pl.multiple_of(self.n * self.rows, 16), self.rows)], self.lsem)

    def plain(self, slot, region, device):
        return self.copy(slot, region, region, device)

    def issue(self):
        src = self.shard.at[pl.ds(pl.multiple_of(self.core * self.half, 16), self.half)]
        dst = self.region(self.n, self.core)
        self.copy(0, src, dst, self.x).start()
        self.copy(1, src, dst, self.y).start()
        self.own().start()

    def forward(self):
        nx, ny = self.x[0], self.y[0]
        self.plain(0, self.region(nx, self.core), self.x).wait_recv()
        self.plain(2, self.region(nx, self.core, 0), self.y).start()
        self.plain(4, self.region(nx, self.core), self.s).start()
        self.plain(1, self.region(ny, self.core), self.y).wait_recv()
        self.plain(3, self.region(ny, self.core, 1), self.x).start()
        self.plain(5, self.region(ny, self.core), self.s).start()

    def finish(self):
        nd = self.d[0]
        self.plain(2, self.region(nd, self.core, 0), self.y).wait_recv()
        self.plain(3, self.region(nd, self.core, 1), self.x).wait_recv()
        self.plain(6, self.region(nd, self.core), self.s).start()

    def use(self):
        other = 1 - self.core
        for slot, who in ((4, self.x), (5, self.y), (6, self.d)):
            self.plain(slot, self.region(who[0], other), self.s).wait_recv()
        self.own().wait()

    def drain(self):
        src = self.shard.at[pl.ds(pl.multiple_of(self.core * self.half, 16), self.half)]
        dst = self.region(self.n, self.core)
        self.copy(0, src, dst, self.x).wait_send()
        self.copy(1, src, dst, self.y).wait_send()
        nx, ny, nd = self.x[0], self.y[0], self.d[0]
        self.plain(2, self.region(nx, self.core, 0), self.y).wait_send()
        self.plain(3, self.region(ny, self.core, 1), self.x).wait_send()
        self.plain(4, self.region(nx, self.core), self.s).wait_send()
        self.plain(5, self.region(ny, self.core), self.s).wait_send()
        self.plain(6, self.region(nd, self.core), self.s).wait_send()


def forward_kernel(
    layers,
    tok, prm, cosr, sinr, bias_c, bias_n, wq, wo, wu, wd,
    result, fq, fo, fu, fd, prm_out, h_out, q_out, nkv_out, kv_out, lse_out, ctx_out, mid_out, act_out, dg_out,
    gq, go, gu, gd, prm_buf, par, hid, a, q, nkv, kv, score, top, lse, ctx, mid, dg, act,
    send, recv, lsem, psend, precv, ksend, krecv, ssem,
):
    n = lax.axis_index("narrow")
    w = lax.axis_index("wide")
    rows, width = tok.shape
    share = rows // 2
    group = share
    pairs = width // 128
    ff = wu.shape[2]
    peers = ((n ^ 1, w), (n ^ 2, w), (n ^ 3, w))

    barrier = pltpu.get_barrier_semaphore()
    for device in peers + ((n, w ^ 1),):
        pl.semaphore_signal(barrier, inc=1, device_id=device, device_id_type=MESH)
    pl.semaphore_wait(barrier, 4)

    tensors = []
    for layer in range(layers):
        for kind, (shard, full) in enumerate(((wq, gq), (wo, go), (wu, gu), (wd, gd))):
            k = layer * 4 + kind
            tensors.append(Gather((n, w), shard.at[layer], full.at[layer], send, recv, 7 * k, lsem.at[k]))

    def params(i):
        return pltpu.make_async_remote_copy(
            src_ref=prm, dst_ref=prm_buf.at[i], send_sem=psend.at[i], recv_sem=precv.at[i],
            device_id=peers[i], device_id_type=MESH)

    def share_kv(layer, i):
        region = kv.at[layer, tile_at(n, share)]
        return pltpu.make_async_remote_copy(
            src_ref=region, dst_ref=region, send_sem=ksend.at[3 * layer + i],
            recv_sem=krecv.at[3 * layer + i], device_id=peers[i], device_id_type=MESH)

    def recv_kv(layer, i):
        region = kv.at[layer, tile_at(peers[i][0], share)]
        return pltpu.make_async_remote_copy(
            src_ref=region, dst_ref=region, send_sem=ksend.at[3 * layer + i],
            recv_sem=krecv.at[3 * layer + i], device_id=peers[i], device_id_type=MESH)

    gives = (n % 2 == 0, n < 2, n < 2)
    takes = (n % 2 == 1, n >= 2, n >= 2)

    for i in range(3):
        params(i).start()
    tensors[0].issue()
    tensors[1].issue()

    def saves(layer):
        pieces = [
            (q, q_out.at[layer]), (nkv, nkv_out.at[layer]), (kv.at[layer], kv_out.at[layer]),
            (lse, lse_out.at[layer]), (ctx, ctx_out.at[layer]), (mid, mid_out.at[layer]), (act, act_out.at[layer]),
            (dg, dg_out.at[layer]), (hid, h_out.at[layer]),
        ]
        return [pltpu.make_async_copy(s, d, ssem.at[layer * 9 + k]) for k, (s, d) in enumerate(pieces)]

    def weight_saves():
        pieces = ((gq, fq), (go, fo), (gu, fu), (gd, fd))
        out = []
        for layer in range(layers):
            for kind, (s, d) in enumerate(pieces):
                k = layer * 4 + kind
                out.append(pltpu.make_async_copy(s.at[layer], d.at[layer], ssem.at[9 * layers + k]))
        return out

    for i in range(3):
        params(i).wait_recv()
    par[...] = prm[...] + prm_buf[0] + prm_buf[1] + prm_buf[2]
    prm_out[...] = par[...]

    first = lane_masks(rows)
    masks = head_masks()
    lanes = lax.broadcasted_iota(jnp.int32, (rows, 128), 1)

    for layer in range(layers):
        t_qkv, t_out, t_up, t_down = tensors[4 * layer:4 * layer + 4]
        later = tensors[4 * layer + 4:]
        gain1, gain2 = par[2 * layer:2 * layer + 1, :], par[2 * layer + 1:2 * layer + 2, :]
        at = 2 * layers + 2 * layer
        bias1, bias2 = par[at:at + 1, :], par[at + 1:at + 2, :]
        saved = saves(layer)
        before = saves(layer - 1) if layer else None
        if layer == 0:
            norm_into(tok, a, gain1, bias1, rows)
        else:
            norm_into(hid, a, gain1, bias1, rows)
        if layer == 0:
            t_qkv.forward()
        t_qkv.finish()
        t_qkv.use()
        if before:
            before[0].wait()
            before[1].wait()

        wqkv = gq.at[layer]

        def query_tile(j):
            x = dot(a[...], wqkv[:, tile_at(j, 256)])
            for part in range(2):
                v = x[:, 128 * part:128 * part + 128]
                v = v * cosr[...] + swap_halves(v, first) * sinr[...]
                q[:, tile_at(2 * j + part, 128)] = (v.astype(BF16).astype(F32) * 0.125).astype(BF16)

        def key_tile(j):
            x = dot(a[...], wqkv[:, tile_at(j + 3, 256)])
            for part in range(2):
                v = x[:, 128 * part:128 * part + 128]
                v = (v * cosr[...] + swap_halves(v, first) * sinr[...]).astype(BF16)
                nkv[:, tile_at(2 * j + part, 128)] = v[:share]
                kv[layer, tile_at(n, share), tile_at(2 * j + part, 128)] = v[share:]

        def value_tile(j):
            v = dot(a[...], wqkv[:, tile_at(j + 6, 256)]).astype(BF16)
            nkv[:, tile_at(j + 3, 256)] = v[:share]
            kv[layer, tile_at(n, share), tile_at(j + 3, 256)] = v[share:]

        loop(3, key_tile)
        loop(3, value_tile)
        for i in range(3):
            @pl.when(gives[i])
            def _():
                share_kv(layer, i).start()
        loop(3, query_tile)
        saved[0].start()
        saved[1].start()
        t_out.forward()
        t_up.issue()
        t_down.issue()
        for i in range(3):
            @pl.when(takes[i])
            def _():
                recv_kv(layer, i).wait_recv()
        saved[2].start()
        if before:
            before[3].wait()
            before[4].wait()

        def pair_step(pair):
            at_pair = tile_at(pair, 128)
            at_value = tile_at(pair + pairs, 128)
            q2 = q[:, at_pair].astype(F32)
            outs = []
            for h in range(2):
                qm = (q2 * masks[h]).astype(BF16)
                s = dot_nt(qm, kv[layer, tile_at(n, group), at_pair]) + bias_c[...]
                score[:, tile_at(n, group)] = s
                top[...] = jnp.maximum(s[:, :128], s[:, 128:])
                s = dot_nt(qm[:share], nkv[:, at_pair]) + bias_n[...]
                score[:share, 4 * group:5 * group] = s
                top[:share] = jnp.maximum(top[:share], jnp.maximum(s[:, :128], s[:, 128:]))

                def scores_of(g):
                    s = dot_nt(qm, kv[layer, tile_at(g, group), at_pair])
                    score[:, tile_at(g, group)] = s
                    top[...] = jnp.maximum(top[...], jnp.maximum(s[:, :128], s[:, 128:]))

                loop(n, scores_of)
                most = jnp.max(top[...], axis=-1, keepdims=True)
                p = jnp.exp(score[:share, 4 * group:5 * group] - most[:share])
                part = p[:, :128] + p[:, 128:]
                add = dot(p.astype(BF16), nkv[:, at_value])
                zeros = jnp.zeros((share, 128), F32)

                def probs_of(g, carry):
                    total, out = carry
                    p = jnp.exp(score[:, tile_at(g, group)] - most)
                    total = total + p[:, :128] + p[:, 128:]
                    out = out + dot(p.astype(BF16), kv[layer, tile_at(g, group), at_value])
                    return total, out

                total, out = lax.fori_loop(
                    0, n + 1, probs_of,
                    (jnp.concatenate([part, zeros], axis=0), jnp.concatenate([add, zeros], axis=0)))
                total = jnp.sum(total, axis=-1, keepdims=True)
                outs.append(out * (masks[h] / total))
                lse[...] = jnp.where(lanes == 2 * pair + h, most + jnp.log(total), lse[...])
            ctx[:, at_pair] = (outs[0] + outs[1]).astype(BF16)

        loop(pairs, pair_step)
        saved[3].start()
        saved[4].start()
        t_out.finish()
        t_out.use()
        t_up.forward()
        if later:
            later[0].issue()
            later[1].issue()
        if before:
            before[5].wait()
            before[6].wait()
            before[7].wait()
            before[8].wait()

        def out_tile(j):
            at = tile_at(j, 256)
            base = (tok if layer == 0 else hid)[:, at].astype(F32)
            mid[:, at] = base + dot(ctx[...], go[layer, :, at])

        loop(width // 256, out_tile)
        saved[5].start()
        norm_into(mid, a, gain2, bias2, rows)
        t_up.finish()
        t_up.use()

        def up_tile(j):
            at = tile_at(j, 256)
            x = dot(a[...], gu[layer, :, at])
            x2 = x * x
            t = jnp.tanh(GELU_C * (x + GELU_A * (x * x2)))
            cdf = 0.5 + 0.5 * t
            act[:, at] = (x * cdf).astype(BF16)
            slope = GELU_C * (1.0 + 3.0 * GELU_A * x2)
            dg[:, at] = (cdf + 0.5 * x * (1.0 - t * t) * slope).astype(BF16)

        loop(ff // 256, up_tile)
        saved[6].start()
        saved[7].start()
        t_down.forward()
        if later:
            later[0].forward()
        t_down.finish()
        t_down.use()

        def down_tile(j):
            at = tile_at(j, 256)
            out = mid[:, at] + dot(act[...], gd[layer, :, at])
            hid[:, at] = out
            if layer == layers - 1:
                result[:, at] = out.astype(BF16)

        loop(width // 256, down_tile)
        saved[8].start()

    for c in weight_saves():
        c.start()
    for c in saves(layers - 1):
        c.wait()
    for layer in range(layers - 1):
        saves(layer)[2].wait()
    for c in weight_saves():
        c.wait()
    for t in tensors:
        t.drain()
    for i in range(3):
        params(i).wait_send()
        for layer in range(layers):
            @pl.when(gives[i])
            def _():
                share_kv(layer, i).wait_send()


def forward(tokens, prm, cosr, sinr, bias_c, bias_n, w_qkv, w_out, w_up, w_down):
    rows, width = tokens.shape
    share = rows // 2
    layers = w_qkv.shape[0]
    seq = share * 4
    qw, ff = w_qkv.shape[2], w_up.shape[2]
    full = [
        jax.ShapeDtypeStruct((layers, width, qw), BF16),
        jax.ShapeDtypeStruct((layers, width, width), BF16),
        jax.ShapeDtypeStruct((layers, width, ff), BF16),
        jax.ShapeDtypeStruct((layers, ff, width), BF16),
    ]
    hbm = pl.BlockSpec(memory_space=pltpu.HBM)
    vmem = pl.BlockSpec(memory_space=pltpu.VMEM)
    shape = jax.ShapeDtypeStruct
    kept = [
        shape((layers, rows, width), F32),
        shape((layers, rows, width), BF16),
        shape((layers, share, 2 * width), BF16),
        shape((layers, seq, 2 * width), BF16),
        shape((layers, rows, 128), F32),
        shape((layers, rows, width), BF16),
        shape((layers, rows, width), F32),
        shape((layers, rows, ff), BF16),
        shape((layers, rows, ff), BF16),
    ]
    dma, count = pltpu.SemaphoreType.DMA, 7 * 4 * layers
    return pl.pallas_call(
        partial(forward_kernel, layers),
        out_shape=[shape((rows, width), BF16)] + full + [shape(prm.shape, F32)] + kept,
        in_specs=[vmem] * 6 + [hbm] * 4,
        out_specs=[vmem] + [hbm] * 4 + [vmem] + [hbm] * 9,
        scratch_shapes=[pltpu.VMEM(f.shape, BF16) for f in full] + [
            pltpu.VMEM((3,) + prm.shape, F32),
            pltpu.VMEM(prm.shape, F32),
            pltpu.VMEM((rows, width), F32),
            pltpu.VMEM((rows, width), BF16),
            pltpu.VMEM((rows, width), BF16),
            pltpu.VMEM((share, 2 * width), BF16),
            pltpu.VMEM((layers, seq, 2 * width), BF16),
            pltpu.VMEM((rows, seq + share), F32),
            pltpu.VMEM((rows, 128), F32),
            pltpu.VMEM((rows, 128), F32),
            pltpu.VMEM((rows, width), BF16),
            pltpu.VMEM((rows, width), F32),
            pltpu.VMEM((rows, ff), BF16),
            pltpu.VMEM((rows, ff), BF16),
            dma((count,)), dma((count,)), dma((4 * layers,)),
            dma((3,)), dma((3,)), dma((3 * layers,)), dma((3 * layers,)),
            dma((9 * layers + 4 * layers,)),
        ],
        compiler_params=pltpu.CompilerParams(
            collective_id=0, has_side_effects=True, vmem_limit_bytes=62 * 2**20),
        cost_estimate=pl.CostEstimate(flops=20 * 10**9, bytes_accessed=10**8, transcendentals=10**7),
        name="forward",
    )(tokens, prm, cosr, sinr, bias_c, bias_n, w_qkv, w_out, w_up, w_down)


def add_rows(dst, at, left, left_at, right, right_at, rows):
    def body(i):
        step = lambda base: pl.ds(pl.multiple_of(base + 16 * i, 16), 16)
        dst[step(at), :] = left[step(left_at), :] + right[step(right_at), :]

    loop(rows // 16, body)


class Reduce:
    def __init__(self, here, turn, turns, grad, bufs, out, send, recv, base, credit, cbase, lsem):
        self.n, self.w = here
        self.turn, self.turns = turn, turns
        self.grad, self.out = grad, out
        self.s1, self.r2, self.r3, self.r4, self.r5, self.zb = bufs
        self.send, self.recv, self.base = send, recv, base
        self.credit, self.cbase, self.lsem = credit, cbase, lsem
        self.core = lax.rem(self.w, 2)
        self.rows = grad.shape[0] // 4
        self.half, self.quarter = self.rows // 2, self.rows // 4
        n, w = here
        self.x, self.y, self.d, self.s = (n ^ 1, w), (n ^ 2, w), (n ^ 3, w), (n, w ^ 1)
        chips = lax.axis_size("wide") // 2
        z = w // 2
        left = z < chips // 2
        step = jnp.where(left, 2, -2)
        self.inner, self.outer = (n, w + step), (n, w - step)
        self.has_outer = jnp.logical_and(z > 0, z < chips - 1)
        self.is_mid = jnp.logical_or(z == chips // 2 - 1, z == chips // 2)
        self.mine = jnp.where(left, 0, 1)

    def at(self, owner, core, quarter=0):
        return pl.multiple_of(owner * self.rows + core * self.half + quarter * self.quarter, 16)

    def part(self, ref, start, count):
        return ref.at[pl.ds(pl.multiple_of(start, 16), count)]

    def copy(self, slot, src, dst, device):
        k = self.base + slot
        return pltpu.make_async_remote_copy(
            src_ref=src, dst_ref=dst, send_sem=self.send.at[k], recv_sem=self.recv.at[k],
            device_id=device, device_id_type=MESH)

    def take(self, slot):
        if self.turn > 0:
            pl.semaphore_wait(self.credit.at[self.cbase + slot], 1)

    def give(self, slot, device):
        if self.turn < self.turns - 1:
            pl.semaphore_signal(
                self.credit.at[self.cbase + slot], inc=1, device_id=device, device_id_type=MESH)

    def to_sibling(self):
        out = []
        for m in range(4):
            src = self.part(self.grad, self.at(m, 1 - self.core), self.half)
            out.append(self.copy(m, src, self.part(self.s1, m * self.half, self.half), self.s))
        return out

    def first_hop(self):
        q, g, c = self.quarter, self.grad, self.core
        nx, ny, nd = self.x[0], self.y[0], self.d[0]
        plan = ((4, nx, 0, 0, self.x), (5, nd, 0, 1, self.x), (6, ny, 1, 2, self.y), (7, nd, 1, 3, self.y))
        return [
            self.copy(slot, self.part(g, self.at(owner, c, quarter), q), self.part(self.r2, place * q, q), device)
            for slot, owner, quarter, place, device in plan]

    def second_hop(self):
        q, g, c = self.quarter, self.grad, self.core
        return [
            self.copy(8, self.part(g, self.at(self.y[0], c, 0), q), self.part(self.r3, 0, q), self.y),
            self.copy(9, self.part(g, self.at(self.x[0], c, 1), q), self.part(self.r3, q, q), self.x)]

    def inward(self):
        return self.copy(10, self.zb, self.r4, self.inner)

    def across(self):
        src = self.part(self.zb, (1 - self.mine) * self.quarter, self.quarter)
        return self.copy(11, src, self.r5, self.inner)

    def done_at(self, core, quarter):
        start = core * self.half + quarter * self.quarter
        return self.part(self.out, start, self.quarter)

    def final(self, quarter, device, slot, from_zb):
        dst = self.done_at(self.core, quarter)
        src = self.part(self.zb, quarter * self.quarter, self.quarter) if from_zb else dst
        return self.copy(slot, src, dst, device)

    def keep(self):
        src = self.part(self.zb, self.mine * self.quarter, self.quarter)
        return pltpu.make_async_copy(src, self.done_at(self.core, self.mine), self.lsem)

    def p1(self):
        self.take(0)
        for c in self.to_sibling():
            c.start()

    def p2(self):
        g = self.grad
        for m, c in enumerate(self.to_sibling()):
            c.wait_recv()
            add_rows(g, self.at(m, self.core), g, self.at(m, self.core), self.s1, m * self.half, self.half)
        self.give(0, self.s)
        self.take(1)
        self.take(2)
        for c in self.first_hop():
            c.start()

    def p3(self):
        g, q = self.grad, self.quarter
        hops = self.first_hop()
        hops[1].wait_recv()
        at = self.at(self.y[0], self.core, 0)
        add_rows(g, at, g, at, self.r2, q, q)
        self.take(3)
        self.second_hop()[0].start()
        hops[3].wait_recv()
        at = self.at(self.x[0], self.core, 1)
        add_rows(g, at, g, at, self.r2, 3 * q, q)
        self.take(4)
        self.second_hop()[1].start()
        for k in range(2):
            hops[2 * k].wait_recv()
            at = self.at(self.n, self.core, k)
            add_rows(g, at, g, at, self.r2, 2 * k * q, q)
        self.give(1, self.x)
        self.give(2, self.y)

    def p4(self):
        g, q = self.grad, self.quarter
        for k, c in enumerate(self.second_hop()):
            c.wait_recv()
            add_rows(self.zb, k * q, g, self.at(self.n, self.core, k), self.r3, k * q, q)
        self.give(3, self.y)
        self.give(4, self.x)

        @pl.when(jnp.logical_not(jnp.logical_or(self.has_outer, self.is_mid)))
        def _():
            self.take(5)
            self.inward().start()

    def p5(self):
        @pl.when(self.has_outer)
        def _():
            self.inward().wait_recv()
            add_rows(self.zb, 0, self.zb, 0, self.r4, 0, self.half)
            self.give(5, self.outer)

        @pl.when(self.is_mid)
        def _():
            self.take(6)
            self.across().start()

        @pl.when(jnp.logical_and(self.has_outer, jnp.logical_not(self.is_mid)))
        def _():
            self.take(5)
            self.inward().start()

    def p6(self):
        @pl.when(self.is_mid)
        def _():
            self.across().wait_recv()
            at = self.mine * self.quarter
            add_rows(self.zb, at, self.zb, at, self.r5, 0, self.quarter)
            self.give(6, self.inner)
            self.keep().start()
            self.final(self.mine, self.inner, 12, True).start()
            self.final(self.mine, self.s, 13, True).start()

        @pl.when(jnp.logical_and(self.is_mid, self.has_outer))
        def _():
            self.final(self.mine, self.outer, 15, True).start()

    def p7(self):
        other = 1 - self.mine

        @pl.when(self.is_mid)
        def _():
            self.final(other, self.inner, 12, False).wait_recv()
            self.final(other, self.s, 14, False).start()

        @pl.when(jnp.logical_and(self.is_mid, self.has_outer))
        def _():
            self.final(other, self.outer, 16, False).start()

        @pl.when(jnp.logical_not(self.is_mid))
        def _():
            self.final(self.mine, self.inner, 15, False).wait_recv()
            self.final(self.mine, self.s, 13, False).start()
            self.final(other, self.inner, 16, False).wait_recv()
            self.final(other, self.s, 14, False).start()

        @pl.when(jnp.logical_and(jnp.logical_not(self.is_mid), self.has_outer))
        def _():
            self.final(self.mine, self.outer, 15, False).start()
            self.final(other, self.outer, 16, False).start()

    def p8(self):
        for k, quarter in ((13, self.mine), (14, 1 - self.mine)):
            region = self.done_at(1 - self.core, quarter)
            self.copy(k, region, region, self.s).wait_recv()

    def free_grad(self):
        for c in self.to_sibling() + self.first_hop() + self.second_hop():
            c.wait_send()

    def free_zb(self):
        @pl.when(jnp.logical_not(self.is_mid))
        def _():
            self.inward().wait_send()

        @pl.when(self.is_mid)
        def _():
            self.across().wait_send()
            self.final(self.mine, self.inner, 12, True).wait_send()
            self.keep().wait()

        other = 1 - self.mine
        self.final(self.mine, self.s, 13, False).wait_send()
        self.final(other, self.s, 14, False).wait_send()

        @pl.when(self.has_outer)
        def _():
            self.final(self.mine, self.outer, 15, False).wait_send()
            self.final(other, self.outer, 16, False).wait_send()


SLOTS = 17


class SmallSum:
    def __init__(self, here, acc, buf, send, recv):
        n, w = here
        self.acc, self.buf, self.send, self.recv = acc, buf, send, recv
        chips = lax.axis_size("wide") // 2
        z = w // 2
        left = z < chips // 2
        step = jnp.where(left, 2, -2)
        self.inner, self.outer = (n, w + step), (n, w - step)
        self.has_outer = jnp.logical_and(z > 0, z < chips - 1)
        self.is_mid = jnp.logical_or(z == chips // 2 - 1, z == chips // 2)
        self.others = ((n, w ^ 1), (n ^ 1, w), (n ^ 2, w))

    def copy(self, slot, device):
        return pltpu.make_async_remote_copy(
            src_ref=self.buf.at[0, slot], dst_ref=self.buf.at[1, slot], send_sem=self.send.at[slot],
            recv_sem=self.recv.at[slot], device_id=device, device_id_type=MESH)

    def begin(self):
        self.buf[0, 0] = self.acc[...]
        self.copy(0, self.others[0]).start()

    def swap(self, slot):
        self.copy(slot, self.others[slot]).wait_recv()
        self.buf[0, slot + 1] = self.buf[0, slot] + self.buf[1, slot]
        if slot < 2:
            self.copy(slot + 1, self.others[slot + 1]).start()

    def chain(self):
        @pl.when(self.has_outer)
        def _():
            self.copy(3, self.outer).wait_recv()
            self.buf[0, 3] = self.buf[0, 3] + self.buf[1, 3]

        @pl.when(jnp.logical_not(self.is_mid))
        def _():
            self.copy(3, self.inner).start()

        @pl.when(self.is_mid)
        def _():
            self.buf[0, 4] = self.buf[0, 3]
            self.copy(4, self.inner).start()

    def settle(self):
        @pl.when(self.is_mid)
        def _():
            self.copy(4, self.inner).wait_recv()
            self.buf[0, 5] = self.buf[0, 4] + self.buf[1, 4]

        @pl.when(jnp.logical_not(self.is_mid))
        def _():
            self.copy(5, self.inner).wait_recv()
            self.buf[0, 5] = self.buf[1, 5]

        @pl.when(self.has_outer)
        def _():
            self.copy(5, self.outer).start()

    def finish(self, out):
        out[...] = self.buf[0, 5]
        for k in range(3):
            self.copy(k, self.others[k]).wait_send()

        @pl.when(jnp.logical_not(self.is_mid))
        def _():
            self.copy(3, self.inner).wait_send()

        @pl.when(self.is_mid)
        def _():
            self.copy(4, self.inner).wait_send()

        @pl.when(self.has_outer)
        def _():
            self.copy(5, self.outer).wait_send()


TILE = 512


def backward_kernel(
    layers,
    lens, cot, tok, par, cosr, sinr, bias_c, bias_n,
    fq, fo, fu, fd, h_in, q_in, nkv_in, kv_in, lse_in, ctx_in, mid_in, act_in, dg_in,
    grad_tok, oq, oo, ou, od, small,
    gq, go, gu, gd, *rest,
):
    bufs, rest = [rest[6 * k:6 * k + 6] for k in range(4)], rest[24:]
    (wd_s, wu_s, act_s, dg_s, wo, wq, dh, mid, da, at_, db, q, kv, nkv, ctx, dctx, lse, lset, delta, dqkv, xfer,
     gacc, sbuf, send, recv, credit, lsem, ksend, krecv, kcredit, stsem, ldsem, ssend, srecv) = rest
    n = lax.axis_index("narrow")
    w = lax.axis_index("wide")
    here = (n, w)
    rows, width = cot.shape
    share = rows // 2
    group = share
    pairs = width // 128
    ff = act_in.shape[2]
    tiles = ff // TILE
    peers = ((n ^ 1, w), (n ^ 2, w), (n ^ 3, w))
    gives = (n % 2 == 0, n < 2, n < 2)
    takes = (n % 2 == 1, n >= 2, n >= 2)
    order = list(reversed(range(layers)))

    def reducers(turn):
        layer = order[turn]
        made = []
        for kind, (g, o) in enumerate(((gq, oq), (go, oo), (gu, ou), (gd, od))):
            k = turn * 4 + kind
            made.append(Reduce(here, turn, layers, g, bufs[kind], o.at[layer], send, recv, SLOTS * k,
                               credit, 7 * kind, lsem.at[k]))
        return made

    every = [reducers(turn) for turn in range(layers)]

    barrier = pltpu.get_barrier_semaphore()
    zdev = every[0][0]
    hello = peers + ((n, w ^ 1), zdev.inner)
    for device in hello:
        pl.semaphore_signal(barrier, inc=1, device_id=device, device_id_type=MESH)

    @pl.when(zdev.has_outer)
    def _():
        pl.semaphore_signal(barrier, inc=1, device_id=zdev.outer, device_id_type=MESH)

    def stream(layer, j, slot):
        cols = tile_at(j, TILE)
        return [
            pltpu.make_async_copy(fd.at[layer, cols], wd_s.at[slot], stsem.at[slot, 0]),
            pltpu.make_async_copy(fu.at[layer, :, cols], wu_s.at[slot], stsem.at[slot, 1]),
            pltpu.make_async_copy(act_in.at[layer, :, cols], act_s.at[slot], stsem.at[slot, 2]),
            pltpu.make_async_copy(dg_in.at[layer, :, cols], dg_s.at[slot], stsem.at[slot, 3]),
        ]

    def loads(layer):
        pieces = ((mid_in, mid), (ctx_in, ctx), (q_in, q), (nkv_in, nkv), (kv_in, kv), (lse_in, lse), (fo, wo), (fq, wq))
        return [pltpu.make_async_copy(s.at[layer], d, ldsem.at[k]) for k, (s, d) in enumerate(pieces)]

    def load_h(layer):
        if layer == 0:
            return pltpu.make_async_copy(tok, db, ldsem.at[8])
        return pltpu.make_async_copy(h_in.at[layer - 1], mid, ldsem.at[8])

    for c in stream(order[0], 0, 0):
        c.start()
    for c in loads(order[0]):
        c.start()

    local = lax.broadcasted_iota(jnp.int32, (share, 1), 0) + n * share
    valid = (local < lens[0]).astype(F32)
    first_load = pltpu.make_async_copy(cot, db, ldsem.at[9])
    first_load.start()
    first_load.wait()
    for k in range(2):
        dh[k * share:(k + 1) * share] = db[k * share:(k + 1) * share, :].astype(F32) * valid
    gacc[...] = jnp.zeros_like(gacc)
    first = lane_masks(rows)
    masks = head_masks()

    def to_bf16(dst):
        def body(i):
            at = tile_at(i, 64)
            dst[at, :] = dh[at, :].astype(BF16)

        loop(rows // 64, body)

    def norm_of(src, at):
        x = src[at, :].astype(F32)
        c = x - jnp.mean(x, axis=-1, keepdims=True)
        inv = lax.rsqrt(jnp.mean(c * c, axis=-1, keepdims=True) + EPS)
        return c * inv, inv

    def normed_transposed(src, gain, bias):
        for i in range(rows // 128):
            normed, _ = norm_of(src, slice(128 * i, 128 * i + 128))
            at_[:, 128 * i:128 * i + 128] = (normed * gain + bias).astype(BF16).T

    def norm_back(src, gain, row_gain, row_bias):
        step = 32

        def body(i, carry):
            at = tile_at(i, step)
            normed, inv = norm_of(src, at)
            g = da[at, :]
            e = g * gain
            dv = inv * (e - jnp.mean(e, axis=-1, keepdims=True)
                        - normed * jnp.mean(e * normed, axis=-1, keepdims=True))
            dh[at, :] = dh[at, :] + dv
            fold = lambda v: v.reshape(step // 8, 8, width).sum(axis=0)
            return carry[0] + fold(g * normed), carry[1] + fold(g)

        zero = jnp.zeros((8, width), F32)
        one, two = lax.fori_loop(0, rows // step, body, (zero, zero))
        gacc[row_gain:row_gain + 1, :] = jnp.sum(one, axis=0, keepdims=True)
        gacc[row_bias:row_bias + 1, :] = jnp.sum(two, axis=0, keepdims=True)

    def block(pair, k2, v2, at, bias):
        at_pair = tile_at(pair, 128)
        q2 = q[at, at_pair].astype(F32)
        d2 = dctx[at, at_pair].astype(F32)
        k2f = k2.astype(F32)
        dk = dv = dq = None
        for h in range(2):
            row = pl.ds(2 * pair + h, 1)
            qm = (q2 * masks[h]).astype(BF16)
            dm = (d2 * masks[h]).astype(BF16)
            km = (k2f * masks[h]).astype(BF16)
            s = dot_nt(k2, qm)
            if bias is not None:
                s = s + bias
            p = jnp.exp(s - lset[row, at])
            dp = dot_nt(v2, dm)
            ds = (p * (dp - delta[row, at])).astype(BF16)
            ak, av, aq = dot(ds, qm), dot(p.astype(BF16), dm), dot_tn(ds, km)
            dk, dv, dq = (ak, av, aq) if dk is None else (dk + ak, dv + av, dq + aq)
        return dk, dv, dq

    everyone = slice(0, rows)

    def kv_copy(i):
        region = xfer.at[i]
        return pltpu.make_async_remote_copy(
            src_ref=region, dst_ref=region, send_sem=ksend.at[i], recv_sem=krecv.at[i],
            device_id=peers[i], device_id_type=MESH)

    def attend_remote(i):
        @pl.when(takes[i])
        def _():
            rows_of = tile_at(peers[i][0], group)

            def pair_step(pair):
                at_k, at_v = tile_at(pair, 128), tile_at(pair + pairs, 128)
                dk, dv, dq = block(pair, kv[rows_of, at_k], kv[rows_of, at_v], everyone, None)
                xfer[i, :, at_k] = dk.astype(BF16)
                xfer[i, :, at_v] = dv.astype(BF16)
                da[:, at_k] = da[:, at_k] + dq

            loop(pairs, pair_step)

    def attend_own():
        rows_of = tile_at(n, group)

        def pair_step(pair):
            at_k, at_v = tile_at(pair, 128), tile_at(pair + pairs, 128)
            dk, dv, dq = block(pair, kv[rows_of, at_k], kv[rows_of, at_v], everyone, bias_c[...])
            dqkv[share:, tile_at(pair + pairs, 128)] = dk.astype(BF16)
            dqkv[share:, tile_at(pair + 2 * pairs, 128)] = dv.astype(BF16)
            da[:, at_k] = da[:, at_k] + dq
            dk, dv, dq = block(pair, nkv[:, at_k], nkv[:, at_v], slice(0, share), bias_n[...])
            dqkv[:share, tile_at(pair + pairs, 128)] = dk.astype(BF16)
            dqkv[:share, tile_at(pair + 2 * pairs, 128)] = dv.astype(BF16)
            da[:share, at_k] = da[:share, at_k] + dq

        loop(pairs, pair_step)

    pl.semaphore_wait(barrier, jnp.where(zdev.has_outer, 6, 5))

    for turn, layer in enumerate(order):
        last = turn == layers - 1
        r_qkv, r_out, r_up, r_down = every[turn]
        prev = every[turn - 1] if turn else None
        gain1, gain2 = par[2 * layer:2 * layer + 1, :], par[2 * layer + 1:2 * layer + 2, :]
        at = 2 * layers + 2 * layer
        bias1, bias2 = par[at:at + 1, :], par[at + 1:at + 2, :]
        load = loads(layer)
        load[0].wait()
        normed_transposed(mid, gain2, bias2)
        to_bf16(db)
        da[...] = jnp.zeros_like(da)
        if prev:
            prev[0].p2()
            prev[3].p4()
            prev[2].p4()
            prev[3].free_grad()
            prev[2].free_grad()

        def ff_step(j):
            slot = lax.rem(j, 2)
            for c in stream(layer, j, slot):
                c.wait()

            @pl.when(j + 1 < tiles)
            def _():
                for c in stream(layer, j + 1, 1 - slot):
                    c.start()

            dact = dot_nt(db[...], wd_s[slot])
            gd[tile_at(j, TILE), :] = dot_tn(act_s[slot], db[...]).astype(BF16)
            du = (dact * dg_s[slot].astype(F32)).astype(BF16)
            dg_s[slot] = du
            gu[:, tile_at(j, TILE)] = dot(at_[...], dg_s[slot]).astype(BF16)
            da[...] = da[...] + dot_nt(dg_s[slot], wu_s[slot])

        loop(tiles, ff_step)
        r_down.p1()
        r_up.p1()
        norm_back(mid, gain2, 2 * layer + 1, 2 * layers + 2 * layer + 1)
        if layer:
            load_h(layer).start()
        to_bf16(db)
        if prev:
            prev[3].p5()
            prev[1].p4()
            prev[2].p5()
            prev[0].p3()
            prev[1].free_grad()
        load[1].wait()
        load[6].wait()

        def out_tile(j):
            at = tile_at(j, 256)
            go[:, at] = dot_tn(ctx[...], db[:, at]).astype(BF16)
            dctx[:, at] = dot_nt(db[...], wo[at, :]).astype(BF16)

        loop(width // 256, out_tile)
        r_out.p1()
        if layer == 0:
            load_h(layer).start()
        load[5].wait()
        lset[...] = lse[...].T

        def delta_step(pair):
            at = tile_at(pair, 128)
            both = (dctx[:, at].astype(F32) * ctx[:, at].astype(F32)).T
            for h in range(2):
                delta[pl.ds(2 * pair + h, 1), :] = jnp.sum(both[64 * h:64 * h + 64], axis=0, keepdims=True)

        loop(pairs, delta_step)
        da[...] = jnp.zeros_like(da)
        r_down.p2()
        if prev:
            prev[3].p6()
            prev[1].p5()
            prev[2].p6()
        for k in (2, 3, 4):
            load[k].wait()
        for i in (2, 1, 0):
            if turn:
                @pl.when(takes[i])
                def _():
                    kv_copy(i).wait_send()
            attend_remote(i)

            @pl.when(takes[i])
            def _():
                if turn:
                    pl.semaphore_wait(kcredit.at[i], 1)
                kv_copy(i).start()
        r_up.p2()
        r_out.p2()
        attend_own()
        r_down.p3()
        if prev:
            prev[0].p4()
            prev[3].p7()
            prev[1].p6()
            prev[2].p7()
        load_h(layer).wait()
        entry = mid if layer else db
        normed_transposed(entry, gain1, bias1)

        def query_tile(t):
            v = da[:, tile_at(t, 128)] * 0.125
            dqkv[:, tile_at(t, 128)] = (v * cosr[...] - swap_halves(v, first) * sinr[...]).astype(BF16)

        loop(pairs, query_tile)
        if prev:
            prev[0].free_grad()

        def grad_tile(j):
            at = tile_at(j, 256)
            gq[:, at] = dot(at_[...], dqkv[:, at]).astype(BF16)

        loop(width // 256, grad_tile)
        r_up.p3()
        for i in range(3):
            @pl.when(gives[i])
            def _():
                kv_copy(i).wait_recv()

        def arrived(cols):
            total = dqkv[share:, pl.ds(pl.multiple_of(width + cols, 128), 128)].astype(F32)
            for i in range(3):
                total = total + jnp.where(gives[i], xfer[i, :, pl.ds(pl.multiple_of(cols, 128), 128)].astype(F32), 0.0)
            return total

        def key_tile(t):
            at = tile_at(pairs + t, 128)
            v = jnp.concatenate([dqkv[:share, at].astype(F32), arrived(128 * t)], axis=0)
            dqkv[:, at] = (v * cosr[...] - swap_halves(v, first) * sinr[...]).astype(BF16)

        def value_tile(t):
            dqkv[share:, tile_at(2 * pairs + t, 128)] = arrived(128 * t + width).astype(BF16)

        loop(pairs, key_tile)
        loop(pairs, value_tile)
        if not last:
            for i in range(3):
                @pl.when(gives[i])
                def _():
                    pl.semaphore_signal(kcredit.at[i], inc=1, device_id=peers[i], device_id_type=MESH)

        def grad_tile_kv(j):
            grad_tile(j + width // 256)

        loop(2 * width // 256, grad_tile_kv)
        r_qkv.p1()
        load[7].wait()

        def first_tile(j):
            at = tile_at(j, 256)
            da[:, at] = dot_nt(dqkv[...], wq[at, :])

        loop(width // 256, first_tile)
        r_out.p3()
        norm_back(entry, gain1, 2 * layer, 2 * layers + 2 * layer)
        if not last:
            for c in stream(order[turn + 1], 0, 0):
                c.start()
            for c in loads(order[turn + 1]):
                c.start()
        if prev:
            prev[0].p5()
            prev[1].p7()

    prev = every[-2] if layers > 1 else None
    r_qkv, r_out, r_up, r_down = every[-1]
    tot = SmallSum(here, gacc, sbuf, ssend, srecv)
    tot.begin()
    to_bf16(grad_tok)
    r_qkv.p2()
    tot.swap(0)
    if prev:
        prev[0].p6()
        prev[3].free_zb()
        prev[2].free_zb()
    r_down.p4()
    r_up.p4()
    tot.swap(1)
    if prev:
        prev[0].p7()
        prev[1].free_zb()
    r_out.p4()
    r_qkv.p3()
    tot.swap(2)
    r_down.p5()
    r_up.p5()
    r_out.p5()
    tot.chain()
    r_down.p6()
    if prev:
        prev[0].free_zb()
    r_qkv.p4()
    r_up.p6()
    r_out.p6()
    tot.settle()
    r_down.p7()
    r_qkv.p5()
    r_up.p7()
    r_out.p7()
    r_qkv.p6()
    r_qkv.p7()
    tot.finish(small)
    for turn in every:
        for r in turn:
            r.p8()
    for r in every[-1]:
        r.free_grad()
        r.free_zb()
    for i in range(3):
        @pl.when(takes[i])
        def _():
            kv_copy(i).wait_send()


def backward(lengths, cot, tok, par, tabs, full, kept):
    cosr, sinr, bias_c, bias_n = tabs
    rows, width = cot.shape
    share = rows // 2
    layers = full[0].shape[0]
    ff = full[2].shape[2]
    hbm = pl.BlockSpec(memory_space=pltpu.HBM)
    vmem = pl.BlockSpec(memory_space=pltpu.VMEM)
    shape = jax.ShapeDtypeStruct
    v = pltpu.VMEM
    dma, regular = pltpu.SemaphoreType.DMA, pltpu.SemaphoreType.REGULAR
    outs = [shape((layers, f.shape[1] // 4, f.shape[2]), BF16) for f in full]
    scratch = [v(f.shape[1:], BF16) for f in full]
    for f in full:
        total, cols = f.shape[1:]
        quarter = total // 16
        scratch += [v((8 * quarter, cols), BF16), v((4 * quarter, cols), BF16), v((2 * quarter, cols), BF16),
                    v((2 * quarter, cols), BF16), v((quarter, cols), BF16), v((2 * quarter, cols), BF16)]
    scratch += [
        v((2, TILE, width), BF16), v((2, width, TILE), BF16), v((2, rows, TILE), BF16), v((2, rows, TILE), BF16),
        v((width, width), BF16), v((width, 3 * width), BF16),
        v((rows, width), F32), v((rows, width), F32), v((rows, width), F32),
        v((width, rows), BF16), v((rows, width), BF16),
        v((rows, width), BF16), v((4 * share, 2 * width), BF16), v((share, 2 * width), BF16),
        v((rows, width), BF16), v((rows, width), BF16),
        v((rows, 128), F32), v((128, rows), F32), v((16, rows), F32),
        v((rows, 3 * width), BF16), v((3, share, 2 * width), BF16),
        v(par.shape, F32), v((2, 6) + par.shape, F32),
        dma((SLOTS * 4 * layers,)), dma((SLOTS * 4 * layers,)), regular((7 * 4,)), dma((4 * layers,)),
        dma((3,)), dma((3,)), regular((3,)), dma((2, 4)), dma((10,)), dma((6,)), dma((6,)),
    ]
    return pl.pallas_call(
        partial(backward_kernel, layers),
        out_shape=[shape((rows, width), BF16)] + outs + [shape(par.shape, F32)],
        in_specs=[pl.BlockSpec(memory_space=pltpu.SMEM)] + [hbm] * 2 + [vmem] * 5 + [hbm] * 13,
        out_specs=[vmem] + [hbm] * 4 + [vmem],
        scratch_shapes=scratch,
        compiler_params=pltpu.CompilerParams(
            collective_id=1, has_side_effects=True, vmem_limit_bytes=63 * 2**20),
        cost_estimate=pl.CostEstimate(flops=40 * 10**9, bytes_accessed=10**8, transcendentals=10**7),
        name="backward",
    )(lengths, cot, tok, par, cosr, sinr, bias_c.T, bias_n.T, *full, *kept)


def shared_params(norm_gains, norm_biases):
    layers, _, part = norm_gains.shape
    mine = jnp.concatenate([norm_gains.reshape(2 * layers, part), norm_biases.reshape(2 * layers, part)]).astype(F32)
    parts = lax.axis_size("narrow")
    owner = jnp.arange(parts) == lax.axis_index("narrow")
    return jnp.where(owner[None, :, None], mine[:, None, :], 0.0).reshape(4 * layers, parts * part)


def attend_tables(share, head_dim):
    local = lax.axis_index("narrow") * share + jnp.arange(share, dtype=jnp.int32)
    half = head_dim // 2
    freq = jnp.exp(-jnp.log(10000.0) * jnp.arange(half, dtype=F32) * 2.0 / head_dim)
    angle = local.astype(F32)[:, None] * freq[None, :]
    cosine, sine = jnp.cos(angle), jnp.sin(angle)
    cosr = jnp.tile(jnp.concatenate([cosine, cosine], axis=1), (2, 2))
    sinr = jnp.tile(jnp.concatenate([-sine, sine], axis=1), (2, 2))
    block = jnp.arange(share, dtype=jnp.int32) // BLOCK
    same = block[:, None] == block[None, :]
    below = block[None, :] < block[:, None]
    bias = lambda allow: jnp.where(allow, 0.0, NEG).astype(F32)
    return cosr, sinr, jnp.concatenate([bias(below), bias(below | same)]), bias(same)


def on_device(tokens, lengths, w_qkv, w_out, w_up, w_down, norm_gains, norm_biases, cotangent):
    _, _, share, width = tokens.shape
    layers, _, part = norm_gains.shape
    tok = tokens.reshape(2 * share, width)
    tabs = attend_tables(share, width // H)
    outs = forward(tok, shared_params(norm_gains, norm_biases), *tabs, w_qkv, w_out, w_up, w_down)
    result, full, par, kept = outs[0], outs[1:5], outs[5], outs[6:]
    grad_tok, gq, go, gu, gd, small = backward(
        lengths, cotangent.reshape(2 * share, width), tok, par, tabs, full, kept)
    mine = lax.dynamic_slice_in_dim(small, lax.axis_index("narrow") * part, part, 1)
    gains = mine[:2 * layers].reshape(layers, 2, part)
    biases = mine[2 * layers:].reshape(layers, 2, part)
    return (
        result.reshape(tokens.shape), grad_tok.reshape(tokens.shape),
        gq.astype(F32), go.astype(F32), gu.astype(F32), gd.astype(F32),
        gains, biases[:, 0], biases[:, 1],
    )


def solution(mesh):
    return jax.shard_map(
        on_device,
        mesh=mesh,
        in_specs=(
            P("wide", None, "narrow", None),
            P("wide"),
            P(None, "narrow", None),
            P(None, "narrow", None),
            P(None, "narrow", None),
            P(None, "narrow", None),
            P(None, None, "narrow"),
            P(None, None, "narrow"),
            P("wide", None, "narrow", None),
        ),
        out_specs=(
            P("wide", None, "narrow", None),
            P("wide", None, "narrow", None),
            P(None, "narrow", None),
            P(None, "narrow", None),
            P(None, "narrow", None),
            P(None, "narrow", None),
            P(None, None, "narrow"),
            P(None, "narrow"),
            P(None, "narrow"),
        ),
        check_vma=False,
    )
```

```python
from functools import partial

import jax
import jax.numpy as jnp
import numpy as np
from jax import lax
from jax.experimental import pallas as pl
from jax.experimental.pallas import tpu as pltpu
from jax.sharding import PartitionSpec as P

H = 12
BLOCK = 16
NEG = -1e30
EPS = 1e-05
MESH = pl.DeviceIdType.MESH
F32 = jnp.float32
BF16 = jnp.bfloat16
GELU_C = 0.7978845608028654
GELU_A = 0.044715


def dot(a, b):
    return jnp.dot(a, b, preferred_element_type=F32)


def dot_nt(a, b):
    return lax.dot_general(a, b, (((1,), (1,)), ((), ())), preferred_element_type=F32)


def dot_tn(a, b):
    return lax.dot_general(a, b, (((0,), (0,)), ((), ())), preferred_element_type=F32)


def tile_at(index, size):
    return pl.ds(pl.multiple_of(index * size, size), size)


def loop(count, body):
    lax.fori_loop(0, count, lambda i, _: (body(i), None)[1], None)


def rotary(x, cosine, sine):
    lane = lax.broadcasted_iota(jnp.int32, x.shape, 1)
    swapped = jnp.where(lane % 64 < 32, pltpu.roll(x, 96, 1), pltpu.roll(x, 32, 1))
    return x * cosine + swapped * sine


def rotary_halves(x, cosine, sine):
    half = x.shape[0] // 2
    return jnp.concatenate([rotary(x[:half], cosine, sine), rotary(x[half:], cosine, sine)], axis=0)


def block_bias(query, key, strict):
    allow = key < query if strict else key <= query
    return jnp.where(allow, 0.0, NEG).astype(F32)


def blocks_of(shape, dim):
    return lax.broadcasted_iota(jnp.int32, shape, dim) // BLOCK


def head_masks():
    lane = lax.broadcasted_iota(jnp.int32, (1, 128), 1)
    low = (lane < 64).astype(F32)
    return low, 1.0 - low


def norm_into(src, dst, gain, bias, rows):
    step = 32

    def body(i):
        at = tile_at(i, step)
        x = src[at, :].astype(F32)
        c = x - jnp.mean(x, axis=-1, keepdims=True)
        inv = lax.rsqrt(jnp.mean(c * c, axis=-1, keepdims=True) + EPS)
        dst[at, :] = (c * inv * gain + bias).astype(BF16)

    loop(rows // step, body)


class Gather:
    def __init__(self, here, shard, full, send, recv, base, lsem):
        self.n, self.w = here
        self.core = lax.rem(self.w, 2)
        self.shard, self.full, self.send, self.recv, self.base, self.lsem = (
            shard, full, send, recv, base, lsem)
        self.rows = shard.shape[0]
        self.half = self.rows // 2
        self.quarter = self.rows // 4
        self.x, self.y, self.d, self.s = (
            (self.n ^ 1, self.w), (self.n ^ 2, self.w), (self.n ^ 3, self.w), (self.n, self.w ^ 1))

    def region(self, owner, core, quarter=None):
        start = owner * self.rows + core * self.half
        if quarter is None:
            return self.full.at[pl.ds(pl.multiple_of(start, 16), self.half)]
        return self.full.at[pl.ds(pl.multiple_of(start + quarter * self.quarter, 16), self.quarter)]

    def copy(self, slot, src, dst, device):
        k = self.base + slot
        return pltpu.make_async_remote_copy(
            src_ref=src, dst_ref=dst, send_sem=self.send.at[k], recv_sem=self.recv.at[k],
            device_id=device, device_id_type=MESH)

    def own(self):
        return pltpu.make_async_copy(
            self.shard, self.full.at[pl.ds(pl.multiple_of(self.n * self.rows, 16), self.rows)], self.lsem)

    def plain(self, slot, region, device):
        return self.copy(slot, region, region, device)

    def issue(self):
        src = self.shard.at[pl.ds(pl.multiple_of(self.core * self.half, 16), self.half)]
        dst = self.region(self.n, self.core)
        self.copy(0, src, dst, self.x).start()
        self.copy(1, src, dst, self.y).start()
        self.own().start()

    def forward(self):
        nx, ny = self.x[0], self.y[0]
        self.plain(0, self.region(nx, self.core), self.x).wait_recv()
        self.plain(2, self.region(nx, self.core, 0), self.y).start()
        self.plain(4, self.region(nx, self.core), self.s).start()
        self.plain(1, self.region(ny, self.core), self.y).wait_recv()
        self.plain(3, self.region(ny, self.core, 1), self.x).start()
        self.plain(5, self.region(ny, self.core), self.s).start()

    def finish(self):
        nd = self.d[0]
        self.plain(2, self.region(nd, self.core, 0), self.y).wait_recv()
        self.plain(3, self.region(nd, self.core, 1), self.x).wait_recv()
        self.plain(6, self.region(nd, self.core), self.s).start()

    def use(self):
        other = 1 - self.core
        for slot, who in ((4, self.x), (5, self.y), (6, self.d)):
            self.plain(slot, self.region(who[0], other), self.s).wait_recv()
        self.own().wait()

    def drain(self):
        src = self.shard.at[pl.ds(pl.multiple_of(self.core * self.half, 16), self.half)]
        dst = self.region(self.n, self.core)
        self.copy(0, src, dst, self.x).wait_send()
        self.copy(1, src, dst, self.y).wait_send()
        nx, ny, nd = self.x[0], self.y[0], self.d[0]
        self.plain(2, self.region(nx, self.core, 0), self.y).wait_send()
        self.plain(3, self.region(ny, self.core, 1), self.x).wait_send()
        self.plain(4, self.region(nx, self.core), self.s).wait_send()
        self.plain(5, self.region(ny, self.core), self.s).wait_send()
        self.plain(6, self.region(nd, self.core), self.s).wait_send()


def forward_kernel(
    layers,
    tok, prm, cosr, sinr, wq, wo, wu, wd,
    result, fq, fo, fu, fd, prm_out,
    h_out, q_out, nkv_out, kv_out, lse_out, ctx_out, mid_out, act_out, dg_out, near_out, all_out, post_out,
    gq, go, gu, gd, prm_buf, par, hid, a, ag, post, q, nkv, kv, bias_c, bias_n,
    score, top, lse, lset, ctx, mid, dg, act,
    send, recv, lsem, psend, precv, ksend, krecv, ssem,
):
    n = lax.axis_index("narrow")
    w = lax.axis_index("wide")
    rows, width = tok.shape
    share = rows // 2
    group = share
    pairs = width // 128
    ff = wu.shape[2]
    peers = ((n ^ 1, w), (n ^ 2, w), (n ^ 3, w))

    barrier = pltpu.get_barrier_semaphore()
    for device in peers + ((n, w ^ 1),):
        pl.semaphore_signal(barrier, inc=1, device_id=device, device_id_type=MESH)
    pl.semaphore_wait(barrier, 4)

    tensors = []
    for layer in range(layers):
        for kind, (shard, full) in enumerate(((wq, gq), (wo, go), (wu, gu), (wd, gd))):
            k = layer * 4 + kind
            tensors.append(Gather((n, w), shard.at[layer], full.at[layer], send, recv, 7 * k, lsem.at[k]))

    def params(i):
        return pltpu.make_async_remote_copy(
            src_ref=prm, dst_ref=prm_buf.at[i], send_sem=psend.at[i], recv_sem=precv.at[i],
            device_id=peers[i], device_id_type=MESH)

    def share_a(layer, i):
        region = ag.at[layer, tile_at(n, share)]
        return pltpu.make_async_remote_copy(
            src_ref=region, dst_ref=region, send_sem=ksend.at[3 * layer + i],
            recv_sem=krecv.at[3 * layer + i], device_id=peers[i], device_id_type=MESH)

    def recv_a(layer, i):
        region = ag.at[layer, tile_at(peers[i][0], share)]
        return pltpu.make_async_remote_copy(
            src_ref=region, dst_ref=region, send_sem=ksend.at[3 * layer + i],
            recv_sem=krecv.at[3 * layer + i], device_id=peers[i], device_id_type=MESH)

    gives = (n % 2 == 0, n < 2, n < 2)
    takes = (n % 2 == 1, n >= 2, n >= 2)

    for i in range(3):
        params(i).start()
    tensors[0].issue()

    def saves(layer):
        pieces = [
            (q, q_out.at[layer]), (nkv, nkv_out.at[layer]), (kv, kv_out.at[layer]),
            (lset, lse_out.at[layer]), (ctx, ctx_out.at[layer]), (mid, mid_out.at[layer]), (act, act_out.at[layer]),
            (dg, dg_out.at[layer]), (hid, h_out.at[layer]), (a.at[:share], near_out.at[layer]),
            (ag.at[layer], all_out.at[layer]), (post, post_out.at[layer]),
        ]
        return [pltpu.make_async_copy(s, d, ssem.at[layer * 12 + k]) for k, (s, d) in enumerate(pieces)]

    def weight_saves():
        pieces = ((gq, fq), (go, fo), (gu, fu), (gd, fd))
        out = []
        for layer in range(layers):
            for kind, (s, d) in enumerate(pieces):
                k = layer * 4 + kind
                out.append(pltpu.make_async_copy(s.at[layer], d.at[layer], ssem.at[12 * layers + k]))
        return out

    for i in range(3):
        params(i).wait_recv()
    par[...] = prm[...] + prm_buf[0] + prm_buf[1] + prm_buf[2]
    prm_out[...] = par[...]

    for k in range(2):
        at = slice(k * share, (k + 1) * share)
        bias_c[at] = block_bias(blocks_of((share, share), 0), blocks_of((share, share), 1), k == 0)
    same = blocks_of((share, share), 0) == blocks_of((share, share), 1)
    bias_n[...] = jnp.where(same, 0.0, NEG).astype(F32)
    masks = head_masks()
    here = tile_at(n, share)
    lanes = lax.broadcasted_iota(jnp.int32, (rows, 128), 1)

    full_saves = weight_saves()
    for layer in range(layers):
        t_qkv, t_out, t_up, t_down = tensors[4 * layer:4 * layer + 4]
        later = tensors[4 * layer + 4:]
        gain1, gain2 = par[2 * layer:2 * layer + 1, :], par[2 * layer + 1:2 * layer + 2, :]
        at = 2 * layers + 2 * layer
        bias1, bias2 = par[at:at + 1, :], par[at + 1:at + 2, :]
        saved = saves(layer)
        before = saves(layer - 1) if layer else None
        if before:
            before[9].wait()
        if layer == 0:
            norm_into(tok, a, gain1, bias1, rows)
        else:
            norm_into(hid, a, gain1, bias1, rows)
        ag[layer, here] = a[share:]
        t_qkv.forward()
        for i in range(3):
            @pl.when(gives[i])
            def _():
                share_a(layer, i).start()
        saved[9].start()
        t_out.issue()
        t_up.issue()
        t_qkv.finish()
        t_qkv.use()
        full_saves[4 * layer].start()
        if before:
            before[0].wait()
            before[1].wait()
            before[2].wait()

        wqkv = gq.at[layer]

        def query_tile(j):
            x = dot(a[...], wqkv[:, tile_at(j, 256)])
            for part in range(2):
                v = rotary_halves(x[:, 128 * part:128 * part + 128], cosr[here, :], sinr[here, :])
                q[:, tile_at(2 * j + part, 128)] = (v.astype(BF16).astype(F32) * 0.125).astype(BF16)

        def key_tile(j):
            x = dot(a[...], wqkv[:, tile_at(j + 3, 256)])
            for part in range(2):
                v = rotary_halves(x[:, 128 * part:128 * part + 128], cosr[here, :], sinr[here, :]).astype(BF16)
                nkv[:, tile_at(2 * j + part, 128)] = v[:share]
                kv[here, tile_at(2 * j + part, 128)] = v[share:]

        def value_tile(j):
            v = dot(a[...], wqkv[:, tile_at(j + 6, 256)]).astype(BF16)
            nkv[:, tile_at(j + 3, 256)] = v[:share]
            kv[here, tile_at(j + 3, 256)] = v[share:]

        def far_tiles(g):
            at = tile_at(g, share)

            def far_key(j):
                x = dot(ag[layer, at, :], wqkv[:, tile_at(j + 3, 256)])
                for part in range(2):
                    v = rotary(x[:, 128 * part:128 * part + 128], cosr[at, :], sinr[at, :])
                    kv[at, tile_at(2 * j + part, 128)] = v.astype(BF16)

            def far_value(j):
                kv[at, tile_at(j + 3, 256)] = dot(ag[layer, at, :], wqkv[:, tile_at(j + 6, 256)]).astype(BF16)

            loop(3, far_key)
            loop(3, far_value)

        loop(3, key_tile)
        loop(3, value_tile)
        loop(3, query_tile)
        saved[0].start()
        saved[1].start()
        t_down.issue()
        for i in range(3):
            @pl.when(takes[i])
            def _():
                recv_a(layer, i).wait_recv()
        saved[10].start()
        loop(n, far_tiles)
        saved[2].start()
        if before:
            before[3].wait()
            before[4].wait()

        def pair_step(pair):
            at_pair = tile_at(pair, 128)
            at_value = tile_at(pair + pairs, 128)
            q2 = q[:, at_pair].astype(F32)
            outs = []
            for h in range(2):
                qm = (q2 * masks[h]).astype(BF16)
                s = dot_nt(qm, kv[tile_at(n, group), at_pair]) + bias_c[...]
                score[:, tile_at(n, group)] = s
                top[...] = jnp.maximum(s[:, :128], s[:, 128:])
                s = dot_nt(qm[:share], nkv[:, at_pair]) + bias_n[...]
                score[:share, 4 * group:5 * group] = s
                top[:share] = jnp.maximum(top[:share], jnp.maximum(s[:, :128], s[:, 128:]))

                def scores_of(g):
                    s = dot_nt(qm, kv[tile_at(g, group), at_pair])
                    score[:, tile_at(g, group)] = s
                    top[...] = jnp.maximum(top[...], jnp.maximum(s[:, :128], s[:, 128:]))

                loop(n, scores_of)
                most = jnp.max(top[...], axis=-1, keepdims=True)
                p = jnp.exp(score[:share, 4 * group:5 * group] - most[:share])
                part = p[:, :128] + p[:, 128:]
                add = dot(p.astype(BF16), nkv[:, at_value])
                zeros = jnp.zeros((share, 128), F32)

                def probs_of(g, carry):
                    total, out = carry
                    p = jnp.exp(score[:, tile_at(g, group)] - most)
                    total = total + p[:, :128] + p[:, 128:]
                    out = out + dot(p.astype(BF16), kv[tile_at(g, group), at_value])
                    return total, out

                total, out = lax.fori_loop(
                    0, n + 1, probs_of,
                    (jnp.concatenate([part, zeros], axis=0), jnp.concatenate([add, zeros], axis=0)))
                total = jnp.sum(total, axis=-1, keepdims=True)
                outs.append(out * (masks[h] / total))
                lse[...] = jnp.where(lanes == 2 * pair + h, most + jnp.log(total), lse[...])
            ctx[:, at_pair] = (outs[0] + outs[1]).astype(BF16)

        loop(pairs // 2, pair_step)
        t_out.forward()
        t_up.forward()
        loop(pairs - pairs // 2, lambda t: pair_step(t + pairs // 2))
        lset[...] = lse[...].T[:16]
        saved[3].start()
        saved[4].start()
        t_out.finish()
        t_up.finish()
        t_down.forward()
        if later:
            later[0].issue()
        t_out.use()
        full_saves[4 * layer + 1].start()
        if before:
            before[5].wait()
            before[6].wait()
            before[7].wait()
            before[8].wait()

        def out_tile(j):
            at = tile_at(j, 256)
            base = (tok if layer == 0 else hid)[:, at].astype(F32)
            mid[:, at] = base + dot(ctx[...], go[layer, :, at])

        loop(width // 256, out_tile)
        saved[5].start()
        if before:
            before[11].wait()
        norm_into(mid, post, gain2, bias2, rows)
        saved[11].start()
        t_up.use()
        full_saves[4 * layer + 2].start()

        def up_tile(j):
            at = tile_at(j, 256)
            x = dot(post[...], gu[layer, :, at])
            x2 = x * x
            t = jnp.tanh(GELU_C * (x + GELU_A * (x * x2)))
            cdf = 0.5 + 0.5 * t
            act[:, at] = (x * cdf).astype(BF16)
            slope = GELU_C * (1.0 + 3.0 * GELU_A * x2)
            dg[:, at] = (cdf + 0.5 * x * (1.0 - t * t) * slope).astype(BF16)

        loop(ff // 256, up_tile)
        saved[6].start()
        saved[7].start()
        t_down.finish()
        t_down.use()
        full_saves[4 * layer + 3].start()

        def down_tile(j):
            at = tile_at(j, 256)
            out = mid[:, at] + dot(act[...], gd[layer, :, at])
            hid[:, at] = out
            if layer == layers - 1:
                result[:, at] = out.astype(BF16)

        loop(width // 256, down_tile)
        saved[8].start()

    for c in saves(layers - 1):
        c.wait()
    for layer in range(layers - 1):
        saves(layer)[10].wait()
    for c in full_saves:
        c.wait()
    for t in tensors:
        t.drain()
    for i in range(3):
        params(i).wait_send()
        for layer in range(layers):
            @pl.when(gives[i])
            def _():
                share_a(layer, i).wait_send()


def forward(tokens, prm, cosr, sinr, w_qkv, w_out, w_up, w_down):
    rows, width = tokens.shape
    share = rows // 2
    layers = w_qkv.shape[0]
    seq = share * 4
    qw, ff = w_qkv.shape[2], w_up.shape[2]
    full = [
        jax.ShapeDtypeStruct((layers, width, qw), BF16),
        jax.ShapeDtypeStruct((layers, width, width), BF16),
        jax.ShapeDtypeStruct((layers, width, ff), BF16),
        jax.ShapeDtypeStruct((layers, ff, width), BF16),
    ]
    hbm = pl.BlockSpec(memory_space=pltpu.HBM)
    vmem = pl.BlockSpec(memory_space=pltpu.VMEM)
    shape = jax.ShapeDtypeStruct
    kept = [
        shape((layers, rows, width), F32),
        shape((layers, rows, width), BF16),
        shape((layers, share, 2 * width), BF16),
        shape((layers, seq, 2 * width), BF16),
        shape((layers, 16, rows), F32),
        shape((layers, rows, width), BF16),
        shape((layers, rows, width), F32),
        shape((layers, rows, ff), BF16),
        shape((layers, rows, ff), BF16),
        shape((layers, share, width), BF16),
        shape((layers, seq, width), BF16),
        shape((layers, rows, width), BF16),
    ]
    dma, count = pltpu.SemaphoreType.DMA, 7 * 4 * layers
    return pl.pallas_call(
        partial(forward_kernel, layers),
        out_shape=[shape((rows, width), BF16)] + full + [shape(prm.shape, F32)] + kept,
        in_specs=[vmem] * 4 + [hbm] * 4,
        out_specs=[vmem] + [hbm] * 4 + [vmem] + [hbm] * 12,
        scratch_shapes=[pltpu.VMEM(f.shape, BF16) for f in full] + [
            pltpu.VMEM((3,) + prm.shape, F32),
            pltpu.VMEM(prm.shape, F32),
            pltpu.VMEM((rows, width), F32),
            pltpu.VMEM((rows, width), BF16),
            pltpu.VMEM((layers, seq, width), BF16),
            pltpu.VMEM((rows, width), BF16),
            pltpu.VMEM((rows, width), BF16),
            pltpu.VMEM((share, 2 * width), BF16),
            pltpu.VMEM((seq, 2 * width), BF16),
            pltpu.VMEM((rows, share), F32),
            pltpu.VMEM((share, share), F32),
            pltpu.VMEM((rows, seq + share), F32),
            pltpu.VMEM((rows, 128), F32),
            pltpu.VMEM((rows, 128), F32),
            pltpu.VMEM((16, rows), F32),
            pltpu.VMEM((rows, width), BF16),
            pltpu.VMEM((rows, width), F32),
            pltpu.VMEM((rows, ff), BF16),
            pltpu.VMEM((rows, ff), BF16),
            dma((count,)), dma((count,)), dma((4 * layers,)),
            dma((3,)), dma((3,)), dma((3 * layers,)), dma((3 * layers,)),
            dma((16 * layers,)),
        ],
        compiler_params=pltpu.CompilerParams(
            collective_id=0, has_side_effects=True, vmem_limit_bytes=62 * 2**20),
        cost_estimate=pl.CostEstimate(flops=20 * 10**9, bytes_accessed=10**8, transcendentals=10**7),
        name="forward",
    )(tokens, prm, cosr, sinr, w_qkv, w_out, w_up, w_down)


def add_rows(dst, at, left, left_at, right, right_at, rows):
    def body(i):
        step = lambda base: pl.ds(pl.multiple_of(base + 16 * i, 16), 16)
        dst[step(at), :] = left[step(left_at), :] + right[step(right_at), :]

    loop(rows // 16, body)


class Reduce:
    def __init__(self, here, turn, turns, kind, grad, bufs, out, send, recv, base, credit, cbase, lend, lsem):
        self.n, self.w = here
        self.turn, self.turns, self.kind = turn, turns, kind
        self.lend = lend
        self.grad, self.out = grad, out
        self.s1, self.r2, self.r3, self.r4, self.r5, self.zb = bufs
        self.send, self.recv, self.base = send, recv, base
        self.credit, self.cbase, self.lsem = credit, cbase, lsem
        self.core = lax.rem(self.w, 2)
        self.rows = grad.shape[0] // 4
        self.half, self.quarter = self.rows // 2, self.rows // 4
        n, w = here
        self.x, self.y, self.d, self.s = (n ^ 1, w), (n ^ 2, w), (n ^ 3, w), (n, w ^ 1)
        chips = lax.axis_size("wide") // 2
        z = w // 2
        left = z < chips // 2
        step = jnp.where(left, 2, -2)
        self.inner, self.outer = (n, w + step), (n, w - step)
        self.has_outer = jnp.logical_and(z > 0, z < chips - 1)
        self.is_mid = jnp.logical_or(z == chips // 2 - 1, z == chips // 2)
        self.mine = jnp.where(left, 0, 1)

    def at(self, owner, core, quarter=0):
        return pl.multiple_of(owner * self.rows + core * self.half + quarter * self.quarter, 16)

    def part(self, ref, start, count):
        return ref.at[pl.ds(pl.multiple_of(start, 16), count)]

    def copy(self, slot, src, dst, device):
        k = self.base + slot
        return pltpu.make_async_remote_copy(
            src_ref=src, dst_ref=dst, send_sem=self.send.at[k], recv_sem=self.recv.at[k],
            device_id=device, device_id_type=MESH)

    def take(self, slot):
        if self.turn > 0:
            pl.semaphore_wait(self.credit.at[self.cbase + slot], 1)

    def give(self, slot, device):
        if self.turn < self.turns - 1:
            pl.semaphore_signal(
                self.credit.at[self.cbase + slot], inc=1, device_id=device, device_id_type=MESH)

    def to_sibling(self):
        out = []
        for m in range(4):
            src = self.part(self.grad, self.at(m, 1 - self.core), self.half)
            out.append(self.copy(m, src, self.part(self.s1, m * self.half, self.half), self.s))
        return out

    def first_hop(self):
        q, g, c = self.quarter, self.grad, self.core
        nx, ny, nd = self.x[0], self.y[0], self.d[0]
        plan = ((4, nx, 0, 0, self.x), (5, nd, 0, 1, self.x), (6, ny, 1, 2, self.y), (7, nd, 1, 3, self.y))
        return [
            self.copy(slot, self.part(g, self.at(owner, c, quarter), q), self.part(self.r2, place * q, q), device)
            for slot, owner, quarter, place, device in plan]

    def second_hop(self):
        q, g, c = self.quarter, self.grad, self.core
        return [
            self.copy(8, self.part(g, self.at(self.y[0], c, 0), q), self.part(self.r3, 0, q), self.y),
            self.copy(9, self.part(g, self.at(self.x[0], c, 1), q), self.part(self.r3, q, q), self.x)]

    def inward(self):
        return self.copy(10, self.zb, self.r4, self.inner)

    def across(self):
        src = self.part(self.zb, (1 - self.mine) * self.quarter, self.quarter)
        return self.copy(11, src, self.r5, self.inner)

    def done_at(self, core, quarter):
        start = core * self.half + quarter * self.quarter
        return self.part(self.out, start, self.quarter)

    def final(self, quarter, device, slot, from_zb):
        dst = self.done_at(self.core, quarter)
        src = self.part(self.zb, quarter * self.quarter, self.quarter) if from_zb else dst
        return self.copy(slot, src, dst, device)

    def keep(self):
        src = self.part(self.zb, self.mine * self.quarter, self.quarter)
        return pltpu.make_async_copy(src, self.done_at(self.core, self.mine), self.lsem)

    def p1(self):
        if self.kind == "d":
            self.take(0)
        elif self.kind == "u":
            for k in range(4 if self.turn else 0):
                pl.semaphore_wait(self.lend.at[k + 4], 1)
        else:
            pl.semaphore_wait(self.lend.at["qkvo".index(self.kind)], 1)
        for c in self.to_sibling():
            c.start()

    def p2(self):
        g = self.grad
        for m, c in enumerate(self.to_sibling()):
            c.wait_recv()
            add_rows(g, self.at(m, self.core), g, self.at(m, self.core), self.s1, m * self.half, self.half)
        if self.kind == "d":
            self.give(0, self.s)
        elif self.kind == "u":
            for k in range(4):
                pl.semaphore_signal(self.lend.at[k], inc=1, device_id=self.s, device_id_type=MESH)
        elif self.turn < self.turns - 1:
            k = "qkvo".index(self.kind) + 4
            pl.semaphore_signal(self.lend.at[k], inc=1, device_id=self.s, device_id_type=MESH)

    def p2s(self):
        self.take(1)
        self.take(2)
        for c in self.first_hop():
            c.start()

    def p3(self):
        g, q = self.grad, self.quarter
        hops = self.first_hop()
        hops[1].wait_recv()
        at = self.at(self.y[0], self.core, 0)
        add_rows(g, at, g, at, self.r2, q, q)
        self.take(3)
        self.second_hop()[0].start()
        hops[3].wait_recv()
        at = self.at(self.x[0], self.core, 1)
        add_rows(g, at, g, at, self.r2, 3 * q, q)
        self.take(4)
        self.second_hop()[1].start()
        for k in range(2):
            hops[2 * k].wait_recv()
            at = self.at(self.n, self.core, k)
            add_rows(self.zb, k * q, g, at, self.r2, 2 * k * q, q)
        self.give(1, self.x)
        self.give(2, self.y)

    def p4(self):
        q = self.quarter
        for k, c in enumerate(self.second_hop()):
            c.wait_recv()
            add_rows(self.zb, k * q, self.zb, k * q, self.r3, k * q, q)
        self.give(3, self.y)
        self.give(4, self.x)

        @pl.when(jnp.logical_not(jnp.logical_or(self.has_outer, self.is_mid)))
        def _():
            self.take(5)
            self.inward().start()

    def p5(self):
        @pl.when(self.has_outer)
        def _():
            self.inward().wait_recv()
            add_rows(self.zb, 0, self.zb, 0, self.r4, 0, self.half)
            self.give(5, self.outer)

        @pl.when(self.is_mid)
        def _():
            self.take(6)
            self.across().start()

        @pl.when(jnp.logical_and(self.has_outer, jnp.logical_not(self.is_mid)))
        def _():
            self.take(5)
            self.inward().start()

    def p6(self):
        @pl.when(self.is_mid)
        def _():
            self.across().wait_recv()
            at = self.mine * self.quarter
            add_rows(self.zb, at, self.zb, at, self.r5, 0, self.quarter)
            self.give(6, self.inner)
            self.keep().start()
            self.final(self.mine, self.inner, 12, True).start()
            self.final(self.mine, self.s, 13, True).start()

        @pl.when(jnp.logical_and(self.is_mid, self.has_outer))
        def _():
            self.final(self.mine, self.outer, 15, True).start()

    def p7(self):
        other = 1 - self.mine

        @pl.when(self.is_mid)
        def _():
            self.final(other, self.inner, 12, False).wait_recv()
            self.final(other, self.s, 14, False).start()

        @pl.when(jnp.logical_and(self.is_mid, self.has_outer))
        def _():
            self.final(other, self.outer, 16, False).start()

        @pl.when(jnp.logical_not(self.is_mid))
        def _():
            self.final(self.mine, self.inner, 15, False).wait_recv()
            self.final(self.mine, self.s, 13, False).start()
            self.final(other, self.inner, 16, False).wait_recv()
            self.final(other, self.s, 14, False).start()

        @pl.when(jnp.logical_and(jnp.logical_not(self.is_mid), self.has_outer))
        def _():
            self.final(self.mine, self.outer, 15, False).start()
            self.final(other, self.outer, 16, False).start()

    def p8(self):
        for k, quarter in ((13, self.mine), (14, 1 - self.mine)):
            region = self.done_at(1 - self.core, quarter)
            self.copy(k, region, region, self.s).wait_recv()

    def free_grad(self):
        for c in self.to_sibling() + self.first_hop() + self.second_hop():
            c.wait_send()

    def free_zb(self):
        @pl.when(jnp.logical_not(self.is_mid))
        def _():
            self.inward().wait_send()

        @pl.when(self.is_mid)
        def _():
            self.across().wait_send()
            self.final(self.mine, self.inner, 12, True).wait_send()
            self.keep().wait()

        other = 1 - self.mine
        self.final(self.mine, self.s, 13, False).wait_send()
        self.final(other, self.s, 14, False).wait_send()

        @pl.when(self.has_outer)
        def _():
            self.final(self.mine, self.outer, 15, False).wait_send()
            self.final(other, self.outer, 16, False).wait_send()


SLOTS = 17


class SmallSum:
    def __init__(self, here, acc, buf, send, recv):
        n, w = here
        self.acc, self.buf, self.send, self.recv = acc, buf, send, recv
        chips = lax.axis_size("wide") // 2
        z = w // 2
        left = z < chips // 2
        step = jnp.where(left, 2, -2)
        self.inner, self.outer = (n, w + step), (n, w - step)
        self.has_outer = jnp.logical_and(z > 0, z < chips - 1)
        self.is_mid = jnp.logical_or(z == chips // 2 - 1, z == chips // 2)
        self.others = ((n, w ^ 1), (n ^ 1, w), (n ^ 2, w))

    def copy(self, slot, device):
        return pltpu.make_async_remote_copy(
            src_ref=self.buf.at[0, slot], dst_ref=self.buf.at[1, slot], send_sem=self.send.at[slot],
            recv_sem=self.recv.at[slot], device_id=device, device_id_type=MESH)

    def begin(self):
        self.buf[0, 0] = self.acc[...]
        self.copy(0, self.others[0]).start()

    def swap(self, slot):
        self.copy(slot, self.others[slot]).wait_recv()
        self.buf[0, slot + 1] = self.buf[0, slot] + self.buf[1, slot]
        if slot < 2:
            self.copy(slot + 1, self.others[slot + 1]).start()

    def chain(self):
        @pl.when(self.has_outer)
        def _():
            self.copy(3, self.outer).wait_recv()
            self.buf[0, 3] = self.buf[0, 3] + self.buf[1, 3]

        @pl.when(jnp.logical_not(self.is_mid))
        def _():
            self.copy(3, self.inner).start()

        @pl.when(self.is_mid)
        def _():
            self.buf[0, 4] = self.buf[0, 3]
            self.copy(4, self.inner).start()

    def settle(self):
        @pl.when(self.is_mid)
        def _():
            self.copy(4, self.inner).wait_recv()
            self.buf[0, 5] = self.buf[0, 4] + self.buf[1, 4]

        @pl.when(jnp.logical_not(self.is_mid))
        def _():
            self.copy(5, self.inner).wait_recv()
            self.buf[0, 5] = self.buf[1, 5]

        @pl.when(self.has_outer)
        def _():
            self.copy(5, self.outer).start()

    def finish(self, out):
        out[...] = self.buf[0, 5]
        for k in range(3):
            self.copy(k, self.others[k]).wait_send()

        @pl.when(jnp.logical_not(self.is_mid))
        def _():
            self.copy(3, self.inner).wait_send()

        @pl.when(self.is_mid)
        def _():
            self.copy(4, self.inner).wait_send()

        @pl.when(self.has_outer)
        def _():
            self.copy(5, self.outer).wait_send()


PLAN = {
    (0, "ffn2"): ("0u1",),
    (0, "out"): ("0u2", "0us",),
    (0, "send2"): ("0o1",),
    (0, "send1"): ("0d1",),
    (0, "rem0"): ("0u3",),
    (0, "q"): ("0d2", "0ds",),
    (0, "gk"): ("0q1", "0u4",),
    (0, "da"): ("0k1",),
    (0, "lna"): ("0v1", "0o2", "0k2", "0ks", "0d3", "0os",),
    (1, "ffn2"): ("0d4", "0o3",),
    (1, "lnb"): ("0k3", "0u5",),
    (1, "out"): ("0v2", "0vs", "0q2", "0qs", "0k4",),
    (1, "delta"): ("1d1",),
    (1, "rem2"): ("0v3", "0d5", "0k5",),
    (1, "send2"): ("0q3", "1u1",),
    (1, "rem1"): ("1d2", "0u6", "0v4", "1u2", "1us",),
    (1, "send1"): ("0q4", "0d6",),
    (1, "own0"): ("0u7",),
    (1, "own1"): ("1u3", "0q5",),
    (1, "tr"): ("0d7",),
    (1, "q"): ("1ds",),
    (1, "gq"): ("0k6",),
    (1, "gk"): ("0q6", "1q1", "1k1", "1u4", "0v5",),
    (1, "da"): ("0o4",),
    (9, "tot0"): ("1d3", "1v1", "0v6", "0v7", "0q7", "1k2", "1ks", "1o1",),
    (9, "tot1"): ("1d4", "1u5", "1o2", "0k7",),
    (9, "tot2"): ("0o5", "1u6", "1v2", "1vs", "1q2", "1qs",),
    (9, "tot3"): ("1k3", "0o6",),
    (9, "tot4"): ("1v3", "1os", "0o7", "1u7", "1d5", "1k4", "1o3", "1q3", "1v4", "1d6", "1k5", "1o4", "1q4", "1v5", "1d7", "1k6", "1o5", "1q5", "1v6", "1k7", "1o6", "1q6", "1v7", "1o7", "1q7",),
}
TILE = 512


def backward_kernel(
    layers,
    lens, cot, tok, par, cosr, sinr,
    fq, fo, fu, fd, h_in, q_in, nkv_in, kv_in, lse_in, ctx_in, mid_in, act_in, dg_in, near_in, all_in, post_in,
    grad_tok, oq, oo, ou, od, small,
    *rest,
):
    width = cot.shape[1]
    grads, big, small_s1 = dict(zip("qkvoud", rest[:6])), rest[6], rest[7]
    bufs = {kind: rest[8 + 5 * k:13 + 5 * k] for k, kind in enumerate("qkvoud")}
    rest = rest[38:]
    (wd_s, wu_s, act_s, dg_s, wo, wq, dh, mid, da, at_, db, q, kv, nkv, ctx, dctx, lset, delta, dqkv, dkv, xda, far, acc,
     gacc, sbuf, send, recv, credit, lend, lsem, ksend, krecv, kcredit, stsem, ldsem, ssend, srecv) = rest
    n = lax.axis_index("narrow")
    w = lax.axis_index("wide")
    here = (n, w)
    rows, width = cot.shape
    share = rows // 2
    group = share
    pairs = width // 128
    ff = act_in.shape[2]
    tiles = ff // TILE
    peers = ((n ^ 1, w), (n ^ 2, w), (n ^ 3, w))
    gives = (n % 2 == 0, n < 2, n < 2)
    takes = (n % 2 == 1, n >= 2, n >= 2)
    order = list(reversed(range(layers)))

    def reducers(turn):
        layer = order[turn]
        made = {}
        for kind, name in enumerate("qkvoud"):
            if name in "qkv":
                out = oq.at[layer, :, kind * width:(kind + 1) * width]
            else:
                out = {"o": oo, "u": ou, "d": od}[name].at[layer]
            s1 = {"u": big, "d": small_s1}.get(name)
            if s1 is None:
                s1 = big.at[:, kind * width:(kind + 1) * width]
            k = turn * 6 + kind
            made[name] = Reduce(here, turn, layers, name, grads[name], (s1,) + tuple(bufs[name]), out, send, recv,
                                SLOTS * k, credit, 7 * kind, lend, lsem.at[k])
        return made

    every = [reducers(turn) for turn in range(layers)]

    barrier = pltpu.get_barrier_semaphore()
    zdev = every[0]["q"]
    hello = peers + ((n, w ^ 1), zdev.inner)
    for device in hello:
        pl.semaphore_signal(barrier, inc=1, device_id=device, device_id_type=MESH)

    @pl.when(zdev.has_outer)
    def _():
        pl.semaphore_signal(barrier, inc=1, device_id=zdev.outer, device_id_type=MESH)

    def stream(layer, j, slot):
        cols = tile_at(j, TILE)
        return [
            pltpu.make_async_copy(fd.at[layer, cols], wd_s.at[slot], stsem.at[slot, 0]),
            pltpu.make_async_copy(fu.at[layer, :, cols], wu_s.at[slot], stsem.at[slot, 1]),
            pltpu.make_async_copy(act_in.at[layer, :, cols], act_s.at[slot], stsem.at[slot, 2]),
            pltpu.make_async_copy(dg_in.at[layer, :, cols], dg_s.at[slot], stsem.at[slot, 3]),
        ]

    def loads(layer):
        pieces = ((mid_in, mid), (ctx_in, ctx), (q_in, q), (nkv_in, nkv), (kv_in, kv), (lse_in, lset), (fo, wo), (fq, wq),
                  (post_in, dctx))
        return [pltpu.make_async_copy(s.at[layer], d, ldsem.at[k]) for k, (s, d) in enumerate(pieces)]

    def load_h(layer):
        if layer == 0:
            return pltpu.make_async_copy(tok, db, ldsem.at[10])
        return pltpu.make_async_copy(h_in.at[layer - 1], mid, ldsem.at[10])

    def load_first(layer):
        own = all_in.at[layer, tile_at(n, share)]
        return [pltpu.make_async_copy(near_in.at[layer], ctx.at[:share], ldsem.at[11]),
                pltpu.make_async_copy(own, ctx.at[share:], ldsem.at[12])]

    def load_far(layer, i):
        return pltpu.make_async_copy(all_in.at[layer, tile_at(peers[i][0], share)], far.at[i], ldsem.at[13 + i])

    for c in stream(order[0], 0, 0):
        c.start()
    for c in loads(order[0]):
        c.start()

    local = lax.broadcasted_iota(jnp.int32, (share, 1), 0) + n * share
    valid = (local < lens[0]).astype(F32)
    first_load = pltpu.make_async_copy(cot, db, ldsem.at[9])
    first_load.start()
    first_load.wait()
    for k in range(2):
        dh[k * share:(k + 1) * share] = db[k * share:(k + 1) * share, :].astype(F32) * valid
    gacc[...] = jnp.zeros_like(gacc)
    go, gu, gd = grads["o"], grads["u"], grads["d"]
    masks = head_masks()
    mine = tile_at(n, share)

    def to_bf16(dst):
        def body(i):
            at = tile_at(i, 64)
            dst[at, :] = dh[at, :].astype(BF16)

        loop(rows // 64, body)

    def norm_of(src, at):
        x = src[at, :].astype(F32)
        c = x - jnp.mean(x, axis=-1, keepdims=True)
        inv = lax.rsqrt(jnp.mean(c * c, axis=-1, keepdims=True) + EPS)
        return c * inv, inv

    def transposed(src):
        for i in range(rows // 128):
            at_[:, 128 * i:128 * i + 128] = src[128 * i:128 * i + 128, :].T

    def norm_back(src, gain, row_gain, row_bias):
        step = 32

        def body(i, carry):
            at = tile_at(i, step)
            normed, inv = norm_of(src, at)
            g = da[at, :]
            e = g * gain
            dv = inv * (e - jnp.mean(e, axis=-1, keepdims=True)
                        - normed * jnp.mean(e * normed, axis=-1, keepdims=True))
            dh[at, :] = dh[at, :] + dv
            fold = lambda v: v.reshape(step // 8, 8, width).sum(axis=0)
            return carry[0] + fold(g * normed), carry[1] + fold(g)

        zero = jnp.zeros((8, width), F32)
        one, two = lax.fori_loop(0, rows // step, body, (zero, zero))
        gacc[row_gain:row_gain + 1, :] = jnp.sum(one, axis=0, keepdims=True)
        gacc[row_bias:row_bias + 1, :] = jnp.sum(two, axis=0, keepdims=True)

    def block(pair, k2, v2, at, bias):
        at_pair = tile_at(pair, 128)
        q2 = q[at, at_pair].astype(F32)
        d2 = dctx[at, at_pair].astype(F32)
        k2f = k2.astype(F32)
        dk = dv = dq = None
        for h in range(2):
            row = pl.ds(2 * pair + h, 1)
            qm = (q2 * masks[h]).astype(BF16)
            dm = (d2 * masks[h]).astype(BF16)
            km = (k2f * masks[h]).astype(BF16)
            s = dot_nt(k2, qm)
            if bias is not None:
                s = s + bias()
            p = jnp.exp(s - lset[row, at])
            dp = dot_nt(v2, dm)
            ds = (p * (dp - delta[row, at])).astype(BF16)
            ak, av, aq = dot(ds, qm), dot(p.astype(BF16), dm), dot_tn(ds, km)
            dk, dv, dq = (ak, av, aq) if dk is None else (dk + ak, dv + av, dq + aq)
        return dk, dv, dq

    everyone = slice(0, rows)

    def kv_copy(i):
        region = xda.at[i]
        return pltpu.make_async_remote_copy(
            src_ref=region, dst_ref=region, send_sem=ksend.at[i], recv_sem=krecv.at[i],
            device_id=peers[i], device_id_type=MESH)

    def attend_remote(i):
        @pl.when(takes[i])
        def _():
            rows_of = tile_at(peers[i][0], group)

            def pair_step(pair):
                at_k, at_v = tile_at(pair, 128), tile_at(pair + pairs, 128)
                dk, dv, dq = block(pair, kv[rows_of, at_k], kv[rows_of, at_v], everyone, None)
                dkv[i, :, at_k] = rotary(dk, cosr[rows_of, :], -sinr[rows_of, :]).astype(BF16)
                dkv[i, :, at_v] = dv.astype(BF16)
                da[:, at_k] = da[:, at_k] + dq

            def away_tile(j):
                at = tile_at(j, 256)
                xda[i, :, at] = dot_nt(dkv[i], wq[at, width:3 * width]).astype(BF16)

            loop(pairs, pair_step)
            loop(width // 256, away_tile)

    def own_bias():
        key = blocks_of((group, share), 0)
        query = blocks_of((group, share), 1)
        return jnp.concatenate([block_bias(query, key, True), block_bias(query, key, False)], axis=1)

    def near_bias():
        same = blocks_of((share, share), 0) == blocks_of((share, share), 1)
        return jnp.where(same, 0.0, NEG).astype(F32)

    def attend_own(low, high):
        rows_of = tile_at(n, group)

        def pair_step(pair):
            at_k, at_v = tile_at(pair, 128), tile_at(pair + pairs, 128)
            dk, dv, dq = block(pair, kv[rows_of, at_k], kv[rows_of, at_v], everyone, own_bias)
            dqkv[share:, tile_at(pair + pairs, 128)] = rotary(dk, cosr[mine, :], -sinr[mine, :]).astype(BF16)
            dqkv[share:, tile_at(pair + 2 * pairs, 128)] = dv.astype(BF16)
            da[:, at_k] = da[:, at_k] + dq
            dk, dv, dq = block(pair, nkv[:, at_k], nkv[:, at_v], slice(0, share), near_bias)
            dqkv[:share, tile_at(pair + pairs, 128)] = rotary(dk, cosr[mine, :], -sinr[mine, :]).astype(BF16)
            dqkv[:share, tile_at(pair + 2 * pairs, 128)] = dv.astype(BF16)
            da[:share, at_k] = da[:share, at_k] + dq

        loop(high - low, lambda t: pair_step(t + low))

    pl.semaphore_wait(barrier, jnp.where(zdev.has_outer, 6, 5))

    def run(turn, slot):
        for word in PLAN.get((turn, slot), ()):
            r, act = every[int(word[0])][word[1]], word[2]
            if act == "3" and r.turn:
                every[r.turn - 1][word[1]].free_zb()
            {"1": r.p1, "2": r.p2, "s": r.p2s, "3": r.p3, "4": r.p4, "5": r.p5, "6": r.p6, "7": r.p7}[act]()

    for turn, layer in enumerate(order):
        last = turn == layers - 1
        after = lambda slot: run(turn, slot)

        def reuse(*names):
            if turn:
                for name in names:
                    every[turn - 1][name].free_grad()

        gain1, gain2 = par[2 * layer:2 * layer + 1, :], par[2 * layer + 1:2 * layer + 2, :]
        load = loads(layer)
        load[8].wait()
        transposed(dctx)
        to_bf16(db)
        da[...] = jnp.zeros_like(da)
        reuse("u", "d")

        def ff_step(j):
            slot = lax.rem(j, 2)
            for c in stream(layer, j, slot):
                c.wait()

            @pl.when(j + 1 < tiles)
            def _():
                for c in stream(layer, j + 1, 1 - slot):
                    c.start()

            dact = dot_nt(db[...], wd_s[slot])
            gd[tile_at(j, TILE), :] = dot_tn(act_s[slot], db[...]).astype(BF16)
            du = (dact * dg_s[slot].astype(F32)).astype(BF16)
            dg_s[slot] = du
            gu[:, tile_at(j, TILE)] = dot(at_[...], dg_s[slot]).astype(BF16)
            da[...] = da[...] + dot_nt(dg_s[slot], wu_s[slot])

        for k in range(3):
            low, high = tiles * k // 3, tiles * (k + 1) // 3
            loop(high - low, lambda j: ff_step(j + low))
            after("ffn%d" % k)
        load[0].wait()
        norm_back(mid, gain2, 2 * layer + 1, 2 * layers + 2 * layer + 1)
        if layer:
            load_h(layer).start()
        after("lnb")
        to_bf16(db)
        after("bf")
        load[1].wait()
        load[6].wait()
        reuse("o")

        def out_tile(j):
            at = tile_at(j, 256)
            go[:, at] = dot_tn(ctx[...], db[:, at]).astype(BF16)
            dctx[:, at] = dot_nt(db[...], wo[at, :]).astype(BF16)

        loop(width // 256, out_tile)
        after("out")
        if layer == 0:
            load_h(layer).start()
        load[5].wait()

        def delta_step(pair):
            at = tile_at(pair, 128)
            both = (dctx[:, at].astype(F32) * ctx[:, at].astype(F32)).T
            for h in range(2):
                delta[pl.ds(2 * pair + h, 1), :] = jnp.sum(both[64 * h:64 * h + 64], axis=0, keepdims=True)

        loop(pairs, delta_step)
        for c in load_first(layer):
            c.start()
        for i in range(3):
            @pl.when(takes[i])
            def _():
                load_far(layer, i).start()
        da[...] = jnp.zeros_like(da)
        after("delta")
        for k in (2, 3, 4, 7):
            load[k].wait()
        for i in (2, 1, 0):
            if turn:
                @pl.when(takes[i])
                def _():
                    kv_copy(i).wait_send()
            attend_remote(i)
            after("rem%d" % i)

            @pl.when(takes[i])
            def _():
                if turn:
                    pl.semaphore_wait(kcredit.at[i], 1)
                kv_copy(i).start()
            after("send%d" % i)
        attend_own(0, pairs // 2)
        after("own0")
        attend_own(pairs // 2, pairs)
        after("own1")
        for c in load_first(layer):
            c.wait()
        transposed(ctx)
        after("tr")

        def query_tile(t):
            v = da[:, tile_at(t, 128)] * 0.125
            dqkv[:, tile_at(t, 128)] = rotary_halves(v, cosr[mine, :], -sinr[mine, :]).astype(BF16)

        loop(pairs, query_tile)
        after("q")
        reuse("q")

        def grad_tile(j):
            at = tile_at(j, 256)
            grads["q"][:, at] = dot(at_[...], dqkv[:, at]).astype(BF16)

        loop(width // 256, grad_tile)
        after("gq")
        for i in range(3):
            @pl.when(takes[i])
            def _():
                load_far(layer, i).wait()

        def grad_tile_kv(j, skip, out):
            acc[...] = dot(at_[...], dqkv[:, tile_at(j + (1 + skip) * (width // 256), 256)])
            for i in range(3):
                @pl.when(takes[i])
                def _():
                    acc[...] = acc[...] + dot_tn(far[i], dkv[i, :, tile_at(j + skip * (width // 256), 256)])
            out[:, tile_at(j, 256)] = acc[...].astype(BF16)

        for k, name in enumerate("kv"):
            reuse(name)
            loop(width // 256, lambda j: grad_tile_kv(j, k, grads[name]))
            after("g" + name)

        def first_tile(j):
            at = tile_at(j, 256)
            da[:, at] = dot_nt(dqkv[...], wq[at, :])

        loop(width // 256, first_tile)
        after("da")
        load_h(layer).wait()
        entry = mid if layer else db
        for i in range(3):
            @pl.when(gives[i])
            def _():
                kv_copy(i).wait_recv()
                da[share:, :] = da[share:, :] + xda[i].astype(F32)
                if not last:
                    pl.semaphore_signal(kcredit.at[i], inc=1, device_id=peers[i], device_id_type=MESH)
        after("kvwait")
        norm_back(entry, gain1, 2 * layer, 2 * layers + 2 * layer)
        if not last:
            for c in stream(order[turn + 1], 0, 0):
                c.start()
            for c in loads(order[turn + 1]):
                c.start()
        after("lna")

    tot = SmallSum(here, gacc, sbuf, ssend, srecv)
    tot.begin()
    to_bf16(grad_tok)
    run(9, "tot0")
    tot.swap(0)
    run(9, "tot1")
    tot.swap(1)
    run(9, "tot2")
    tot.swap(2)
    run(9, "tot3")
    tot.chain()
    run(9, "tot4")
    tot.settle()
    tot.finish(small)
    for turn in every:
        for r in turn.values():
            r.p8()
    for r in every[-1].values():
        r.free_grad()
        r.free_zb()
    for i in range(3):
        @pl.when(takes[i])
        def _():
            kv_copy(i).wait_send()


def backward(lengths, cot, tok, par, tabs, full, kept):
    cosr, sinr = tabs
    rows, width = cot.shape
    share = rows // 2
    layers = full[0].shape[0]
    ff = full[2].shape[2]
    hbm = pl.BlockSpec(memory_space=pltpu.HBM)
    vmem = pl.BlockSpec(memory_space=pltpu.VMEM)
    shape = jax.ShapeDtypeStruct
    v = pltpu.VMEM
    dma, regular = pltpu.SemaphoreType.DMA, pltpu.SemaphoreType.REGULAR
    outs = [shape((layers, f.shape[1] // 4, f.shape[2]), BF16) for f in full]
    kinds = [(width, width)] * 4 + [(width, ff), (ff, width)]
    scratch = [v(k, BF16) for k in kinds] + [v((width // 2, ff), BF16), v((ff // 2, width), BF16)]
    for total, cols in kinds:
        quarter = total // 16
        scratch += [v((4 * quarter, cols), BF16), v((2 * quarter, cols), BF16),
                    v((2 * quarter, cols), BF16), v((quarter, cols), BF16), v((2 * quarter, cols), BF16)]
    scratch += [
        v((2, TILE, width), BF16), v((2, width, TILE), BF16), v((2, rows, TILE), BF16), v((2, rows, TILE), BF16),
        v((width, width), BF16), v((width, 3 * width), BF16),
        v((rows, width), F32), v((rows, width), F32), v((rows, width), F32),
        v((width, rows), BF16), v((rows, width), BF16),
        v((rows, width), BF16), v((4 * share, 2 * width), BF16), v((share, 2 * width), BF16),
        v((rows, width), BF16), v((rows, width), BF16),
        v((16, rows), F32), v((16, rows), F32),
        v((rows, 3 * width), BF16), v((3, share, 2 * width), BF16), v((3, share, width), BF16),
        v((3, share, width), BF16), v((width, 256), F32),
        v(par.shape, F32), v((2, 6) + par.shape, F32),
        dma((SLOTS * 6 * layers,)), dma((SLOTS * 6 * layers,)), regular((7 * 6,)), regular((8,)), dma((6 * layers,)),
        dma((3,)), dma((3,)), regular((3,)), dma((2, 4)), dma((16,)), dma((6,)), dma((6,)),
    ]
    return pl.pallas_call(
        partial(backward_kernel, layers),
        out_shape=[shape((rows, width), BF16)] + outs + [shape(par.shape, F32)],
        in_specs=[pl.BlockSpec(memory_space=pltpu.SMEM)] + [hbm] * 2 + [vmem] * 3 + [hbm] * 16,
        out_specs=[vmem] + [hbm] * 4 + [vmem],
        scratch_shapes=scratch,
        compiler_params=pltpu.CompilerParams(
            collective_id=1, has_side_effects=True, vmem_limit_bytes=63 * 2**20),
        cost_estimate=pl.CostEstimate(flops=40 * 10**9, bytes_accessed=10**8, transcendentals=10**7),
        name="backward",
    )(lengths, cot, tok, par, cosr, sinr, *full, *kept)


def shared_params(norm_gains, norm_biases):
    layers, _, part = norm_gains.shape
    mine = jnp.concatenate([norm_gains.reshape(2 * layers, part), norm_biases.reshape(2 * layers, part)]).astype(F32)
    parts = lax.axis_size("narrow")
    owner = jnp.arange(parts) == lax.axis_index("narrow")
    return jnp.where(owner[None, :, None], mine[:, None, :], 0.0).reshape(4 * layers, parts * part)


def rotary_tables(seq, head_dim):
    half = head_dim // 2
    freq = np.exp(-np.log(np.float32(10000.0)) * np.arange(half, dtype=np.float32) * np.float32(2.0) / np.float32(head_dim))
    angle = np.arange(seq, dtype=np.float32)[:, None] * freq.astype(np.float32)[None, :]
    cosine, sine = np.cos(angle), np.sin(angle)
    return (jnp.asarray(np.tile(cosine, (1, 4)), F32),
            jnp.asarray(np.tile(np.concatenate([-sine, sine], axis=1), (1, 2)), F32))


def on_device(tokens, lengths, w_qkv, w_out, w_up, w_down, norm_gains, norm_biases, cotangent):
    _, _, share, width = tokens.shape
    layers, _, part = norm_gains.shape
    tok = tokens.reshape(2 * share, width)
    tabs = rotary_tables(4 * share, width // H)
    outs = forward(tok, shared_params(norm_gains, norm_biases), *tabs, w_qkv, w_out, w_up, w_down)
    result, full, par, kept = outs[0], outs[1:5], outs[5], outs[6:]
    grad_tok, gq, go, gu, gd, small = backward(
        lengths, cotangent.reshape(2 * share, width), tok, par, tabs, full, kept)
    mine = lax.dynamic_slice_in_dim(small, lax.axis_index("narrow") * part, part, 1)
    gains = mine[:2 * layers].reshape(layers, 2, part)
    biases = mine[2 * layers:].reshape(layers, 2, part)
    return (
        result.reshape(tokens.shape), grad_tok.reshape(tokens.shape),
        gq.astype(F32), go.astype(F32), gu.astype(F32), gd.astype(F32),
        gains, biases[:, 0], biases[:, 1],
    )


def solution(mesh):
    return jax.shard_map(
        on_device,
        mesh=mesh,
        in_specs=(
            P("wide", None, "narrow", None),
            P("wide"),
            P(None, "narrow", None),
            P(None, "narrow", None),
            P(None, "narrow", None),
            P(None, "narrow", None),
            P(None, None, "narrow"),
            P(None, None, "narrow"),
            P("wide", None, "narrow", None),
        ),
        out_specs=(
            P("wide", None, "narrow", None),
            P("wide", None, "narrow", None),
            P(None, "narrow", None),
            P(None, "narrow", None),
            P(None, "narrow", None),
            P(None, "narrow", None),
            P(None, None, "narrow"),
            P(None, "narrow"),
            P(None, "narrow"),
        ),
        check_vma=False,
    )
```

```python
from functools import partial

import jax
import jax.numpy as jnp
import numpy as np
from jax import lax
from jax.experimental import pallas as pl
from jax.experimental.pallas import tpu as pltpu
from jax.sharding import PartitionSpec as P

H = 12
BLOCK = 16
NEG = -1e30
EPS = 1e-05
MESH = pl.DeviceIdType.MESH
F32 = jnp.float32
BF16 = jnp.bfloat16
GELU_C = 0.7978845608028654
GELU_A = 0.044715


def dot(a, b):
    return jnp.dot(a, b, preferred_element_type=F32)


def dot_nt(a, b):
    return lax.dot_general(a, b, (((1,), (1,)), ((), ())), preferred_element_type=F32)


def dot_tn(a, b):
    return lax.dot_general(a, b, (((0,), (0,)), ((), ())), preferred_element_type=F32)


def tile_at(index, size):
    return pl.ds(pl.multiple_of(index * size, size), size)


def loop(count, body):
    lax.fori_loop(0, count, lambda i, _: (body(i), None)[1], None)


def rotary(x, cosine, sine):
    lane = lax.broadcasted_iota(jnp.int32, x.shape, 1)
    swapped = jnp.where(lane % 64 < 32, pltpu.roll(x, 96, 1), pltpu.roll(x, 32, 1))
    return x * cosine + swapped * sine


def rotary_halves(x, cosine, sine):
    half = x.shape[0] // 2
    return jnp.concatenate([rotary(x[:half], cosine, sine), rotary(x[half:], cosine, sine)], axis=0)


def block_bias(query, key, strict):
    allow = key < query if strict else key <= query
    return jnp.where(allow, 0.0, NEG).astype(F32)


def blocks_of(shape, dim):
    return lax.broadcasted_iota(jnp.int32, shape, dim) // BLOCK


def head_masks():
    lane = lax.broadcasted_iota(jnp.int32, (1, 128), 1)
    low = (lane < 64).astype(F32)
    return low, 1.0 - low


def norm_into(src, dst, gain, bias, rows):
    step = 256

    def body(i):
        at = tile_at(i, step)
        x = src[at, :].astype(F32)
        c = x - jnp.mean(x, axis=-1, keepdims=True)
        inv = lax.rsqrt(jnp.mean(c * c, axis=-1, keepdims=True) + EPS)
        dst[at, :] = (c * inv * gain + bias).astype(BF16)

    loop(rows // step, body)


class Gather:
    def __init__(self, here, shard, full, send, recv, base, lsem):
        self.n, self.w = here
        self.core = lax.rem(self.w, 2)
        self.shard, self.full, self.send, self.recv, self.base, self.lsem = (
            shard, full, send, recv, base, lsem)
        self.rows = shard.shape[0]
        self.half = self.rows // 2
        self.quarter = self.rows // 4
        self.x, self.y, self.d, self.s = (
            (self.n ^ 1, self.w), (self.n ^ 2, self.w), (self.n ^ 3, self.w), (self.n, self.w ^ 1))

    def region(self, owner, core, quarter=None):
        start = owner * self.rows + core * self.half
        if quarter is None:
            return self.full.at[pl.ds(pl.multiple_of(start, 16), self.half)]
        return self.full.at[pl.ds(pl.multiple_of(start + quarter * self.quarter, 16), self.quarter)]

    def copy(self, slot, src, dst, device):
        k = self.base + slot
        return pltpu.make_async_remote_copy(
            src_ref=src, dst_ref=dst, send_sem=self.send.at[k], recv_sem=self.recv.at[k],
            device_id=device, device_id_type=MESH)

    def own(self):
        return pltpu.make_async_copy(
            self.shard, self.full.at[pl.ds(pl.multiple_of(self.n * self.rows, 16), self.rows)], self.lsem)

    def plain(self, slot, region, device):
        return self.copy(slot, region, region, device)

    def issue(self):
        src = self.shard.at[pl.ds(pl.multiple_of(self.core * self.half, 16), self.half)]
        dst = self.region(self.n, self.core)
        self.copy(0, src, dst, self.x).start()
        self.copy(1, src, dst, self.y).start()
        self.own().start()

    def forward(self):
        nx, ny = self.x[0], self.y[0]
        self.plain(0, self.region(nx, self.core), self.x).wait_recv()
        self.plain(2, self.region(nx, self.core, 0), self.y).start()
        self.plain(4, self.region(nx, self.core), self.s).start()
        self.plain(1, self.region(ny, self.core), self.y).wait_recv()
        self.plain(3, self.region(ny, self.core, 1), self.x).start()
        self.plain(5, self.region(ny, self.core), self.s).start()

    def finish(self):
        nd = self.d[0]
        self.plain(2, self.region(nd, self.core, 0), self.y).wait_recv()
        self.plain(3, self.region(nd, self.core, 1), self.x).wait_recv()
        self.plain(6, self.region(nd, self.core), self.s).start()

    def use(self):
        other = 1 - self.core
        for slot, who in ((4, self.x), (5, self.y), (6, self.d)):
            self.plain(slot, self.region(who[0], other), self.s).wait_recv()
        self.own().wait()

    def drain(self):
        src = self.shard.at[pl.ds(pl.multiple_of(self.core * self.half, 16), self.half)]
        dst = self.region(self.n, self.core)
        self.copy(0, src, dst, self.x).wait_send()
        self.copy(1, src, dst, self.y).wait_send()
        nx, ny, nd = self.x[0], self.y[0], self.d[0]
        self.plain(2, self.region(nx, self.core, 0), self.y).wait_send()
        self.plain(3, self.region(ny, self.core, 1), self.x).wait_send()
        self.plain(4, self.region(nx, self.core), self.s).wait_send()
        self.plain(5, self.region(ny, self.core), self.s).wait_send()
        self.plain(6, self.region(nd, self.core), self.s).wait_send()


def forward_kernel(
    layers,
    tok, prm, cosr, sinr, wq, wo, wu, wd,
    result, fq, fo, fu, fd, prm_out,
    h_out, q_out, nkv_out, kv_out, lse_out, ctx_out, mid_out, act_out, dg_out, near_out, all_out, post_out,
    gq, go, gu, gd, prm_buf, par, hid, a, ag, post, q, nkv, kv, bias_c, bias_n,
    lset, ctx, mid, dg, act,
    send, recv, lsem, psend, precv, ksend, krecv, ssem,
):
    n = lax.axis_index("narrow")
    w = lax.axis_index("wide")
    rows, width = tok.shape
    share = rows // 2
    group = share
    pairs = width // 128
    ff = wu.shape[2]
    peers = ((n ^ 1, w), (n ^ 2, w), (n ^ 3, w))

    barrier = pltpu.get_barrier_semaphore()
    for device in peers + ((n, w ^ 1),):
        pl.semaphore_signal(barrier, inc=1, device_id=device, device_id_type=MESH)
    pl.semaphore_wait(barrier, 4)

    tensors = []
    for layer in range(layers):
        for kind, (shard, full) in enumerate(((wq, gq), (wo, go), (wu, gu), (wd, gd))):
            k = layer * 4 + kind
            tensors.append(Gather((n, w), shard.at[layer], full.at[layer], send, recv, 7 * k, lsem.at[k]))

    def params(i):
        return pltpu.make_async_remote_copy(
            src_ref=prm, dst_ref=prm_buf.at[i], send_sem=psend.at[i], recv_sem=precv.at[i],
            device_id=peers[i], device_id_type=MESH)

    def share_a(layer, i):
        region = ag.at[layer, tile_at(n, share)]
        return pltpu.make_async_remote_copy(
            src_ref=region, dst_ref=region, send_sem=ksend.at[3 * layer + i],
            recv_sem=krecv.at[3 * layer + i], device_id=peers[i], device_id_type=MESH)

    def recv_a(layer, i):
        region = ag.at[layer, tile_at(peers[i][0], share)]
        return pltpu.make_async_remote_copy(
            src_ref=region, dst_ref=region, send_sem=ksend.at[3 * layer + i],
            recv_sem=krecv.at[3 * layer + i], device_id=peers[i], device_id_type=MESH)

    gives = (n % 2 == 0, n < 2, n < 2)
    takes = (n % 2 == 1, n >= 2, n >= 2)

    for i in range(3):
        params(i).start()
    tensors[0].issue()

    def saves(layer):
        pieces = [
            (q, q_out.at[layer]), (nkv, nkv_out.at[layer]), (kv, kv_out.at[layer]),
            (lset, lse_out.at[layer]), (ctx, ctx_out.at[layer]), (mid, mid_out.at[layer]), (act, act_out.at[layer]),
            (dg, dg_out.at[layer]), (hid, h_out.at[layer]), (a.at[:share], near_out.at[layer]),
            (ag.at[layer], all_out.at[layer]), (post, post_out.at[layer]),
        ]
        return [pltpu.make_async_copy(s, d, ssem.at[layer * 12 + k]) for k, (s, d) in enumerate(pieces)]

    def weight_saves():
        pieces = ((gq, fq), (go, fo), (gu, fu), (gd, fd))
        out = []
        for layer in range(layers):
            for kind, (s, d) in enumerate(pieces):
                k = layer * 4 + kind
                out.append(pltpu.make_async_copy(s.at[layer], d.at[layer], ssem.at[12 * layers + k]))
        return out

    for i in range(3):
        params(i).wait_recv()
    par[...] = prm[...] + prm_buf[0] + prm_buf[1] + prm_buf[2]
    prm_out[...] = par[...]

    for k in range(2):
        at = slice(k * share, (k + 1) * share)
        bias_c[:, at] = block_bias(blocks_of((share, share), 1), blocks_of((share, share), 0), k == 0)
    same = blocks_of((share, share), 0) == blocks_of((share, share), 1)
    bias_n[...] = jnp.where(same, 0.0, NEG).astype(F32)
    masks = head_masks()
    here = tile_at(n, share)

    full_saves = weight_saves()
    for layer in range(layers):
        t_qkv, t_out, t_up, t_down = tensors[4 * layer:4 * layer + 4]
        later = tensors[4 * layer + 4:]
        gain1, gain2 = par[2 * layer:2 * layer + 1, :], par[2 * layer + 1:2 * layer + 2, :]
        at = 2 * layers + 2 * layer
        bias1, bias2 = par[at:at + 1, :], par[at + 1:at + 2, :]
        saved = saves(layer)
        before = saves(layer - 1) if layer else None
        if before:
            before[9].wait()
        if layer == 0:
            norm_into(tok, a, gain1, bias1, rows)
        else:
            norm_into(hid, a, gain1, bias1, rows)
        ag[layer, here] = a[share:]
        t_qkv.forward()
        for i in range(3):
            @pl.when(gives[i])
            def _():
                share_a(layer, i).start()
        saved[9].start()
        t_out.issue()
        t_up.issue()
        t_qkv.finish()
        t_qkv.use()
        full_saves[4 * layer].start()
        if before:
            before[0].wait()
            before[1].wait()
            before[2].wait()

        wqkv = gq.at[layer]

        def query_tile(j):
            x = dot(a[...], wqkv[:, tile_at(j, 256)])
            for part in range(2):
                v = rotary_halves(x[:, 128 * part:128 * part + 128], cosr[here, :], sinr[here, :])
                q[:, tile_at(2 * j + part, 128)] = (v.astype(BF16).astype(F32) * 0.125).astype(BF16)

        def key_tile(j):
            x = dot(a[...], wqkv[:, tile_at(j + 3, 256)])
            for part in range(2):
                v = rotary_halves(x[:, 128 * part:128 * part + 128], cosr[here, :], sinr[here, :]).astype(BF16)
                nkv[:, tile_at(2 * j + part, 128)] = v[:share]
                kv[here, tile_at(2 * j + part, 128)] = v[share:]

        def value_tile(j):
            v = dot(a[...], wqkv[:, tile_at(j + 6, 256)]).astype(BF16)
            nkv[:, tile_at(j + 3, 256)] = v[:share]
            kv[here, tile_at(j + 3, 256)] = v[share:]

        def far_tiles(g):
            at = tile_at(g, share)

            def far_key(j):
                x = dot(ag[layer, at, :], wqkv[:, tile_at(j + 3, 256)])
                for part in range(2):
                    v = rotary(x[:, 128 * part:128 * part + 128], cosr[at, :], sinr[at, :])
                    kv[at, tile_at(2 * j + part, 128)] = v.astype(BF16)

            def far_value(j):
                kv[at, tile_at(j + 3, 256)] = dot(ag[layer, at, :], wqkv[:, tile_at(j + 6, 256)]).astype(BF16)

            loop(3, far_key)
            loop(3, far_value)

        loop(3, key_tile)
        loop(3, value_tile)
        loop(3, query_tile)
        saved[0].start()
        saved[1].start()
        t_down.issue()
        for i in range(3):
            @pl.when(takes[i])
            def _():
                recv_a(layer, i).wait_recv()
        saved[10].start()
        loop(n, far_tiles)
        saved[2].start()
        if before:
            before[3].wait()
            before[4].wait()

        def fold(v, how):
            v = v.reshape(v.shape[0] // 8, 8, v.shape[1])
            return how(how(v, axis=0), axis=0, keepdims=True)

        def pair_step(pair):
            at_pair = tile_at(pair, 128)
            at_value = tile_at(pair + pairs, 128)
            q2 = q[:, at_pair].astype(F32)
            qm = [(q2 * masks[h]).astype(BF16) for h in range(2)]
            lower = [slice(64 * h, 64 * h + 64) for h in range(2)]

            def absorb(s, v2, carry):
                most, total, out = carry
                peak = jnp.maximum(most, fold(s, jnp.max))
                p = jnp.exp(s - peak)
                shrink = jnp.exp(most - peak)
                total = total * shrink + fold(p, jnp.sum)
                out = out * shrink + dot(v2, p.astype(BF16))
                return peak, total, out

            near_v = nkv[:, at_value].T
            own_v = kv[here, at_value].T
            blank = (jnp.full((1, share), NEG, F32), jnp.zeros((1, share), F32), jnp.zeros((64, share), F32))
            states = []
            for h in range(2):
                s = dot_nt(nkv[:, at_pair], qm[h][:share]) + bias_n[...]
                most = fold(s, jnp.max)
                p = jnp.exp(s - most)
                near = (most, fold(p, jnp.sum), dot(near_v[lower[h]], p.astype(BF16)))
                state = tuple(jnp.concatenate([a, b], axis=1) for a, b in zip(near, blank))
                s = dot_nt(kv[here, at_pair], qm[h]) + bias_c[...]
                states.append(absorb(s, own_v[lower[h]], state))

            def far_step(g, states):
                at = tile_at(g, group)
                far_v = kv[at, at_value].T
                scores = [dot_nt(kv[at, at_pair], qm[h]) for h in range(2)]
                return tuple(absorb(scores[h], far_v[lower[h]], states[h]) for h in range(2))

            states = lax.fori_loop(0, n, far_step, tuple(states))
            outs = []
            for h, (most, total, out) in enumerate(states):
                outs.append(out / total)
                lset[pl.ds(2 * pair + h, 1), :] = most + jnp.log(total)
            ctx[:, at_pair] = jnp.concatenate(outs, axis=0).T.astype(BF16)

        loop(pairs // 2, pair_step)
        t_out.forward()
        t_up.forward()
        loop(pairs - pairs // 2, lambda t: pair_step(t + pairs // 2))
        saved[3].start()
        saved[4].start()
        t_out.finish()
        t_up.finish()
        t_down.forward()
        if later:
            later[0].issue()
        t_out.use()
        full_saves[4 * layer + 1].start()
        if before:
            before[5].wait()
            before[6].wait()
            before[7].wait()
            before[8].wait()

        def out_tile(j):
            at = tile_at(j, 256)
            base = (tok if layer == 0 else hid)[:, at].astype(F32)
            mid[:, at] = base + dot(ctx[...], go[layer, :, at])

        loop(width // 256, out_tile)
        saved[5].start()
        if before:
            before[11].wait()
        norm_into(mid, post, gain2, bias2, rows)
        saved[11].start()
        t_up.use()
        full_saves[4 * layer + 2].start()

        def up_tile(j):
            at = tile_at(j, 256)
            x = dot(post[...], gu[layer, :, at])
            x2 = x * x
            t = jnp.tanh(GELU_C * (x + GELU_A * (x * x2)))
            cdf = 0.5 + 0.5 * t
            act[:, at] = (x * cdf).astype(BF16)
            slope = GELU_C * (1.0 + 3.0 * GELU_A * x2)
            dg[:, at] = (cdf + 0.5 * x * (1.0 - t * t) * slope).astype(BF16)

        loop(ff // 256, up_tile)
        saved[6].start()
        saved[7].start()
        t_down.finish()
        t_down.use()
        full_saves[4 * layer + 3].start()

        def down_tile(j):
            at = tile_at(j, 256)
            out = mid[:, at] + dot(act[...], gd[layer, :, at])
            hid[:, at] = out
            if layer == layers - 1:
                result[:, at] = out.astype(BF16)

        loop(width // 256, down_tile)
        saved[8].start()

    for c in saves(layers - 1):
        c.wait()
    for layer in range(layers - 1):
        saves(layer)[10].wait()
    for c in full_saves:
        c.wait()
    for t in tensors:
        t.drain()
    for i in range(3):
        params(i).wait_send()
        for layer in range(layers):
            @pl.when(gives[i])
            def _():
                share_a(layer, i).wait_send()


def forward(tokens, prm, cosr, sinr, w_qkv, w_out, w_up, w_down):
    rows, width = tokens.shape
    share = rows // 2
    layers = w_qkv.shape[0]
    seq = share * 4
    qw, ff = w_qkv.shape[2], w_up.shape[2]
    full = [
        jax.ShapeDtypeStruct((layers, width, qw), BF16),
        jax.ShapeDtypeStruct((layers, width, width), BF16),
        jax.ShapeDtypeStruct((layers, width, ff), BF16),
        jax.ShapeDtypeStruct((layers, ff, width), BF16),
    ]
    hbm = pl.BlockSpec(memory_space=pltpu.HBM)
    vmem = pl.BlockSpec(memory_space=pltpu.VMEM)
    shape = jax.ShapeDtypeStruct
    kept = [
        shape((layers, rows, width), F32),
        shape((layers, rows, width), BF16),
        shape((layers, share, 2 * width), BF16),
        shape((layers, seq, 2 * width), BF16),
        shape((layers, 16, rows), F32),
        shape((layers, rows, width), BF16),
        shape((layers, rows, width), F32),
        shape((layers, rows, ff), BF16),
        shape((layers, rows, ff), BF16),
        shape((layers, share, width), BF16),
        shape((layers, seq, width), BF16),
        shape((layers, rows, width), BF16),
    ]
    dma, count = pltpu.SemaphoreType.DMA, 7 * 4 * layers
    return pl.pallas_call(
        partial(forward_kernel, layers),
        out_shape=[shape((rows, width), BF16)] + full + [shape(prm.shape, F32)] + kept,
        in_specs=[vmem] * 4 + [hbm] * 4,
        out_specs=[vmem] + [hbm] * 4 + [vmem] + [hbm] * 12,
        scratch_shapes=[pltpu.VMEM(f.shape, BF16) for f in full] + [
            pltpu.VMEM((3,) + prm.shape, F32),
            pltpu.VMEM(prm.shape, F32),
            pltpu.VMEM((rows, width), F32),
            pltpu.VMEM((rows, width), BF16),
            pltpu.VMEM((layers, seq, width), BF16),
            pltpu.VMEM((rows, width), BF16),
            pltpu.VMEM((rows, width), BF16),
            pltpu.VMEM((share, 2 * width), BF16),
            pltpu.VMEM((seq, 2 * width), BF16),
            pltpu.VMEM((share, rows), F32),
            pltpu.VMEM((share, share), F32),
            pltpu.VMEM((16, rows), F32),
            pltpu.VMEM((rows, width), BF16),
            pltpu.VMEM((rows, width), F32),
            pltpu.VMEM((rows, ff), BF16),
            pltpu.VMEM((rows, ff), BF16),
            dma((count,)), dma((count,)), dma((4 * layers,)),
            dma((3,)), dma((3,)), dma((3 * layers,)), dma((3 * layers,)),
            dma((16 * layers,)),
        ],
        compiler_params=pltpu.CompilerParams(
            collective_id=0, has_side_effects=True, vmem_limit_bytes=62 * 2**20),
        cost_estimate=pl.CostEstimate(flops=20 * 10**9, bytes_accessed=10**8, transcendentals=10**7),
        name="forward",
    )(tokens, prm, cosr, sinr, w_qkv, w_out, w_up, w_down)


def add_rows(dst, at, left, left_at, right, right_at, rows):
    size = 48 if rows % 48 == 0 else 16

    def body(i):
        step = lambda base: pl.ds(pl.multiple_of(base + size * i, 16), size)
        dst[step(at), :] = left[step(left_at), :] + right[step(right_at), :]

    loop(rows // size, body)


class Reduce:
    def __init__(self, here, turn, turns, kind, grad, bufs, out, send, recv, base, credit, cbase, lend, lsem):
        self.n, self.w = here
        self.turn, self.turns, self.kind = turn, turns, kind
        self.lend = lend
        self.grad, self.out = grad, out
        self.s1, self.r2, self.r3, self.r4, self.r5, self.zb = bufs
        self.send, self.recv, self.base = send, recv, base
        self.credit, self.cbase, self.lsem = credit, cbase, lsem
        self.core = lax.rem(self.w, 2)
        self.rows = grad.shape[0] // 4
        self.half, self.quarter = self.rows // 2, self.rows // 4
        n, w = here
        self.x, self.y, self.d, self.s = (n ^ 1, w), (n ^ 2, w), (n ^ 3, w), (n, w ^ 1)
        chips = lax.axis_size("wide") // 2
        z = w // 2
        left = z < chips // 2
        step = jnp.where(left, 2, -2)
        self.inner, self.outer = (n, w + step), (n, w - step)
        self.has_outer = jnp.logical_and(z > 0, z < chips - 1)
        self.is_mid = jnp.logical_or(z == chips // 2 - 1, z == chips // 2)
        self.mine = jnp.where(left, 0, 1)

    def at(self, owner, core, quarter=0):
        return pl.multiple_of(owner * self.rows + core * self.half + quarter * self.quarter, 16)

    def part(self, ref, start, count):
        return ref.at[pl.ds(pl.multiple_of(start, 16), count)]

    def copy(self, slot, src, dst, device):
        k = self.base + slot
        return pltpu.make_async_remote_copy(
            src_ref=src, dst_ref=dst, send_sem=self.send.at[k], recv_sem=self.recv.at[k],
            device_id=device, device_id_type=MESH)

    def take(self, slot):
        if self.turn > 0:
            pl.semaphore_wait(self.credit.at[self.cbase + slot], 1)

    def give(self, slot, device):
        if self.turn < self.turns - 1:
            pl.semaphore_signal(
                self.credit.at[self.cbase + slot], inc=1, device_id=device, device_id_type=MESH)

    def to_sibling(self):
        out = []
        for m in range(4):
            src = self.part(self.grad, self.at(m, 1 - self.core), self.half)
            out.append(self.copy(m, src, self.part(self.s1, m * self.half, self.half), self.s))
        return out

    def first_hop(self):
        q, g, c = self.quarter, self.grad, self.core
        nx, ny, nd = self.x[0], self.y[0], self.d[0]
        plan = ((4, nx, 0, 0, self.x), (5, nd, 0, 1, self.x), (6, ny, 1, 2, self.y), (7, nd, 1, 3, self.y))
        return [
            self.copy(slot, self.part(g, self.at(owner, c, quarter), q), self.part(self.r2, place * q, q), device)
            for slot, owner, quarter, place, device in plan]

    def second_hop(self):
        q, g, c = self.quarter, self.grad, self.core
        return [
            self.copy(8, self.part(g, self.at(self.y[0], c, 0), q), self.part(self.r3, 0, q), self.y),
            self.copy(9, self.part(g, self.at(self.x[0], c, 1), q), self.part(self.r3, q, q), self.x)]

    def inward(self):
        return self.copy(10, self.zb, self.r4, self.inner)

    def across(self):
        src = self.part(self.zb, (1 - self.mine) * self.quarter, self.quarter)
        return self.copy(11, src, self.r5, self.inner)

    def done_at(self, core, quarter):
        start = core * self.half + quarter * self.quarter
        return self.part(self.out, start, self.quarter)

    def final(self, quarter, device, slot, from_zb):
        dst = self.done_at(self.core, quarter)
        src = self.part(self.zb, quarter * self.quarter, self.quarter) if from_zb else dst
        return self.copy(slot, src, dst, device)

    def keep(self):
        src = self.part(self.zb, self.mine * self.quarter, self.quarter)
        return pltpu.make_async_copy(src, self.done_at(self.core, self.mine), self.lsem)

    def p1(self):
        if self.kind == "d":
            self.take(0)
        elif self.kind == "u":
            for k in range(4 if self.turn else 0):
                pl.semaphore_wait(self.lend.at[k + 4], 1)
        else:
            pl.semaphore_wait(self.lend.at["qkvo".index(self.kind)], 1)
        for c in self.to_sibling():
            c.start()

    def p2(self):
        g = self.grad
        for m, c in enumerate(self.to_sibling()):
            c.wait_recv()
            add_rows(g, self.at(m, self.core), g, self.at(m, self.core), self.s1, m * self.half, self.half)
        if self.kind == "d":
            self.give(0, self.s)
        elif self.kind == "u":
            for k in range(4):
                pl.semaphore_signal(self.lend.at[k], inc=1, device_id=self.s, device_id_type=MESH)
        elif self.turn < self.turns - 1:
            k = "qkvo".index(self.kind) + 4
            pl.semaphore_signal(self.lend.at[k], inc=1, device_id=self.s, device_id_type=MESH)

    def p2s(self):
        self.take(1)
        self.take(2)
        for c in self.first_hop():
            c.start()

    def p3(self):
        g, q = self.grad, self.quarter
        hops = self.first_hop()
        hops[1].wait_recv()
        at = self.at(self.y[0], self.core, 0)
        add_rows(g, at, g, at, self.r2, q, q)
        self.take(3)
        self.second_hop()[0].start()
        hops[3].wait_recv()
        at = self.at(self.x[0], self.core, 1)
        add_rows(g, at, g, at, self.r2, 3 * q, q)
        self.take(4)
        self.second_hop()[1].start()
        for k in range(2):
            hops[2 * k].wait_recv()
            at = self.at(self.n, self.core, k)
            add_rows(self.zb, k * q, g, at, self.r2, 2 * k * q, q)
        self.give(1, self.x)
        self.give(2, self.y)

    def p4(self):
        q = self.quarter
        for k, c in enumerate(self.second_hop()):
            c.wait_recv()
            add_rows(self.zb, k * q, self.zb, k * q, self.r3, k * q, q)
        self.give(3, self.y)
        self.give(4, self.x)

        @pl.when(jnp.logical_not(jnp.logical_or(self.has_outer, self.is_mid)))
        def _():
            self.take(5)
            self.inward().start()

    def p5(self):
        @pl.when(self.has_outer)
        def _():
            self.inward().wait_recv()
            add_rows(self.zb, 0, self.zb, 0, self.r4, 0, self.half)
            self.give(5, self.outer)

        @pl.when(self.is_mid)
        def _():
            self.take(6)
            self.across().start()

        @pl.when(jnp.logical_and(self.has_outer, jnp.logical_not(self.is_mid)))
        def _():
            self.take(5)
            self.inward().start()

    def p6(self):
        @pl.when(self.is_mid)
        def _():
            self.across().wait_recv()
            at = self.mine * self.quarter
            add_rows(self.zb, at, self.zb, at, self.r5, 0, self.quarter)
            self.give(6, self.inner)
            self.keep().start()
            self.final(self.mine, self.inner, 12, True).start()
            self.final(self.mine, self.s, 13, True).start()

        @pl.when(jnp.logical_and(self.is_mid, self.has_outer))
        def _():
            self.final(self.mine, self.outer, 15, True).start()

    def p7(self):
        other = 1 - self.mine

        @pl.when(self.is_mid)
        def _():
            self.final(other, self.inner, 12, False).wait_recv()
            self.final(other, self.s, 14, False).start()

        @pl.when(jnp.logical_and(self.is_mid, self.has_outer))
        def _():
            self.final(other, self.outer, 16, False).start()

        @pl.when(jnp.logical_not(self.is_mid))
        def _():
            self.final(self.mine, self.inner, 15, False).wait_recv()
            self.final(self.mine, self.s, 13, False).start()
            self.final(other, self.inner, 16, False).wait_recv()
            self.final(other, self.s, 14, False).start()

        @pl.when(jnp.logical_and(jnp.logical_not(self.is_mid), self.has_outer))
        def _():
            self.final(self.mine, self.outer, 15, False).start()
            self.final(other, self.outer, 16, False).start()

    def p8(self):
        for k, quarter in ((13, self.mine), (14, 1 - self.mine)):
            region = self.done_at(1 - self.core, quarter)
            self.copy(k, region, region, self.s).wait_recv()

    def free_grad(self):
        for c in self.to_sibling() + self.first_hop() + self.second_hop():
            c.wait_send()

    def free_zb(self):
        @pl.when(jnp.logical_not(self.is_mid))
        def _():
            self.inward().wait_send()

        @pl.when(self.is_mid)
        def _():
            self.across().wait_send()
            self.final(self.mine, self.inner, 12, True).wait_send()
            self.keep().wait()

        other = 1 - self.mine
        self.final(self.mine, self.s, 13, False).wait_send()
        self.final(other, self.s, 14, False).wait_send()

        @pl.when(self.has_outer)
        def _():
            self.final(self.mine, self.outer, 15, False).wait_send()
            self.final(other, self.outer, 16, False).wait_send()


SLOTS = 17


class SmallSum:
    def __init__(self, here, acc, buf, send, recv):
        n, w = here
        self.acc, self.buf, self.send, self.recv = acc, buf, send, recv
        chips = lax.axis_size("wide") // 2
        z = w // 2
        left = z < chips // 2
        step = jnp.where(left, 2, -2)
        self.inner, self.outer = (n, w + step), (n, w - step)
        self.has_outer = jnp.logical_and(z > 0, z < chips - 1)
        self.is_mid = jnp.logical_or(z == chips // 2 - 1, z == chips // 2)
        self.others = ((n, w ^ 1), (n ^ 1, w), (n ^ 2, w))

    def copy(self, slot, device):
        return pltpu.make_async_remote_copy(
            src_ref=self.buf.at[0, slot], dst_ref=self.buf.at[1, slot], send_sem=self.send.at[slot],
            recv_sem=self.recv.at[slot], device_id=device, device_id_type=MESH)

    def begin(self):
        self.buf[0, 0] = self.acc[...]
        self.copy(0, self.others[0]).start()

    def swap(self, slot):
        self.copy(slot, self.others[slot]).wait_recv()
        self.buf[0, slot + 1] = self.buf[0, slot] + self.buf[1, slot]
        if slot < 2:
            self.copy(slot + 1, self.others[slot + 1]).start()

    def chain(self):
        @pl.when(self.has_outer)
        def _():
            self.copy(3, self.outer).wait_recv()
            self.buf[0, 3] = self.buf[0, 3] + self.buf[1, 3]

        @pl.when(jnp.logical_not(self.is_mid))
        def _():
            self.copy(3, self.inner).start()

        @pl.when(self.is_mid)
        def _():
            self.buf[0, 4] = self.buf[0, 3]
            self.copy(4, self.inner).start()

    def settle(self):
        @pl.when(self.is_mid)
        def _():
            self.copy(4, self.inner).wait_recv()
            self.buf[0, 5] = self.buf[0, 4] + self.buf[1, 4]

        @pl.when(jnp.logical_not(self.is_mid))
        def _():
            self.copy(5, self.inner).wait_recv()
            self.buf[0, 5] = self.buf[1, 5]

        @pl.when(self.has_outer)
        def _():
            self.copy(5, self.outer).start()

    def finish(self, out):
        out[...] = self.buf[0, 5]
        for k in range(3):
            self.copy(k, self.others[k]).wait_send()

        @pl.when(jnp.logical_not(self.is_mid))
        def _():
            self.copy(3, self.inner).wait_send()

        @pl.when(self.is_mid)
        def _():
            self.copy(4, self.inner).wait_send()

        @pl.when(self.has_outer)
        def _():
            self.copy(5, self.outer).wait_send()


PLAN = {
    (0, "ffn2"): ("0u1",),
    (0, "out"): ("0u2", "0us",),
    (0, "send2"): ("0o1",),
    (0, "send1"): ("0d1",),
    (0, "rem0"): ("0u3",),
    (0, "q"): ("0d2", "0ds",),
    (0, "gk"): ("0q1", "0u4",),
    (0, "da"): ("0k1",),
    (0, "lna"): ("0v1", "0o2", "0k2", "0ks", "0d3", "0os",),
    (1, "ffn2"): ("0d4", "0o3",),
    (1, "lnb"): ("0k3", "0u5",),
    (1, "out"): ("0v2", "0vs", "0q2", "0qs", "0k4",),
    (1, "delta"): ("1d1",),
    (1, "rem2"): ("0v3", "0d5", "0k5",),
    (1, "send2"): ("0q3", "1u1",),
    (1, "rem1"): ("1d2", "0u6", "0v4", "1u2", "1us",),
    (1, "send1"): ("0q4", "0d6",),
    (1, "own0"): ("0u7",),
    (1, "own1"): ("1u3", "0q5",),
    (1, "tr"): ("0d7",),
    (1, "q"): ("1ds",),
    (1, "gq"): ("0k6",),
    (1, "gk"): ("0q6", "1q1", "1k1", "1u4", "0v5",),
    (1, "da"): ("0o4",),
    (9, "tot0"): ("1d3", "1v1", "0v6", "0v7", "0q7", "1k2", "1ks", "1o1",),
    (9, "tot1"): ("1d4", "1u5", "1o2", "0k7",),
    (9, "tot2"): ("0o5", "1u6", "1v2", "1vs", "1q2", "1qs",),
    (9, "tot3"): ("1k3", "0o6",),
    (9, "tot4"): ("1v3", "1os", "0o7", "1u7", "1d5", "1k4", "1o3", "1q3", "1v4", "1d6", "1k5", "1o4", "1q4", "1v5", "1d7", "1k6", "1o5", "1q5", "1v6", "1k7", "1o6", "1q6", "1v7", "1o7", "1q7",),
}
TILE = 512


def backward_kernel(
    layers,
    lens, cot, tok, par, cosr, sinr,
    fq, fo, fu, fd, h_in, q_in, nkv_in, kv_in, lse_in, ctx_in, mid_in, act_in, dg_in, near_in, all_in, post_in,
    grad_tok, oq, oo, ou, od, small,
    *rest,
):
    width = cot.shape[1]
    grads, big, small_s1 = dict(zip("qkvoud", rest[:6])), rest[6], rest[7]
    bufs = {kind: rest[8 + 5 * k:13 + 5 * k] for k, kind in enumerate("qkvoud")}
    rest = rest[38:]
    (wd_s, wu_s, act_s, dg_s, wo, wq, dh, mid, da, at_, db, q, kv, nkv, ctx, dctx, lset, delta, dqkv, dkv, xda, far, acc,
     gacc, sbuf, send, recv, credit, lend, lsem, ksend, krecv, kcredit, stsem, ldsem, ssend, srecv) = rest
    n = lax.axis_index("narrow")
    w = lax.axis_index("wide")
    here = (n, w)
    rows, width = cot.shape
    share = rows // 2
    group = share
    pairs = width // 128
    ff = act_in.shape[2]
    tiles = ff // TILE
    peers = ((n ^ 1, w), (n ^ 2, w), (n ^ 3, w))
    gives = (n % 2 == 0, n < 2, n < 2)
    takes = (n % 2 == 1, n >= 2, n >= 2)
    order = list(reversed(range(layers)))

    def reducers(turn):
        layer = order[turn]
        made = {}
        for kind, name in enumerate("qkvoud"):
            if name in "qkv":
                out = oq.at[layer, :, kind * width:(kind + 1) * width]
            else:
                out = {"o": oo, "u": ou, "d": od}[name].at[layer]
            s1 = {"u": big, "d": small_s1}.get(name)
            if s1 is None:
                s1 = big.at[:, kind * width:(kind + 1) * width]
            k = turn * 6 + kind
            made[name] = Reduce(here, turn, layers, name, grads[name], (s1,) + tuple(bufs[name]), out, send, recv,
                                SLOTS * k, credit, 7 * kind, lend, lsem.at[k])
        return made

    every = [reducers(turn) for turn in range(layers)]

    barrier = pltpu.get_barrier_semaphore()
    zdev = every[0]["q"]
    hello = peers + ((n, w ^ 1), zdev.inner)
    for device in hello:
        pl.semaphore_signal(barrier, inc=1, device_id=device, device_id_type=MESH)

    @pl.when(zdev.has_outer)
    def _():
        pl.semaphore_signal(barrier, inc=1, device_id=zdev.outer, device_id_type=MESH)

    def stream(layer, j, slot):
        cols = tile_at(j, TILE)
        return [
            pltpu.make_async_copy(fd.at[layer, cols], wd_s.at[slot], stsem.at[slot, 0]),
            pltpu.make_async_copy(fu.at[layer, :, cols], wu_s.at[slot], stsem.at[slot, 1]),
            pltpu.make_async_copy(act_in.at[layer, :, cols], act_s.at[slot], stsem.at[slot, 2]),
            pltpu.make_async_copy(dg_in.at[layer, :, cols], dg_s.at[slot], stsem.at[slot, 3]),
        ]

    def loads(layer):
        pieces = ((mid_in, mid), (ctx_in, ctx), (q_in, q), (nkv_in, nkv), (kv_in, kv), (lse_in, lset), (fo, wo), (fq, wq),
                  (post_in, dctx))
        return [pltpu.make_async_copy(s.at[layer], d, ldsem.at[k]) for k, (s, d) in enumerate(pieces)]

    def load_h(layer):
        if layer == 0:
            return pltpu.make_async_copy(tok, db, ldsem.at[10])
        return pltpu.make_async_copy(h_in.at[layer - 1], mid, ldsem.at[10])

    def load_first(layer):
        own = all_in.at[layer, tile_at(n, share)]
        return [pltpu.make_async_copy(near_in.at[layer], ctx.at[:share], ldsem.at[11]),
                pltpu.make_async_copy(own, ctx.at[share:], ldsem.at[12])]

    def load_far(layer, i):
        return pltpu.make_async_copy(all_in.at[layer, tile_at(peers[i][0], share)], far.at[i], ldsem.at[13 + i])

    for c in stream(order[0], 0, 0):
        c.start()
    for c in loads(order[0]):
        c.start()

    local = lax.broadcasted_iota(jnp.int32, (share, 1), 0) + n * share
    valid = (local < lens[0]).astype(F32)
    first_load = pltpu.make_async_copy(cot, db, ldsem.at[9])
    first_load.start()
    first_load.wait()
    for k in range(2):
        dh[k * share:(k + 1) * share] = db[k * share:(k + 1) * share, :].astype(F32) * valid
    gacc[...] = jnp.zeros_like(gacc)
    go, gu, gd = grads["o"], grads["u"], grads["d"]
    masks = head_masks()
    mine = tile_at(n, share)

    def to_bf16(dst):
        def body(i):
            at = tile_at(i, 256)
            dst[at, :] = dh[at, :].astype(BF16)

        loop(rows // 256, body)

    def norm_of(src, at):
        x = src[at, :].astype(F32)
        c = x - jnp.mean(x, axis=-1, keepdims=True)
        inv = lax.rsqrt(jnp.mean(c * c, axis=-1, keepdims=True) + EPS)
        return c * inv, inv

    def transposed(src):
        for i in range(rows // 128):
            at_[:, 128 * i:128 * i + 128] = src[128 * i:128 * i + 128, :].T

    def norm_back(src, gain, row_gain, row_bias):
        step = 256

        def body(i, carry):
            at = tile_at(i, step)
            normed, inv = norm_of(src, at)
            g = da[at, :]
            e = g * gain
            dv = inv * (e - jnp.mean(e, axis=-1, keepdims=True)
                        - normed * jnp.mean(e * normed, axis=-1, keepdims=True))
            dh[at, :] = dh[at, :] + dv
            fold = lambda v: v.reshape(step // 8, 8, width).sum(axis=0)
            return carry[0] + fold(g * normed), carry[1] + fold(g)

        zero = jnp.zeros((8, width), F32)
        one, two = lax.fori_loop(0, rows // step, body, (zero, zero))
        gacc[row_gain:row_gain + 1, :] = jnp.sum(one, axis=0, keepdims=True)
        gacc[row_bias:row_bias + 1, :] = jnp.sum(two, axis=0, keepdims=True)

    def block(pair, k2, v2, at, bias):
        at_pair = tile_at(pair, 128)
        q2 = q[at, at_pair].astype(F32)
        d2 = dctx[at, at_pair].astype(F32)
        k2f = k2.astype(F32)
        dk = dv = dq = None
        for h in range(2):
            row = pl.ds(2 * pair + h, 1)
            qm = (q2 * masks[h]).astype(BF16)
            dm = (d2 * masks[h]).astype(BF16)
            km = (k2f * masks[h]).astype(BF16)
            s = dot_nt(k2, qm)
            if bias is not None:
                s = s + bias()
            p = jnp.exp(s - lset[row, at])
            dp = dot_nt(v2, dm)
            ds = (p * (dp - delta[row, at])).astype(BF16)
            ak, av, aq = dot(ds, qm), dot(p.astype(BF16), dm), dot_tn(ds, km)
            dk, dv, dq = (ak, av, aq) if dk is None else (dk + ak, dv + av, dq + aq)
        return dk, dv, dq

    everyone = slice(0, rows)

    def kv_copy(i):
        region = xda.at[i]
        return pltpu.make_async_remote_copy(
            src_ref=region, dst_ref=region, send_sem=ksend.at[i], recv_sem=krecv.at[i],
            device_id=peers[i], device_id_type=MESH)

    def attend_remote(i):
        @pl.when(takes[i])
        def _():
            rows_of = tile_at(peers[i][0], group)

            def pair_step(pair):
                at_k, at_v = tile_at(pair, 128), tile_at(pair + pairs, 128)
                dk, dv, dq = block(pair, kv[rows_of, at_k], kv[rows_of, at_v], everyone, None)
                dkv[i, :, at_k] = rotary(dk, cosr[rows_of, :], -sinr[rows_of, :]).astype(BF16)
                dkv[i, :, at_v] = dv.astype(BF16)
                da[:, at_k] = da[:, at_k] + dq

            def away_tile(j):
                at = tile_at(j, 256)
                xda[i, :, at] = dot_nt(dkv[i], wq[at, width:3 * width]).astype(BF16)

            loop(pairs, pair_step)
            loop(width // 256, away_tile)

    def own_bias():
        key = blocks_of((group, share), 0)
        query = blocks_of((group, share), 1)
        return jnp.concatenate([block_bias(query, key, True), block_bias(query, key, False)], axis=1)

    def near_bias():
        same = blocks_of((share, share), 0) == blocks_of((share, share), 1)
        return jnp.where(same, 0.0, NEG).astype(F32)

    def attend_own(low, high):
        rows_of = tile_at(n, group)

        def pair_step(pair):
            at_k, at_v = tile_at(pair, 128), tile_at(pair + pairs, 128)
            dk, dv, dq = block(pair, kv[rows_of, at_k], kv[rows_of, at_v], everyone, own_bias)
            dqkv[share:, tile_at(pair + pairs, 128)] = rotary(dk, cosr[mine, :], -sinr[mine, :]).astype(BF16)
            dqkv[share:, tile_at(pair + 2 * pairs, 128)] = dv.astype(BF16)
            da[:, at_k] = da[:, at_k] + dq
            dk, dv, dq = block(pair, nkv[:, at_k], nkv[:, at_v], slice(0, share), near_bias)
            dqkv[:share, tile_at(pair + pairs, 128)] = rotary(dk, cosr[mine, :], -sinr[mine, :]).astype(BF16)
            dqkv[:share, tile_at(pair + 2 * pairs, 128)] = dv.astype(BF16)
            da[:share, at_k] = da[:share, at_k] + dq

        loop(high - low, lambda t: pair_step(t + low))

    pl.semaphore_wait(barrier, jnp.where(zdev.has_outer, 6, 5))

    def run(turn, slot):
        for word in PLAN.get((turn, slot), ()):
            r, act = every[int(word[0])][word[1]], word[2]
            if act == "3" and r.turn:
                every[r.turn - 1][word[1]].free_zb()
            {"1": r.p1, "2": r.p2, "s": r.p2s, "3": r.p3, "4": r.p4, "5": r.p5, "6": r.p6, "7": r.p7}[act]()

    for turn, layer in enumerate(order):
        last = turn == layers - 1
        after = lambda slot: run(turn, slot)

        def reuse(*names):
            if turn:
                for name in names:
                    every[turn - 1][name].free_grad()

        gain1, gain2 = par[2 * layer:2 * layer + 1, :], par[2 * layer + 1:2 * layer + 2, :]
        load = loads(layer)
        load[8].wait()
        transposed(dctx)
        to_bf16(db)
        da[...] = jnp.zeros_like(da)
        reuse("u", "d")

        def ff_step(j):
            slot = lax.rem(j, 2)
            for c in stream(layer, j, slot):
                c.wait()

            @pl.when(j + 1 < tiles)
            def _():
                for c in stream(layer, j + 1, 1 - slot):
                    c.start()

            dact = dot_nt(db[...], wd_s[slot])
            gd[tile_at(j, TILE), :] = dot_tn(act_s[slot], db[...]).astype(BF16)
            du = (dact * dg_s[slot].astype(F32)).astype(BF16)
            dg_s[slot] = du
            gu[:, tile_at(j, TILE)] = dot(at_[...], dg_s[slot]).astype(BF16)
            da[...] = da[...] + dot_nt(dg_s[slot], wu_s[slot])

        for k in range(3):
            low, high = tiles * k // 3, tiles * (k + 1) // 3
            loop(high - low, lambda j: ff_step(j + low))
            after("ffn%d" % k)
        load[0].wait()
        norm_back(mid, gain2, 2 * layer + 1, 2 * layers + 2 * layer + 1)
        if layer:
            load_h(layer).start()
        after("lnb")
        to_bf16(db)
        after("bf")
        load[1].wait()
        load[6].wait()
        reuse("o")

        def out_tile(j):
            at = tile_at(j, 256)
            go[:, at] = dot_tn(ctx[...], db[:, at]).astype(BF16)
            dctx[:, at] = dot_nt(db[...], wo[at, :]).astype(BF16)

        loop(width // 256, out_tile)
        after("out")
        if layer == 0:
            load_h(layer).start()
        load[5].wait()

        def delta_step(pair):
            at = tile_at(pair, 128)
            both = (dctx[:, at].astype(F32) * ctx[:, at].astype(F32)).T
            for h in range(2):
                delta[pl.ds(2 * pair + h, 1), :] = jnp.sum(both[64 * h:64 * h + 64], axis=0, keepdims=True)

        loop(pairs, delta_step)
        for c in load_first(layer):
            c.start()
        for i in range(3):
            @pl.when(takes[i])
            def _():
                load_far(layer, i).start()
        da[...] = jnp.zeros_like(da)
        after("delta")
        for k in (2, 3, 4, 7):
            load[k].wait()
        for i in (2, 1, 0):
            if turn:
                @pl.when(takes[i])
                def _():
                    kv_copy(i).wait_send()
            attend_remote(i)
            after("rem%d" % i)

            @pl.when(takes[i])
            def _():
                if turn:
                    pl.semaphore_wait(kcredit.at[i], 1)
                kv_copy(i).start()
            after("send%d" % i)
        attend_own(0, pairs // 2)
        after("own0")
        attend_own(pairs // 2, pairs)
        after("own1")
        for c in load_first(layer):
            c.wait()
        transposed(ctx)
        after("tr")

        def query_tile(t):
            v = da[:, tile_at(t, 128)] * 0.125
            dqkv[:, tile_at(t, 128)] = rotary_halves(v, cosr[mine, :], -sinr[mine, :]).astype(BF16)

        loop(pairs, query_tile)
        after("q")
        reuse("q")

        def grad_tile(j):
            at = tile_at(j, 256)
            grads["q"][:, at] = dot(at_[...], dqkv[:, at]).astype(BF16)

        loop(width // 256, grad_tile)
        after("gq")
        for i in range(3):
            @pl.when(takes[i])
            def _():
                load_far(layer, i).wait()

        def grad_tile_kv(j, skip, out):
            acc[...] = dot(at_[...], dqkv[:, tile_at(j + (1 + skip) * (width // 256), 256)])
            for i in range(3):
                @pl.when(takes[i])
                def _():
                    acc[...] = acc[...] + dot_tn(far[i], dkv[i, :, tile_at(j + skip * (width // 256), 256)])
            out[:, tile_at(j, 256)] = acc[...].astype(BF16)

        for k, name in enumerate("kv"):
            reuse(name)
            loop(width // 256, lambda j: grad_tile_kv(j, k, grads[name]))
            after("g" + name)

        def first_tile(j):
            at = tile_at(j, 256)
            da[:, at] = dot_nt(dqkv[...], wq[at, :])

        loop(width // 256, first_tile)
        after("da")
        load_h(layer).wait()
        entry = mid if layer else db
        for i in range(3):
            @pl.when(gives[i])
            def _():
                kv_copy(i).wait_recv()
                da[share:, :] = da[share:, :] + xda[i].astype(F32)
                if not last:
                    pl.semaphore_signal(kcredit.at[i], inc=1, device_id=peers[i], device_id_type=MESH)
        after("kvwait")
        norm_back(entry, gain1, 2 * layer, 2 * layers + 2 * layer)
        if not last:
            for c in stream(order[turn + 1], 0, 0):
                c.start()
            for c in loads(order[turn + 1]):
                c.start()
        after("lna")

    tot = SmallSum(here, gacc, sbuf, ssend, srecv)
    tot.begin()
    to_bf16(grad_tok)
    run(9, "tot0")
    tot.swap(0)
    run(9, "tot1")
    tot.swap(1)
    run(9, "tot2")
    tot.swap(2)
    run(9, "tot3")
    tot.chain()
    run(9, "tot4")
    tot.settle()
    tot.finish(small)
    for turn in every:
        for r in turn.values():
            r.p8()
    for r in every[-1].values():
        r.free_grad()
        r.free_zb()
    for i in range(3):
        @pl.when(takes[i])
        def _():
            kv_copy(i).wait_send()


def backward(lengths, cot, tok, par, tabs, full, kept):
    cosr, sinr = tabs
    rows, width = cot.shape
    share = rows // 2
    layers = full[0].shape[0]
    ff = full[2].shape[2]
    hbm = pl.BlockSpec(memory_space=pltpu.HBM)
    vmem = pl.BlockSpec(memory_space=pltpu.VMEM)
    shape = jax.ShapeDtypeStruct
    v = pltpu.VMEM
    dma, regular = pltpu.SemaphoreType.DMA, pltpu.SemaphoreType.REGULAR
    outs = [shape((layers, f.shape[1] // 4, f.shape[2]), BF16) for f in full]
    kinds = [(width, width)] * 4 + [(width, ff), (ff, width)]
    scratch = [v(k, BF16) for k in kinds] + [v((width // 2, ff), BF16), v((ff // 2, width), BF16)]
    for total, cols in kinds:
        quarter = total // 16
        scratch += [v((4 * quarter, cols), BF16), v((2 * quarter, cols), BF16),
                    v((2 * quarter, cols), BF16), v((quarter, cols), BF16), v((2 * quarter, cols), BF16)]
    scratch += [
        v((2, TILE, width), BF16), v((2, width, TILE), BF16), v((2, rows, TILE), BF16), v((2, rows, TILE), BF16),
        v((width, width), BF16), v((width, 3 * width), BF16),
        v((rows, width), F32), v((rows, width), F32), v((rows, width), F32),
        v((width, rows), BF16), v((rows, width), BF16),
        v((rows, width), BF16), v((4 * share, 2 * width), BF16), v((share, 2 * width), BF16),
        v((rows, width), BF16), v((rows, width), BF16),
        v((16, rows), F32), v((16, rows), F32),
        v((rows, 3 * width), BF16), v((3, share, 2 * width), BF16), v((3, share, width), BF16),
        v((3, share, width), BF16), v((width, 256), F32),
        v(par.shape, F32), v((2, 6) + par.shape, F32),
        dma((SLOTS * 6 * layers,)), dma((SLOTS * 6 * layers,)), regular((7 * 6,)), regular((8,)), dma((6 * layers,)),
        dma((3,)), dma((3,)), regular((3,)), dma((2, 4)), dma((16,)), dma((6,)), dma((6,)),
    ]
    return pl.pallas_call(
        partial(backward_kernel, layers),
        out_shape=[shape((rows, width), BF16)] + outs + [shape(par.shape, F32)],
        in_specs=[pl.BlockSpec(memory_space=pltpu.SMEM)] + [hbm] * 2 + [vmem] * 3 + [hbm] * 16,
        out_specs=[vmem] + [hbm] * 4 + [vmem],
        scratch_shapes=scratch,
        compiler_params=pltpu.CompilerParams(
            collective_id=1, has_side_effects=True, vmem_limit_bytes=63 * 2**20),
        cost_estimate=pl.CostEstimate(flops=40 * 10**9, bytes_accessed=10**8, transcendentals=10**7),
        name="backward",
    )(lengths, cot, tok, par, cosr, sinr, *full, *kept)


def shared_params(norm_gains, norm_biases):
    layers, _, part = norm_gains.shape
    mine = jnp.concatenate([norm_gains.reshape(2 * layers, part), norm_biases.reshape(2 * layers, part)]).astype(F32)
    parts = lax.axis_size("narrow")
    owner = jnp.arange(parts) == lax.axis_index("narrow")
    return jnp.where(owner[None, :, None], mine[:, None, :], 0.0).reshape(4 * layers, parts * part)


def rotary_tables(seq, head_dim):
    half = head_dim // 2
    freq = np.exp(-np.log(np.float32(10000.0)) * np.arange(half, dtype=np.float32) * np.float32(2.0) / np.float32(head_dim))
    angle = np.arange(seq, dtype=np.float32)[:, None] * freq.astype(np.float32)[None, :]
    cosine, sine = np.cos(angle), np.sin(angle)
    return (jnp.asarray(np.tile(cosine, (1, 4)), F32),
            jnp.asarray(np.tile(np.concatenate([-sine, sine], axis=1), (1, 2)), F32))


def on_device(tokens, lengths, w_qkv, w_out, w_up, w_down, norm_gains, norm_biases, cotangent):
    _, _, share, width = tokens.shape
    layers, _, part = norm_gains.shape
    tok = tokens.reshape(2 * share, width)
    tabs = rotary_tables(4 * share, width // H)
    outs = forward(tok, shared_params(norm_gains, norm_biases), *tabs, w_qkv, w_out, w_up, w_down)
    result, full, par, kept = outs[0], outs[1:5], outs[5], outs[6:]
    grad_tok, gq, go, gu, gd, small = backward(
        lengths, cotangent.reshape(2 * share, width), tok, par, tabs, full, kept)
    mine = lax.dynamic_slice_in_dim(small, lax.axis_index("narrow") * part, part, 1)
    gains = mine[:2 * layers].reshape(layers, 2, part)
    biases = mine[2 * layers:].reshape(layers, 2, part)
    return (
        result.reshape(tokens.shape), grad_tok.reshape(tokens.shape),
        gq.astype(F32), go.astype(F32), gu.astype(F32), gd.astype(F32),
        gains, biases[:, 0], biases[:, 1],
    )


def solution(mesh):
    return jax.shard_map(
        on_device,
        mesh=mesh,
        in_specs=(
            P("wide", None, "narrow", None),
            P("wide"),
            P(None, "narrow", None),
            P(None, "narrow", None),
            P(None, "narrow", None),
            P(None, "narrow", None),
            P(None, None, "narrow"),
            P(None, None, "narrow"),
            P("wide", None, "narrow", None),
        ),
        out_specs=(
            P("wide", None, "narrow", None),
            P("wide", None, "narrow", None),
            P(None, "narrow", None),
            P(None, "narrow", None),
            P(None, "narrow", None),
            P(None, "narrow", None),
            P(None, None, "narrow"),
            P(None, "narrow"),
            P(None, "narrow"),
        ),
        check_vma=False,
    )
```

```python
from functools import partial

import jax
import jax.numpy as jnp
import numpy as np
from jax import lax
from jax.experimental import pallas as pl
from jax.experimental.pallas import tpu as pltpu
from jax.sharding import PartitionSpec as P

H = 12
BLOCK = 16
NEG = -1e30
EPS = 1e-05
MESH = pl.DeviceIdType.MESH
F32 = jnp.float32
BF16 = jnp.bfloat16
GELU_C = 0.7978845608028654
GELU_A = 0.044715


def dot(a, b):
    return jnp.dot(a, b, preferred_element_type=F32)


def dot_nt(a, b):
    return lax.dot_general(a, b, (((1,), (1,)), ((), ())), preferred_element_type=F32)


def dot_tn(a, b):
    return lax.dot_general(a, b, (((0,), (0,)), ((), ())), preferred_element_type=F32)


def tile_at(index, size):
    return pl.ds(pl.multiple_of(index * size, size), size)


def loop(count, body):
    lax.fori_loop(0, count, lambda i, _: (body(i), None)[1], None)


def rotary(x, cosine, sine):
    lane = lax.broadcasted_iota(jnp.int32, x.shape, 1)
    swapped = jnp.where(lane % 64 < 32, pltpu.roll(x, 96, 1), pltpu.roll(x, 32, 1))
    return x * cosine + swapped * sine


def rotary_halves(x, cosine, sine):
    half = x.shape[0] // 2
    return jnp.concatenate([rotary(x[:half], cosine, sine), rotary(x[half:], cosine, sine)], axis=0)


def block_bias(query, key, strict):
    allow = key < query if strict else key <= query
    return jnp.where(allow, 0.0, NEG).astype(F32)


def blocks_of(shape, dim):
    return lax.broadcasted_iota(jnp.int32, shape, dim) // BLOCK


def head_masks():
    lane = lax.broadcasted_iota(jnp.int32, (1, 128), 1)
    low = (lane < 64).astype(F32)
    return low, 1.0 - low


def norm_into(src, dst, gain, bias, rows):
    step = 256

    def body(i):
        at = tile_at(i, step)
        x = src[at, :].astype(F32)
        c = x - jnp.mean(x, axis=-1, keepdims=True)
        inv = lax.rsqrt(jnp.mean(c * c, axis=-1, keepdims=True) + EPS)
        dst[at, :] = (c * inv * gain + bias).astype(BF16)

    loop(rows // step, body)


class Gather:
    def __init__(self, here, shard, full, send, recv, base, lsem):
        self.n, self.w = here
        self.core = lax.rem(self.w, 2)
        self.shard, self.full, self.send, self.recv, self.base, self.lsem = (
            shard, full, send, recv, base, lsem)
        self.rows = shard.shape[0]
        self.half = self.rows // 2
        self.quarter = self.rows // 4
        self.x, self.y, self.d, self.s = (
            (self.n ^ 1, self.w), (self.n ^ 2, self.w), (self.n ^ 3, self.w), (self.n, self.w ^ 1))

    def region(self, owner, core, quarter=None):
        start = owner * self.rows + core * self.half
        if quarter is None:
            return self.full.at[pl.ds(pl.multiple_of(start, 16), self.half)]
        return self.full.at[pl.ds(pl.multiple_of(start + quarter * self.quarter, 16), self.quarter)]

    def copy(self, slot, src, dst, device):
        k = self.base + slot
        return pltpu.make_async_remote_copy(
            src_ref=src, dst_ref=dst, send_sem=self.send.at[k], recv_sem=self.recv.at[k],
            device_id=device, device_id_type=MESH)

    def own(self):
        return pltpu.make_async_copy(
            self.shard, self.full.at[pl.ds(pl.multiple_of(self.n * self.rows, 16), self.rows)], self.lsem)

    def plain(self, slot, region, device):
        return self.copy(slot, region, region, device)

    def issue(self):
        src = self.shard.at[pl.ds(pl.multiple_of(self.core * self.half, 16), self.half)]
        dst = self.region(self.n, self.core)
        self.copy(0, src, dst, self.x).start()
        self.copy(1, src, dst, self.y).start()
        self.own().start()

    def forward(self):
        nx, ny = self.x[0], self.y[0]
        self.plain(0, self.region(nx, self.core), self.x).wait_recv()
        self.plain(2, self.region(nx, self.core, 0), self.y).start()
        self.plain(4, self.region(nx, self.core), self.s).start()
        self.plain(1, self.region(ny, self.core), self.y).wait_recv()
        self.plain(3, self.region(ny, self.core, 1), self.x).start()
        self.plain(5, self.region(ny, self.core), self.s).start()

    def finish(self):
        nd = self.d[0]
        self.plain(2, self.region(nd, self.core, 0), self.y).wait_recv()
        self.plain(3, self.region(nd, self.core, 1), self.x).wait_recv()
        self.plain(6, self.region(nd, self.core), self.s).start()

    def use(self):
        other = 1 - self.core
        for slot, who in ((4, self.x), (5, self.y), (6, self.d)):
            self.plain(slot, self.region(who[0], other), self.s).wait_recv()
        self.own().wait()

    def drain(self):
        src = self.shard.at[pl.ds(pl.multiple_of(self.core * self.half, 16), self.half)]
        dst = self.region(self.n, self.core)
        self.copy(0, src, dst, self.x).wait_send()
        self.copy(1, src, dst, self.y).wait_send()
        nx, ny, nd = self.x[0], self.y[0], self.d[0]
        self.plain(2, self.region(nx, self.core, 0), self.y).wait_send()
        self.plain(3, self.region(ny, self.core, 1), self.x).wait_send()
        self.plain(4, self.region(nx, self.core), self.s).wait_send()
        self.plain(5, self.region(ny, self.core), self.s).wait_send()
        self.plain(6, self.region(nd, self.core), self.s).wait_send()


def forward_kernel(
    layers,
    tok, prm, cosr, sinr, wq, wo, wu, wd,
    result, fq, fo, fu, fd, prm_out,
    h_out, q_out, nkv_out, kv_out, lse_out, ctx_out, mid_out, act_out, dg_out, near_out, all_out, post_out,
    gq, go, gu, gd, prm_buf, par, hid, a, ag, post, q, nkv, kv, bias_c, bias_n,
    lset, ctx, mid, dg, act,
    send, recv, lsem, psend, precv, ksend, krecv, ssem,
):
    n = lax.axis_index("narrow")
    w = lax.axis_index("wide")
    rows, width = tok.shape
    share = rows // 2
    group = share
    pairs = width // 128
    ff = wu.shape[2]
    peers = ((n ^ 1, w), (n ^ 2, w), (n ^ 3, w))

    barrier = pltpu.get_barrier_semaphore()
    for device in peers + ((n, w ^ 1),):
        pl.semaphore_signal(barrier, inc=1, device_id=device, device_id_type=MESH)
    pl.semaphore_wait(barrier, 4)

    tensors = []
    for layer in range(layers):
        for kind, (shard, full) in enumerate(((wq, gq), (wo, go), (wu, gu), (wd, gd))):
            k = layer * 4 + kind
            tensors.append(Gather((n, w), shard.at[layer], full.at[layer], send, recv, 7 * k, lsem.at[k]))

    def params(i):
        return pltpu.make_async_remote_copy(
            src_ref=prm, dst_ref=prm_buf.at[i], send_sem=psend.at[i], recv_sem=precv.at[i],
            device_id=peers[i], device_id_type=MESH)

    def share_a(layer, i):
        region = ag.at[layer, tile_at(n, share)]
        return pltpu.make_async_remote_copy(
            src_ref=region, dst_ref=region, send_sem=ksend.at[3 * layer + i],
            recv_sem=krecv.at[3 * layer + i], device_id=peers[i], device_id_type=MESH)

    def recv_a(layer, i):
        region = ag.at[layer, tile_at(peers[i][0], share)]
        return pltpu.make_async_remote_copy(
            src_ref=region, dst_ref=region, send_sem=ksend.at[3 * layer + i],
            recv_sem=krecv.at[3 * layer + i], device_id=peers[i], device_id_type=MESH)

    gives = (n % 2 == 0, n < 2, n < 2)
    takes = (n % 2 == 1, n >= 2, n >= 2)

    for i in range(3):
        params(i).start()
    tensors[0].issue()

    def saves(layer):
        pieces = [
            (q, q_out.at[layer]), (nkv, nkv_out.at[layer]), (kv, kv_out.at[layer]),
            (lset, lse_out.at[layer]), (ctx, ctx_out.at[layer]), (mid, mid_out.at[layer]), (act, act_out.at[layer]),
            (dg, dg_out.at[layer]), (hid, h_out.at[layer]), (a.at[:share], near_out.at[layer]),
            (ag.at[layer], all_out.at[layer]), (post, post_out.at[layer]),
        ]
        return [pltpu.make_async_copy(s, d, ssem.at[layer * 12 + k]) for k, (s, d) in enumerate(pieces)]

    def weight_saves():
        pieces = ((gq, fq), (go, fo), (gu, fu), (gd, fd))
        out = []
        for layer in range(layers):
            for kind, (s, d) in enumerate(pieces):
                k = layer * 4 + kind
                out.append(pltpu.make_async_copy(s.at[layer], d.at[layer], ssem.at[12 * layers + k]))
        return out

    for i in range(3):
        params(i).wait_recv()
    par[...] = prm[...] + prm_buf[0] + prm_buf[1] + prm_buf[2]
    prm_out[...] = par[...]

    for k in range(2):
        at = slice(k * share, (k + 1) * share)
        bias_c[:, at] = block_bias(blocks_of((share, share), 1), blocks_of((share, share), 0), k == 0)
    same = blocks_of((share, share), 0) == blocks_of((share, share), 1)
    bias_n[...] = jnp.where(same, 0.0, NEG).astype(F32)
    masks = head_masks()
    here = tile_at(n, share)

    full_saves = weight_saves()
    for layer in range(layers):
        t_qkv, t_out, t_up, t_down = tensors[4 * layer:4 * layer + 4]
        later = tensors[4 * layer + 4:]
        gain1, gain2 = par[2 * layer:2 * layer + 1, :], par[2 * layer + 1:2 * layer + 2, :]
        at = 2 * layers + 2 * layer
        bias1, bias2 = par[at:at + 1, :], par[at + 1:at + 2, :]
        saved = saves(layer)
        before = saves(layer - 1) if layer else None
        if before:
            before[9].wait()
        if layer == 0:
            norm_into(tok, a, gain1, bias1, rows)
        else:
            norm_into(hid, a, gain1, bias1, rows)
        ag[layer, here] = a[share:]
        t_qkv.forward()
        for i in range(3):
            @pl.when(gives[i])
            def _():
                share_a(layer, i).start()
        saved[9].start()
        t_out.issue()
        t_up.issue()
        t_qkv.finish()
        t_qkv.use()
        full_saves[4 * layer].start()
        if before:
            before[0].wait()
            before[1].wait()
            before[2].wait()

        wqkv = gq.at[layer]

        def query_tile(j):
            x = dot(a[...], wqkv[:, tile_at(j, 256)])
            for part in range(2):
                v = rotary_halves(x[:, 128 * part:128 * part + 128], cosr[here, :], sinr[here, :])
                q[:, tile_at(2 * j + part, 128)] = (v.astype(BF16).astype(F32) * 0.125).astype(BF16)

        def key_tile(j):
            x = dot(a[...], wqkv[:, tile_at(j + 3, 256)])
            for part in range(2):
                v = rotary_halves(x[:, 128 * part:128 * part + 128], cosr[here, :], sinr[here, :]).astype(BF16)
                nkv[:, tile_at(2 * j + part, 128)] = v[:share]
                kv[here, tile_at(2 * j + part, 128)] = v[share:]

        def value_tile(j):
            v = dot(a[...], wqkv[:, tile_at(j + 6, 256)]).astype(BF16)
            nkv[:, tile_at(j + 3, 256)] = v[:share]
            kv[here, tile_at(j + 3, 256)] = v[share:]

        def far_tiles(g):
            at = tile_at(g, share)

            def far_key(j):
                x = dot(ag[layer, at, :], wqkv[:, tile_at(j + 3, 256)])
                for part in range(2):
                    v = rotary(x[:, 128 * part:128 * part + 128], cosr[at, :], sinr[at, :])
                    kv[at, tile_at(2 * j + part, 128)] = v.astype(BF16)

            def far_value(j):
                kv[at, tile_at(j + 3, 256)] = dot(ag[layer, at, :], wqkv[:, tile_at(j + 6, 256)]).astype(BF16)

            loop(3, far_key)
            loop(3, far_value)

        loop(3, key_tile)
        loop(3, value_tile)
        loop(3, query_tile)
        saved[0].start()
        saved[1].start()
        t_down.issue()
        for i in range(3):
            @pl.when(takes[i])
            def _():
                recv_a(layer, i).wait_recv()
        saved[10].start()
        loop(n, far_tiles)
        saved[2].start()
        if before:
            before[3].wait()
            before[4].wait()

        def fold(v, how):
            v = v.reshape(v.shape[0] // 8, 8, v.shape[1])
            return how(how(v, axis=0), axis=0, keepdims=True)

        def pair_step(pair):
            at_pair = tile_at(pair, 128)
            at_value = tile_at(pair + pairs, 128)
            q2 = q[:, at_pair].astype(F32)
            qm = [(q2 * masks[h]).astype(BF16) for h in range(2)]
            lower = [slice(64 * h, 64 * h + 64) for h in range(2)]

            def absorb(s, v2, carry):
                most, total, out = carry
                peak = jnp.maximum(most, fold(s, jnp.max))
                p = jnp.exp(s - peak)
                shrink = jnp.exp(most - peak)
                total = total * shrink + fold(p, jnp.sum)
                out = out * shrink + dot(v2, p.astype(BF16))
                return peak, total, out

            near_v = nkv[:, at_value].T
            own_v = kv[here, at_value].T
            blank = (jnp.full((1, share), NEG, F32), jnp.zeros((1, share), F32), jnp.zeros((64, share), F32))
            states = []
            for h in range(2):
                s = dot_nt(nkv[:, at_pair], qm[h][:share]) + bias_n[...]
                most = fold(s, jnp.max)
                p = jnp.exp(s - most)
                near = (most, fold(p, jnp.sum), dot(near_v[lower[h]], p.astype(BF16)))
                state = tuple(jnp.concatenate([a, b], axis=1) for a, b in zip(near, blank))
                s = dot_nt(kv[here, at_pair], qm[h]) + bias_c[...]
                states.append(absorb(s, own_v[lower[h]], state))

            def far_step(g, states):
                at = tile_at(g, group)
                far_v = kv[at, at_value].T
                scores = [dot_nt(kv[at, at_pair], qm[h]) for h in range(2)]
                return tuple(absorb(scores[h], far_v[lower[h]], states[h]) for h in range(2))

            states = lax.fori_loop(0, n, far_step, tuple(states))
            outs = []
            for h, (most, total, out) in enumerate(states):
                outs.append(out / total)
                lset[pl.ds(2 * pair + h, 1), :] = most + jnp.log(total)
            ctx[:, at_pair] = jnp.concatenate(outs, axis=0).T.astype(BF16)

        loop(pairs // 2, pair_step)
        t_out.forward()
        t_up.forward()
        loop(pairs - pairs // 2, lambda t: pair_step(t + pairs // 2))
        saved[3].start()
        saved[4].start()
        t_out.finish()
        t_up.finish()
        t_down.forward()
        if later:
            later[0].issue()
        t_out.use()
        full_saves[4 * layer + 1].start()
        if before:
            before[5].wait()
            before[6].wait()
            before[7].wait()
            before[8].wait()

        def out_tile(j):
            at = tile_at(j, 256)
            base = (tok if layer == 0 else hid)[:, at].astype(F32)
            mid[:, at] = base + dot(ctx[...], go[layer, :, at])

        loop(width // 256, out_tile)
        saved[5].start()
        if before:
            before[11].wait()
        norm_into(mid, post, gain2, bias2, rows)
        saved[11].start()
        t_up.use()
        full_saves[4 * layer + 2].start()

        def up_tile(j):
            at = tile_at(j, 256)
            x = dot(post[...], gu[layer, :, at])
            x2 = x * x
            t = jnp.tanh(GELU_C * (x + GELU_A * (x * x2)))
            cdf = 0.5 + 0.5 * t
            act[:, at] = (x * cdf).astype(BF16)
            slope = GELU_C * (1.0 + 3.0 * GELU_A * x2)
            dg[:, at] = (cdf + 0.5 * x * (1.0 - t * t) * slope).astype(BF16)

        loop(ff // 256, up_tile)
        saved[6].start()
        saved[7].start()
        t_down.finish()
        t_down.use()
        full_saves[4 * layer + 3].start()

        def down_tile(j):
            at = tile_at(j, 256)
            out = mid[:, at] + dot(act[...], gd[layer, :, at])
            hid[:, at] = out
            if layer == layers - 1:
                result[:, at] = out.astype(BF16)

        loop(width // 256, down_tile)
        saved[8].start()

    for c in saves(layers - 1):
        c.wait()
    for layer in range(layers - 1):
        saves(layer)[10].wait()
    for c in full_saves:
        c.wait()
    for t in tensors:
        t.drain()
    for i in range(3):
        params(i).wait_send()
        for layer in range(layers):
            @pl.when(gives[i])
            def _():
                share_a(layer, i).wait_send()


def forward(tokens, prm, cosr, sinr, w_qkv, w_out, w_up, w_down):
    rows, width = tokens.shape
    share = rows // 2
    layers = w_qkv.shape[0]
    seq = share * 4
    qw, ff = w_qkv.shape[2], w_up.shape[2]
    full = [
        jax.ShapeDtypeStruct((layers, width, qw), BF16),
        jax.ShapeDtypeStruct((layers, width, width), BF16),
        jax.ShapeDtypeStruct((layers, width, ff), BF16),
        jax.ShapeDtypeStruct((layers, ff, width), BF16),
    ]
    hbm = pl.BlockSpec(memory_space=pltpu.HBM)
    vmem = pl.BlockSpec(memory_space=pltpu.VMEM)
    shape = jax.ShapeDtypeStruct
    kept = [
        shape((layers, rows, width), F32),
        shape((layers, rows, width), BF16),
        shape((layers, share, 2 * width), BF16),
        shape((layers, seq, 2 * width), BF16),
        shape((layers, 16, rows), F32),
        shape((layers, rows, width), BF16),
        shape((layers, rows, width), F32),
        shape((layers, rows, ff), BF16),
        shape((layers, rows, ff), BF16),
        shape((layers, share, width), BF16),
        shape((layers, seq, width), BF16),
        shape((layers, rows, width), BF16),
    ]
    dma, count = pltpu.SemaphoreType.DMA, 7 * 4 * layers
    return pl.pallas_call(
        partial(forward_kernel, layers),
        out_shape=[shape((rows, width), BF16)] + full + [shape(prm.shape, F32)] + kept,
        in_specs=[vmem] * 4 + [hbm] * 4,
        out_specs=[vmem] + [hbm] * 4 + [vmem] + [hbm] * 12,
        scratch_shapes=[pltpu.VMEM(f.shape, BF16) for f in full] + [
            pltpu.VMEM((3,) + prm.shape, F32),
            pltpu.VMEM(prm.shape, F32),
            pltpu.VMEM((rows, width), F32),
            pltpu.VMEM((rows, width), BF16),
            pltpu.VMEM((layers, seq, width), BF16),
            pltpu.VMEM((rows, width), BF16),
            pltpu.VMEM((rows, width), BF16),
            pltpu.VMEM((share, 2 * width), BF16),
            pltpu.VMEM((seq, 2 * width), BF16),
            pltpu.VMEM((share, rows), F32),
            pltpu.VMEM((share, share), F32),
            pltpu.VMEM((16, rows), F32),
            pltpu.VMEM((rows, width), BF16),
            pltpu.VMEM((rows, width), F32),
            pltpu.VMEM((rows, ff), BF16),
            pltpu.VMEM((rows, ff), BF16),
            dma((count,)), dma((count,)), dma((4 * layers,)),
            dma((3,)), dma((3,)), dma((3 * layers,)), dma((3 * layers,)),
            dma((16 * layers,)),
        ],
        compiler_params=pltpu.CompilerParams(
            collective_id=0, has_side_effects=True, vmem_limit_bytes=62 * 2**20),
        cost_estimate=pl.CostEstimate(flops=20 * 10**9, bytes_accessed=10**8, transcendentals=10**7),
        name="forward",
    )(tokens, prm, cosr, sinr, w_qkv, w_out, w_up, w_down)


def add_rows(dst, at, left, left_at, right, right_at, rows):
    size = 48 if rows % 48 == 0 else 16

    def body(i):
        step = lambda base: pl.ds(pl.multiple_of(base + size * i, 16), size)
        dst[step(at), :] = left[step(left_at), :] + right[step(right_at), :]

    loop(rows // size, body)


class Reduce:
    def __init__(self, here, turn, turns, kind, grad, bufs, out, send, recv, base, credit, cbase, lend, lsem):
        self.n, self.w = here
        self.turn, self.turns, self.kind = turn, turns, kind
        self.lend = lend
        self.grad, self.out = grad, out
        self.s1, self.r2, self.r3, self.r4, self.r5, self.zb = bufs
        self.send, self.recv, self.base = send, recv, base
        self.credit, self.cbase, self.lsem = credit, cbase, lsem
        self.core = lax.rem(self.w, 2)
        self.rows = grad.shape[0] // 4
        self.half, self.quarter = self.rows // 2, self.rows // 4
        n, w = here
        self.x, self.y, self.d, self.s = (n ^ 1, w), (n ^ 2, w), (n ^ 3, w), (n, w ^ 1)
        chips = lax.axis_size("wide") // 2
        z = w // 2
        left = z < chips // 2
        step = jnp.where(left, 2, -2)
        self.inner, self.outer = (n, w + step), (n, w - step)
        self.has_outer = jnp.logical_and(z > 0, z < chips - 1)
        self.is_mid = jnp.logical_or(z == chips // 2 - 1, z == chips // 2)
        self.mine = jnp.where(left, 0, 1)

    def at(self, owner, core, quarter=0):
        return pl.multiple_of(owner * self.rows + core * self.half + quarter * self.quarter, 16)

    def part(self, ref, start, count):
        return ref.at[pl.ds(pl.multiple_of(start, 16), count)]

    def copy(self, slot, src, dst, device):
        k = self.base + slot
        return pltpu.make_async_remote_copy(
            src_ref=src, dst_ref=dst, send_sem=self.send.at[k], recv_sem=self.recv.at[k],
            device_id=device, device_id_type=MESH)

    def take(self, slot):
        if self.turn > 0:
            pl.semaphore_wait(self.credit.at[self.cbase + slot], 1)

    def give(self, slot, device):
        if self.turn < self.turns - 1:
            pl.semaphore_signal(
                self.credit.at[self.cbase + slot], inc=1, device_id=device, device_id_type=MESH)

    def to_sibling(self):
        out = []
        for m in range(4):
            src = self.part(self.grad, self.at(m, 1 - self.core), self.half)
            out.append(self.copy(m, src, self.part(self.s1, m * self.half, self.half), self.s))
        return out

    def first_hop(self):
        q, g, c = self.quarter, self.grad, self.core
        nx, ny, nd = self.x[0], self.y[0], self.d[0]
        plan = ((4, nx, 0, 0, self.x), (5, nd, 0, 1, self.x), (6, ny, 1, 2, self.y), (7, nd, 1, 3, self.y))
        return [
            self.copy(slot, self.part(g, self.at(owner, c, quarter), q), self.part(self.r2, place * q, q), device)
            for slot, owner, quarter, place, device in plan]

    def second_hop(self):
        q, g, c = self.quarter, self.grad, self.core
        return [
            self.copy(8, self.part(g, self.at(self.y[0], c, 0), q), self.part(self.r3, 0, q), self.y),
            self.copy(9, self.part(g, self.at(self.x[0], c, 1), q), self.part(self.r3, q, q), self.x)]

    def inward(self):
        return self.copy(10, self.zb, self.r4, self.inner)

    def across(self):
        src = self.part(self.zb, (1 - self.mine) * self.quarter, self.quarter)
        return self.copy(11, src, self.r5, self.inner)

    def done_at(self, core, quarter):
        start = core * self.half + quarter * self.quarter
        return self.part(self.out, start, self.quarter)

    def final(self, quarter, device, slot, from_zb):
        dst = self.done_at(self.core, quarter)
        src = self.part(self.zb, quarter * self.quarter, self.quarter) if from_zb else dst
        return self.copy(slot, src, dst, device)

    def keep(self):
        src = self.part(self.zb, self.mine * self.quarter, self.quarter)
        return pltpu.make_async_copy(src, self.done_at(self.core, self.mine), self.lsem)

    def p1(self):
        if self.kind == "d":
            self.take(0)
        elif self.kind == "u":
            for k in range(4 if self.turn else 0):
                pl.semaphore_wait(self.lend.at[k + 4], 1)
        else:
            pl.semaphore_wait(self.lend.at["qkvo".index(self.kind)], 1)
        for c in self.to_sibling():
            c.start()

    def p2(self):
        g = self.grad
        for m, c in enumerate(self.to_sibling()):
            c.wait_recv()
            add_rows(g, self.at(m, self.core), g, self.at(m, self.core), self.s1, m * self.half, self.half)
        if self.kind == "d":
            self.give(0, self.s)
        elif self.kind == "u":
            for k in range(4):
                pl.semaphore_signal(self.lend.at[k], inc=1, device_id=self.s, device_id_type=MESH)
        elif self.turn < self.turns - 1:
            k = "qkvo".index(self.kind) + 4
            pl.semaphore_signal(self.lend.at[k], inc=1, device_id=self.s, device_id_type=MESH)

    def p2s(self):
        self.take(1)
        self.take(2)
        for c in self.first_hop():
            c.start()

    def p3(self):
        g, q = self.grad, self.quarter
        hops = self.first_hop()
        hops[1].wait_recv()
        at = self.at(self.y[0], self.core, 0)
        add_rows(g, at, g, at, self.r2, q, q)
        self.take(3)
        self.second_hop()[0].start()
        hops[3].wait_recv()
        at = self.at(self.x[0], self.core, 1)
        add_rows(g, at, g, at, self.r2, 3 * q, q)
        self.take(4)
        self.second_hop()[1].start()
        for k in range(2):
            hops[2 * k].wait_recv()
            at = self.at(self.n, self.core, k)
            add_rows(self.zb, k * q, g, at, self.r2, 2 * k * q, q)
        self.give(1, self.x)
        self.give(2, self.y)

    def p4(self):
        q = self.quarter
        for k, c in enumerate(self.second_hop()):
            c.wait_recv()
            add_rows(self.zb, k * q, self.zb, k * q, self.r3, k * q, q)
        self.give(3, self.y)
        self.give(4, self.x)

        @pl.when(jnp.logical_not(jnp.logical_or(self.has_outer, self.is_mid)))
        def _():
            self.take(5)
            self.inward().start()

    def p5(self):
        @pl.when(self.has_outer)
        def _():
            self.inward().wait_recv()
            add_rows(self.zb, 0, self.zb, 0, self.r4, 0, self.half)
            self.give(5, self.outer)

        @pl.when(self.is_mid)
        def _():
            self.take(6)
            self.across().start()

        @pl.when(jnp.logical_and(self.has_outer, jnp.logical_not(self.is_mid)))
        def _():
            self.take(5)
            self.inward().start()

    def p6(self):
        @pl.when(self.is_mid)
        def _():
            self.across().wait_recv()
            at = self.mine * self.quarter
            add_rows(self.zb, at, self.zb, at, self.r5, 0, self.quarter)
            self.give(6, self.inner)
            self.keep().start()
            self.final(self.mine, self.inner, 12, True).start()
            self.final(self.mine, self.s, 13, True).start()

        @pl.when(jnp.logical_and(self.is_mid, self.has_outer))
        def _():
            self.final(self.mine, self.outer, 15, True).start()

    def p7(self):
        other = 1 - self.mine

        @pl.when(self.is_mid)
        def _():
            self.final(other, self.inner, 12, False).wait_recv()
            self.final(other, self.s, 14, False).start()

        @pl.when(jnp.logical_and(self.is_mid, self.has_outer))
        def _():
            self.final(other, self.outer, 16, False).start()

        @pl.when(jnp.logical_not(self.is_mid))
        def _():
            self.final(self.mine, self.inner, 15, False).wait_recv()
            self.final(self.mine, self.s, 13, False).start()
            self.final(other, self.inner, 16, False).wait_recv()
            self.final(other, self.s, 14, False).start()

        @pl.when(jnp.logical_and(jnp.logical_not(self.is_mid), self.has_outer))
        def _():
            self.final(self.mine, self.outer, 15, False).start()
            self.final(other, self.outer, 16, False).start()

    def p8(self):
        for k, quarter in ((13, self.mine), (14, 1 - self.mine)):
            region = self.done_at(1 - self.core, quarter)
            self.copy(k, region, region, self.s).wait_recv()

    def free_grad(self):
        for c in self.to_sibling() + self.first_hop() + self.second_hop():
            c.wait_send()

    def free_zb(self):
        @pl.when(jnp.logical_not(self.is_mid))
        def _():
            self.inward().wait_send()

        @pl.when(self.is_mid)
        def _():
            self.across().wait_send()
            self.final(self.mine, self.inner, 12, True).wait_send()
            self.keep().wait()

        other = 1 - self.mine
        self.final(self.mine, self.s, 13, False).wait_send()
        self.final(other, self.s, 14, False).wait_send()

        @pl.when(self.has_outer)
        def _():
            self.final(self.mine, self.outer, 15, False).wait_send()
            self.final(other, self.outer, 16, False).wait_send()


SLOTS = 17


class SmallSum:
    def __init__(self, here, acc, buf, send, recv):
        n, w = here
        self.acc, self.buf, self.send, self.recv = acc, buf, send, recv
        chips = lax.axis_size("wide") // 2
        z = w // 2
        left = z < chips // 2
        step = jnp.where(left, 2, -2)
        self.inner, self.outer = (n, w + step), (n, w - step)
        self.has_outer = jnp.logical_and(z > 0, z < chips - 1)
        self.is_mid = jnp.logical_or(z == chips // 2 - 1, z == chips // 2)
        self.others = ((n, w ^ 1), (n ^ 1, w), (n ^ 2, w))

    def copy(self, slot, device):
        return pltpu.make_async_remote_copy(
            src_ref=self.buf.at[0, slot], dst_ref=self.buf.at[1, slot], send_sem=self.send.at[slot],
            recv_sem=self.recv.at[slot], device_id=device, device_id_type=MESH)

    def begin(self):
        self.buf[0, 0] = self.acc[...]
        self.copy(0, self.others[0]).start()

    def swap(self, slot):
        self.copy(slot, self.others[slot]).wait_recv()
        self.buf[0, slot + 1] = self.buf[0, slot] + self.buf[1, slot]
        if slot < 2:
            self.copy(slot + 1, self.others[slot + 1]).start()

    def chain(self):
        @pl.when(self.has_outer)
        def _():
            self.copy(3, self.outer).wait_recv()
            self.buf[0, 3] = self.buf[0, 3] + self.buf[1, 3]

        @pl.when(jnp.logical_not(self.is_mid))
        def _():
            self.copy(3, self.inner).start()

        @pl.when(self.is_mid)
        def _():
            self.buf[0, 4] = self.buf[0, 3]
            self.copy(4, self.inner).start()

    def settle(self):
        @pl.when(self.is_mid)
        def _():
            self.copy(4, self.inner).wait_recv()
            self.buf[0, 5] = self.buf[0, 4] + self.buf[1, 4]

        @pl.when(jnp.logical_not(self.is_mid))
        def _():
            self.copy(5, self.inner).wait_recv()
            self.buf[0, 5] = self.buf[1, 5]

        @pl.when(self.has_outer)
        def _():
            self.copy(5, self.outer).start()

    def finish(self):
        for k in range(3):
            self.copy(k, self.others[k]).wait_send()

        @pl.when(jnp.logical_not(self.is_mid))
        def _():
            self.copy(3, self.inner).wait_send()

        @pl.when(self.is_mid)
        def _():
            self.copy(4, self.inner).wait_send()

        @pl.when(self.has_outer)
        def _():
            self.copy(5, self.outer).wait_send()


PLAN = {
    (0, "ffn2"): ("0u1",),
    (0, "out"): ("0u2", "0us",),
    (0, "send2"): ("0o1",),
    (0, "send1"): ("0d1",),
    (0, "rem0"): ("0u3",),
    (0, "q"): ("0d2", "0ds",),
    (0, "gk"): ("0q1", "0u4",),
    (0, "da"): ("0k1",),
    (0, "lna"): ("0v1", "0o2", "0k2", "0ks", "0d3", "0os",),
    (1, "ffn2"): ("0d4", "0o3",),
    (1, "lnb"): ("0k3", "0u5",),
    (1, "out"): ("0v2", "0vs", "0q2", "0qs", "0k4",),
    (1, "delta"): ("1d1",),
    (1, "rem2"): ("0v3", "0d5", "0k5",),
    (1, "send2"): ("0q3", "1u1",),
    (1, "rem1"): ("1d2", "0u6", "0v4", "1u2", "1us",),
    (1, "send1"): ("0q4", "0d6",),
    (1, "own0"): ("0u7",),
    (1, "own1"): ("1u3", "0q5",),
    (1, "tr"): ("0d7",),
    (1, "q"): ("1ds",),
    (1, "gq"): ("0k6",),
    (1, "gk"): ("0q6", "1q1", "1k1", "1u4", "0v5",),
    (1, "da"): ("0o4",),
    (9, "tot0"): ("1d3", "1v1", "0v6", "0v7", "0q7", "1k2", "1ks", "1o1",),
    (9, "tot1"): ("1d4", "1u5", "1o2", "0k7",),
    (9, "tot2"): ("0o5", "1u6", "1v2", "1vs", "1q2", "1qs",),
    (9, "tot3"): ("1k3", "0o6",),
    (9, "tot4"): ("1v3", "1os", "0o7", "1u7", "1d5", "1k4", "1o3", "1q3", "1v4", "1d6", "1k5", "1o4", "1q4", "1v5", "1d7", "1k6", "1o5", "1q5", "1v6", "1k7", "1o6", "1q6", "1v7", "1o7", "1q7",),
}
TILE = 512


def backward_kernel(
    layers,
    lens, cot, tok, par, cosr, sinr,
    fq, fo, fu, fd, h_in, q_in, nkv_in, kv_in, lse_in, ctx_in, mid_in, act_in, dg_in, near_in, all_in, post_in,
    grad_tok, oq, oo, ou, od, out_gain, out_first, out_second,
    *rest,
):
    width = cot.shape[1]
    grads, big, small_s1 = dict(zip("qkvoud", rest[:6])), rest[6], rest[7]
    bufs = {kind: rest[8 + 5 * k:13 + 5 * k] for k, kind in enumerate("qkvoud")}
    rest = rest[38:]
    (wd_s, wu_s, act_s, dg_s, wo, wq, dh, mid, da, at_, db, q, kv, nkv, ctx, dctx, lset, delta, dqkv, dkv, xda, far, acc,
     gacc, sbuf, send, recv, credit, lend, lsem, ksend, krecv, kcredit, stsem, ldsem, ssend, srecv) = rest
    n = lax.axis_index("narrow")
    w = lax.axis_index("wide")
    here = (n, w)
    rows, width = cot.shape
    share = rows // 2
    group = share
    pairs = width // 128
    ff = act_in.shape[2]
    tiles = ff // TILE
    peers = ((n ^ 1, w), (n ^ 2, w), (n ^ 3, w))
    gives = (n % 2 == 0, n < 2, n < 2)
    takes = (n % 2 == 1, n >= 2, n >= 2)
    order = list(reversed(range(layers)))

    def reducers(turn):
        layer = order[turn]
        made = {}
        for kind, name in enumerate("qkvoud"):
            if name in "qkv":
                out = oq.at[layer, :, kind * width:(kind + 1) * width]
            else:
                out = {"o": oo, "u": ou, "d": od}[name].at[layer]
            s1 = {"u": big, "d": small_s1}.get(name)
            if s1 is None:
                s1 = big.at[:, kind * width:(kind + 1) * width]
            k = turn * 6 + kind
            made[name] = Reduce(here, turn, layers, name, grads[name], (s1,) + tuple(bufs[name]), out, send, recv,
                                SLOTS * k, credit, 7 * kind, lend, lsem.at[k])
        return made

    every = [reducers(turn) for turn in range(layers)]

    barrier = pltpu.get_barrier_semaphore()
    zdev = every[0]["q"]
    hello = peers + ((n, w ^ 1), zdev.inner)
    for device in hello:
        pl.semaphore_signal(barrier, inc=1, device_id=device, device_id_type=MESH)

    @pl.when(zdev.has_outer)
    def _():
        pl.semaphore_signal(barrier, inc=1, device_id=zdev.outer, device_id_type=MESH)

    def stream(layer, j, slot):
        cols = tile_at(j, TILE)
        return [
            pltpu.make_async_copy(fd.at[layer, cols], wd_s.at[slot], stsem.at[slot, 0]),
            pltpu.make_async_copy(fu.at[layer, :, cols], wu_s.at[slot], stsem.at[slot, 1]),
            pltpu.make_async_copy(act_in.at[layer, :, cols], act_s.at[slot], stsem.at[slot, 2]),
            pltpu.make_async_copy(dg_in.at[layer, :, cols], dg_s.at[slot], stsem.at[slot, 3]),
        ]

    def loads(layer):
        pieces = ((mid_in, mid), (ctx_in, ctx), (q_in, q), (nkv_in, nkv), (kv_in, kv), (lse_in, lset), (fo, wo), (fq, wq),
                  (post_in, dctx))
        return [pltpu.make_async_copy(s.at[layer], d, ldsem.at[k]) for k, (s, d) in enumerate(pieces)]

    def load_h(layer):
        if layer == 0:
            return pltpu.make_async_copy(tok, db, ldsem.at[10])
        return pltpu.make_async_copy(h_in.at[layer - 1], mid, ldsem.at[10])

    def load_first(layer):
        own = all_in.at[layer, tile_at(n, share)]
        return [pltpu.make_async_copy(near_in.at[layer], ctx.at[:share], ldsem.at[11]),
                pltpu.make_async_copy(own, ctx.at[share:], ldsem.at[12])]

    def load_far(layer, i):
        return pltpu.make_async_copy(all_in.at[layer, tile_at(peers[i][0], share)], far.at[i], ldsem.at[13 + i])

    for c in stream(order[0], 0, 0):
        c.start()
    for c in loads(order[0]):
        c.start()

    local = lax.broadcasted_iota(jnp.int32, (share, 1), 0) + n * share
    valid = (local < lens[0]).astype(F32)
    first_load = pltpu.make_async_copy(cot, db, ldsem.at[9])
    first_load.start()
    first_load.wait()
    for k in range(2):
        dh[k * share:(k + 1) * share] = db[k * share:(k + 1) * share, :].astype(F32) * valid
    gacc[...] = jnp.zeros_like(gacc)
    go, gu, gd = grads["o"], grads["u"], grads["d"]
    masks = head_masks()
    mine = tile_at(n, share)

    def to_bf16(dst):
        def body(i):
            at = tile_at(i, 256)
            dst[at, :] = dh[at, :].astype(BF16)

        loop(rows // 256, body)

    def norm_of(src, at):
        x = src[at, :].astype(F32)
        c = x - jnp.mean(x, axis=-1, keepdims=True)
        inv = lax.rsqrt(jnp.mean(c * c, axis=-1, keepdims=True) + EPS)
        return c * inv, inv

    def transposed(src):
        for i in range(rows // 128):
            at_[:, 128 * i:128 * i + 128] = src[128 * i:128 * i + 128, :].T

    def norm_back(src, gain, row_gain, row_bias):
        step = 256

        def body(i, carry):
            at = tile_at(i, step)
            normed, inv = norm_of(src, at)
            g = da[at, :]
            e = g * gain
            dv = inv * (e - jnp.mean(e, axis=-1, keepdims=True)
                        - normed * jnp.mean(e * normed, axis=-1, keepdims=True))
            dh[at, :] = dh[at, :] + dv
            fold = lambda v: v.reshape(step // 8, 8, width).sum(axis=0)
            return carry[0] + fold(g * normed), carry[1] + fold(g)

        zero = jnp.zeros((8, width), F32)
        one, two = lax.fori_loop(0, rows // step, body, (zero, zero))
        gacc[row_gain:row_gain + 1, :] = jnp.sum(one, axis=0, keepdims=True)
        gacc[row_bias:row_bias + 1, :] = jnp.sum(two, axis=0, keepdims=True)

    def block(pair, k2, v2, at, bias):
        at_pair = tile_at(pair, 128)
        q2 = q[at, at_pair].astype(F32)
        d2 = dctx[at, at_pair].astype(F32)
        k2f = k2.astype(F32)
        dk = dv = dq = None
        for h in range(2):
            row = pl.ds(2 * pair + h, 1)
            qm = (q2 * masks[h]).astype(BF16)
            dm = (d2 * masks[h]).astype(BF16)
            km = (k2f * masks[h]).astype(BF16)
            s = dot_nt(k2, qm)
            if bias is not None:
                s = s + bias()
            p = jnp.exp(s - lset[row, at])
            dp = dot_nt(v2, dm)
            ds = (p * (dp - delta[row, at])).astype(BF16)
            ak, av, aq = dot(ds, qm), dot(p.astype(BF16), dm), dot_tn(ds, km)
            dk, dv, dq = (ak, av, aq) if dk is None else (dk + ak, dv + av, dq + aq)
        return dk, dv, dq

    everyone = slice(0, rows)

    def kv_copy(i):
        region = xda.at[i]
        return pltpu.make_async_remote_copy(
            src_ref=region, dst_ref=region, send_sem=ksend.at[i], recv_sem=krecv.at[i],
            device_id=peers[i], device_id_type=MESH)

    def attend_remote(i):
        @pl.when(takes[i])
        def _():
            rows_of = tile_at(peers[i][0], group)

            def pair_step(pair):
                at_k, at_v = tile_at(pair, 128), tile_at(pair + pairs, 128)
                dk, dv, dq = block(pair, kv[rows_of, at_k], kv[rows_of, at_v], everyone, None)
                dkv[i, :, at_k] = rotary(dk, cosr[rows_of, :], -sinr[rows_of, :]).astype(BF16)
                dkv[i, :, at_v] = dv.astype(BF16)
                da[:, at_k] = da[:, at_k] + dq

            def away_tile(j):
                at = tile_at(j, 256)
                xda[i, :, at] = dot_nt(dkv[i], wq[at, width:3 * width]).astype(BF16)

            loop(pairs, pair_step)
            loop(width // 256, away_tile)

    def own_bias():
        key = blocks_of((group, share), 0)
        query = blocks_of((group, share), 1)
        return jnp.concatenate([block_bias(query, key, True), block_bias(query, key, False)], axis=1)

    def near_bias():
        same = blocks_of((share, share), 0) == blocks_of((share, share), 1)
        return jnp.where(same, 0.0, NEG).astype(F32)

    def attend_own(low, high):
        rows_of = tile_at(n, group)

        def pair_step(pair):
            at_k, at_v = tile_at(pair, 128), tile_at(pair + pairs, 128)
            dk, dv, dq = block(pair, kv[rows_of, at_k], kv[rows_of, at_v], everyone, own_bias)
            dqkv[share:, tile_at(pair + pairs, 128)] = rotary(dk, cosr[mine, :], -sinr[mine, :]).astype(BF16)
            dqkv[share:, tile_at(pair + 2 * pairs, 128)] = dv.astype(BF16)
            da[:, at_k] = da[:, at_k] + dq
            dk, dv, dq = block(pair, nkv[:, at_k], nkv[:, at_v], slice(0, share), near_bias)
            dqkv[:share, tile_at(pair + pairs, 128)] = rotary(dk, cosr[mine, :], -sinr[mine, :]).astype(BF16)
            dqkv[:share, tile_at(pair + 2 * pairs, 128)] = dv.astype(BF16)
            da[:share, at_k] = da[:share, at_k] + dq

        loop(high - low, lambda t: pair_step(t + low))

    pl.semaphore_wait(barrier, jnp.where(zdev.has_outer, 6, 5))

    def run(turn, slot):
        for word in PLAN.get((turn, slot), ()):
            r, act = every[int(word[0])][word[1]], word[2]
            if act == "3" and r.turn:
                every[r.turn - 1][word[1]].free_zb()
            {"1": r.p1, "2": r.p2, "s": r.p2s, "3": r.p3, "4": r.p4, "5": r.p5, "6": r.p6, "7": r.p7}[act]()

    for turn, layer in enumerate(order):
        last = turn == layers - 1
        after = lambda slot: run(turn, slot)

        def reuse(*names):
            if turn:
                for name in names:
                    every[turn - 1][name].free_grad()

        gain1, gain2 = par[2 * layer:2 * layer + 1, :], par[2 * layer + 1:2 * layer + 2, :]
        load = loads(layer)
        load[8].wait()
        transposed(dctx)
        to_bf16(db)
        da[...] = jnp.zeros_like(da)
        reuse("u", "d")

        def ff_step(j):
            slot = lax.rem(j, 2)
            for c in stream(layer, j, slot):
                c.wait()

            @pl.when(j + 1 < tiles)
            def _():
                for c in stream(layer, j + 1, 1 - slot):
                    c.start()

            dact = dot_nt(db[...], wd_s[slot])
            gd[tile_at(j, TILE), :] = dot_tn(act_s[slot], db[...]).astype(BF16)
            du = (dact * dg_s[slot].astype(F32)).astype(BF16)
            dg_s[slot] = du
            gu[:, tile_at(j, TILE)] = dot(at_[...], dg_s[slot]).astype(BF16)
            da[...] = da[...] + dot_nt(dg_s[slot], wu_s[slot])

        for k in range(3):
            low, high = tiles * k // 3, tiles * (k + 1) // 3
            loop(high - low, lambda j: ff_step(j + low))
            after("ffn%d" % k)
        load[0].wait()
        norm_back(mid, gain2, 2 * layer + 1, 2 * layers + 2 * layer + 1)
        if layer:
            load_h(layer).start()
        after("lnb")
        to_bf16(db)
        after("bf")
        load[1].wait()
        load[6].wait()
        reuse("o")

        def out_tile(j):
            at = tile_at(j, 256)
            go[:, at] = dot_tn(ctx[...], db[:, at]).astype(BF16)
            dctx[:, at] = dot_nt(db[...], wo[at, :]).astype(BF16)

        loop(width // 256, out_tile)
        after("out")
        if layer == 0:
            load_h(layer).start()
        load[5].wait()

        def delta_step(pair):
            at = tile_at(pair, 128)
            both = (dctx[:, at].astype(F32) * ctx[:, at].astype(F32)).T
            for h in range(2):
                delta[pl.ds(2 * pair + h, 1), :] = jnp.sum(both[64 * h:64 * h + 64], axis=0, keepdims=True)

        loop(pairs, delta_step)
        for c in load_first(layer):
            c.start()
        for i in range(3):
            @pl.when(takes[i])
            def _():
                load_far(layer, i).start()
        da[...] = jnp.zeros_like(da)
        after("delta")
        for k in (2, 3, 4, 7):
            load[k].wait()
        for i in (2, 1, 0):
            if turn:
                @pl.when(takes[i])
                def _():
                    kv_copy(i).wait_send()
            attend_remote(i)
            after("rem%d" % i)

            @pl.when(takes[i])
            def _():
                if turn:
                    pl.semaphore_wait(kcredit.at[i], 1)
                kv_copy(i).start()
            after("send%d" % i)
        attend_own(0, pairs // 2)
        after("own0")
        attend_own(pairs // 2, pairs)
        after("own1")
        for c in load_first(layer):
            c.wait()
        transposed(ctx)
        after("tr")

        def query_tile(t):
            v = da[:, tile_at(t, 128)] * 0.125
            dqkv[:, tile_at(t, 128)] = rotary_halves(v, cosr[mine, :], -sinr[mine, :]).astype(BF16)

        loop(pairs, query_tile)
        after("q")
        reuse("q")

        def grad_tile(j):
            at = tile_at(j, 256)
            grads["q"][:, at] = dot(at_[...], dqkv[:, at]).astype(BF16)

        loop(width // 256, grad_tile)
        after("gq")
        for i in range(3):
            @pl.when(takes[i])
            def _():
                load_far(layer, i).wait()

        def grad_tile_kv(j, skip, out):
            acc[...] = dot(at_[...], dqkv[:, tile_at(j + (1 + skip) * (width // 256), 256)])
            for i in range(3):
                @pl.when(takes[i])
                def _():
                    acc[...] = acc[...] + dot_tn(far[i], dkv[i, :, tile_at(j + skip * (width // 256), 256)])
            out[:, tile_at(j, 256)] = acc[...].astype(BF16)

        for k, name in enumerate("kv"):
            reuse(name)
            loop(width // 256, lambda j: grad_tile_kv(j, k, grads[name]))
            after("g" + name)

        def first_tile(j):
            at = tile_at(j, 256)
            da[:, at] = dot_nt(dqkv[...], wq[at, :])

        loop(width // 256, first_tile)
        after("da")
        load_h(layer).wait()
        entry = mid if layer else db
        for i in range(3):
            @pl.when(gives[i])
            def _():
                kv_copy(i).wait_recv()
                da[share:, :] = da[share:, :] + xda[i].astype(F32)
                if not last:
                    pl.semaphore_signal(kcredit.at[i], inc=1, device_id=peers[i], device_id_type=MESH)
        after("kvwait")
        norm_back(entry, gain1, 2 * layer, 2 * layers + 2 * layer)
        if not last:
            for c in stream(order[turn + 1], 0, 0):
                c.start()
            for c in loads(order[turn + 1]):
                c.start()
        after("lna")

    tot = SmallSum(here, gacc, sbuf, ssend, srecv)
    tot.begin()
    to_bf16(grad_tok)
    run(9, "tot0")
    tot.swap(0)
    run(9, "tot1")
    tot.swap(1)
    run(9, "tot2")
    tot.swap(2)
    run(9, "tot3")
    tot.chain()
    run(9, "tot4")
    tot.settle()
    tot.finish()
    part = width // 4
    for owner in range(4):
        @pl.when(n == owner)
        def _():
            cut = sbuf[0, 5, :, owner * part:(owner + 1) * part]
            for layer in range(layers):
                out_gain[layer] = cut[2 * layer:2 * layer + 2]
                row = 2 * layers + 2 * layer
                out_first[layer:layer + 1] = cut[row:row + 1]
                out_second[layer:layer + 1] = cut[row + 1:row + 2]
    for turn in every:
        for r in turn.values():
            r.p8()
    for r in every[-1].values():
        r.free_grad()
        r.free_zb()
    for i in range(3):
        @pl.when(takes[i])
        def _():
            kv_copy(i).wait_send()


def backward(lengths, cot, tok, par, tabs, full, kept):
    cosr, sinr = tabs
    rows, width = cot.shape
    share = rows // 2
    layers = full[0].shape[0]
    ff = full[2].shape[2]
    hbm = pl.BlockSpec(memory_space=pltpu.HBM)
    vmem = pl.BlockSpec(memory_space=pltpu.VMEM)
    shape = jax.ShapeDtypeStruct
    v = pltpu.VMEM
    dma, regular = pltpu.SemaphoreType.DMA, pltpu.SemaphoreType.REGULAR
    outs = [shape((layers, f.shape[1] // 4, f.shape[2]), BF16) for f in full]
    part = width // 4
    small = [shape((layers, 2, part), F32), shape((layers, part), F32), shape((layers, part), F32)]
    kinds = [(width, width)] * 4 + [(width, ff), (ff, width)]
    scratch = [v(k, BF16) for k in kinds] + [v((width // 2, ff), BF16), v((ff // 2, width), BF16)]
    for total, cols in kinds:
        quarter = total // 16
        scratch += [v((4 * quarter, cols), BF16), v((2 * quarter, cols), BF16),
                    v((2 * quarter, cols), BF16), v((quarter, cols), BF16), v((2 * quarter, cols), BF16)]
    scratch += [
        v((2, TILE, width), BF16), v((2, width, TILE), BF16), v((2, rows, TILE), BF16), v((2, rows, TILE), BF16),
        v((width, width), BF16), v((width, 3 * width), BF16),
        v((rows, width), F32), v((rows, width), F32), v((rows, width), F32),
        v((width, rows), BF16), v((rows, width), BF16),
        v((rows, width), BF16), v((4 * share, 2 * width), BF16), v((share, 2 * width), BF16),
        v((rows, width), BF16), v((rows, width), BF16),
        v((16, rows), F32), v((16, rows), F32),
        v((rows, 3 * width), BF16), v((3, share, 2 * width), BF16), v((3, share, width), BF16),
        v((3, share, width), BF16), v((width, 256), F32),
        v(par.shape, F32), v((2, 6) + par.shape, F32),
        dma((SLOTS * 6 * layers,)), dma((SLOTS * 6 * layers,)), regular((7 * 6,)), regular((8,)), dma((6 * layers,)),
        dma((3,)), dma((3,)), regular((3,)), dma((2, 4)), dma((16,)), dma((6,)), dma((6,)),
    ]
    return pl.pallas_call(
        partial(backward_kernel, layers),
        out_shape=[shape((rows, width), BF16)] + outs + small,
        in_specs=[pl.BlockSpec(memory_space=pltpu.SMEM)] + [hbm] * 2 + [vmem] * 3 + [hbm] * 16,
        out_specs=[vmem] + [hbm] * 4 + [vmem] * 3,
        scratch_shapes=scratch,
        compiler_params=pltpu.CompilerParams(
            collective_id=1, has_side_effects=True, vmem_limit_bytes=63 * 2**20),
        cost_estimate=pl.CostEstimate(flops=40 * 10**9, bytes_accessed=10**8, transcendentals=10**7),
        name="backward",
    )(lengths, cot, tok, par, cosr, sinr, *full, *kept)


def shared_params(norm_gains, norm_biases):
    layers, _, part = norm_gains.shape
    mine = jnp.concatenate([norm_gains.reshape(2 * layers, part), norm_biases.reshape(2 * layers, part)]).astype(F32)
    parts = lax.axis_size("narrow")
    owner = jnp.arange(parts) == lax.axis_index("narrow")
    return jnp.where(owner[None, :, None], mine[:, None, :], 0.0).reshape(4 * layers, parts * part)


def rotary_tables(seq, head_dim):
    half = head_dim // 2
    freq = np.exp(-np.log(np.float32(10000.0)) * np.arange(half, dtype=np.float32) * np.float32(2.0) / np.float32(head_dim))
    angle = np.arange(seq, dtype=np.float32)[:, None] * freq.astype(np.float32)[None, :]
    cosine, sine = np.cos(angle), np.sin(angle)
    return (jnp.asarray(np.tile(cosine, (1, 4)), F32),
            jnp.asarray(np.tile(np.concatenate([-sine, sine], axis=1), (1, 2)), F32))


def settle_kernel(*refs):
    half = len(refs) // 2
    for src, dst in zip(refs[:half], refs[half:]):
        dst[...] = src[...].astype(dst.dtype)


def settle(grads, rows, small):
    layers = grads[0].shape[0]
    halves = 2
    cut = lambda a: pl.BlockSpec((1, a.shape[1] // halves, a.shape[2]), lambda i, j: (i, j, 0))
    strip = lambda a: pl.BlockSpec((a.shape[0] // (layers * halves), a.shape[1]), lambda i, j: (i * halves + j, 0))
    whole = lambda a: pl.BlockSpec(a.shape, lambda i, j: (0,) * a.ndim)
    specs = [cut(a) for a in grads] + [strip(a) for a in rows] + [whole(a) for a in small]
    shape = jax.ShapeDtypeStruct
    outs = [shape(a.shape, F32) for a in grads] + [shape(a.shape, a.dtype) for a in (*rows, *small)]
    return pl.pallas_call(
        settle_kernel,
        grid=(layers, halves),
        out_shape=outs,
        in_specs=specs,
        out_specs=specs,
        compiler_params=pltpu.CompilerParams(vmem_limit_bytes=62 * 2**20),
        name="settle",
    )(*grads, *rows, *small)


def on_device(tokens, lengths, w_qkv, w_out, w_up, w_down, norm_gains, norm_biases, cotangent):
    _, _, share, width = tokens.shape
    tok = tokens.reshape(2 * share, width)
    tabs = rotary_tables(4 * share, width // H)
    outs = forward(tok, shared_params(norm_gains, norm_biases), *tabs, w_qkv, w_out, w_up, w_down)
    result, full, par, kept = outs[0], outs[1:5], outs[5], outs[6:]
    grad_tok, gq, go, gu, gd, gains, first, second = backward(
        lengths, cotangent.reshape(2 * share, width), tok, par, tabs, full, kept)
    gq, go, gu, gd, result, grad_tok, gains, first, second = settle(
        (gq, go, gu, gd), (result, grad_tok), (gains, first, second))
    return (
        result.reshape(tokens.shape), grad_tok.reshape(tokens.shape), gq, go, gu, gd, gains, first, second)


def solution(mesh):
    return jax.shard_map(
        on_device,
        mesh=mesh,
        in_specs=(
            P("wide", None, "narrow", None),
            P("wide"),
            P(None, "narrow", None),
            P(None, "narrow", None),
            P(None, "narrow", None),
            P(None, "narrow", None),
            P(None, None, "narrow"),
            P(None, None, "narrow"),
            P("wide", None, "narrow", None),
        ),
        out_specs=(
            P("wide", None, "narrow", None),
            P("wide", None, "narrow", None),
            P(None, "narrow", None),
            P(None, "narrow", None),
            P(None, "narrow", None),
            P(None, "narrow", None),
            P(None, None, "narrow"),
            P(None, "narrow"),
            P(None, "narrow"),
        ),
        check_vma=False,
    )
```

```python
from functools import partial

import jax
import jax.numpy as jnp
import numpy as np
from jax import lax
from jax.experimental import pallas as pl
from jax.experimental.pallas import tpu as pltpu
from jax.sharding import PartitionSpec as P

H = 12
BLOCK = 16
NEG = -1e30
EPS = 1e-05
MESH = pl.DeviceIdType.MESH
F32 = jnp.float32
BF16 = jnp.bfloat16
GELU_C = 0.7978845608028654
GELU_A = 0.044715


def dot(a, b):
    return jnp.dot(a, b, preferred_element_type=F32)


def dot_nt(a, b):
    return lax.dot_general(a, b, (((1,), (1,)), ((), ())), preferred_element_type=F32)


def dot_tn(a, b):
    return lax.dot_general(a, b, (((0,), (0,)), ((), ())), preferred_element_type=F32)


def tile_at(index, size):
    return pl.ds(pl.multiple_of(index * size, size), size)


def loop(count, body):
    lax.fori_loop(0, count, lambda i, _: (body(i), None)[1], None)


def rotary(x, cosine, sine):
    lane = lax.broadcasted_iota(jnp.int32, x.shape, 1)
    swapped = jnp.where(lane % 64 < 32, pltpu.roll(x, 96, 1), pltpu.roll(x, 32, 1))
    return x * cosine + swapped * sine


def rotary_halves(x, cosine, sine):
    half = x.shape[0] // 2
    return jnp.concatenate([rotary(x[:half], cosine, sine), rotary(x[half:], cosine, sine)], axis=0)


def block_bias(query, key, strict):
    allow = key < query if strict else key <= query
    return jnp.where(allow, 0.0, NEG).astype(F32)


def blocks_of(shape, dim):
    return lax.broadcasted_iota(jnp.int32, shape, dim) // BLOCK


def head_masks():
    lane = lax.broadcasted_iota(jnp.int32, (1, 128), 1)
    low = (lane < 64).astype(F32)
    return low, 1.0 - low


def norm_into(src, dst, gain, bias, rows):
    step = 256

    def body(i):
        at = tile_at(i, step)
        x = src[at, :].astype(F32)
        c = x - jnp.mean(x, axis=-1, keepdims=True)
        inv = lax.rsqrt(jnp.mean(c * c, axis=-1, keepdims=True) + EPS)
        dst[at, :] = (c * inv * gain + bias).astype(BF16)

    loop(rows // step, body)


class Gather:
    def __init__(self, here, shard, full, send, recv, base, lsem):
        self.n, self.w = here
        self.core = lax.rem(self.w, 2)
        self.shard, self.full, self.send, self.recv, self.base, self.lsem = (
            shard, full, send, recv, base, lsem)
        self.rows = shard.shape[0]
        self.half = self.rows // 2
        self.quarter = self.rows // 4
        self.x, self.y, self.d, self.s = (
            (self.n ^ 1, self.w), (self.n ^ 2, self.w), (self.n ^ 3, self.w), (self.n, self.w ^ 1))

    def region(self, owner, core, quarter=None):
        start = owner * self.rows + core * self.half
        if quarter is None:
            return self.full.at[pl.ds(pl.multiple_of(start, 16), self.half)]
        return self.full.at[pl.ds(pl.multiple_of(start + quarter * self.quarter, 16), self.quarter)]

    def copy(self, slot, src, dst, device):
        k = self.base + slot
        return pltpu.make_async_remote_copy(
            src_ref=src, dst_ref=dst, send_sem=self.send.at[k], recv_sem=self.recv.at[k],
            device_id=device, device_id_type=MESH)

    def own(self):
        return pltpu.make_async_copy(
            self.shard, self.full.at[pl.ds(pl.multiple_of(self.n * self.rows, 16), self.rows)], self.lsem)

    def plain(self, slot, region, device):
        return self.copy(slot, region, region, device)

    def issue(self):
        src = self.shard.at[pl.ds(pl.multiple_of(self.core * self.half, 16), self.half)]
        dst = self.region(self.n, self.core)
        self.copy(0, src, dst, self.x).start()
        self.copy(1, src, dst, self.y).start()
        self.own().start()

    def forward(self):
        nx, ny = self.x[0], self.y[0]
        self.plain(0, self.region(nx, self.core), self.x).wait_recv()
        self.plain(2, self.region(nx, self.core, 0), self.y).start()
        self.plain(4, self.region(nx, self.core), self.s).start()
        self.plain(1, self.region(ny, self.core), self.y).wait_recv()
        self.plain(3, self.region(ny, self.core, 1), self.x).start()
        self.plain(5, self.region(ny, self.core), self.s).start()

    def finish(self):
        nd = self.d[0]
        self.plain(2, self.region(nd, self.core, 0), self.y).wait_recv()
        self.plain(3, self.region(nd, self.core, 1), self.x).wait_recv()
        self.plain(6, self.region(nd, self.core), self.s).start()

    def use(self):
        other = 1 - self.core
        for slot, who in ((4, self.x), (5, self.y), (6, self.d)):
            self.plain(slot, self.region(who[0], other), self.s).wait_recv()
        self.own().wait()

    def drain(self):
        src = self.shard.at[pl.ds(pl.multiple_of(self.core * self.half, 16), self.half)]
        dst = self.region(self.n, self.core)
        self.copy(0, src, dst, self.x).wait_send()
        self.copy(1, src, dst, self.y).wait_send()
        nx, ny, nd = self.x[0], self.y[0], self.d[0]
        self.plain(2, self.region(nx, self.core, 0), self.y).wait_send()
        self.plain(3, self.region(ny, self.core, 1), self.x).wait_send()
        self.plain(4, self.region(nx, self.core), self.s).wait_send()
        self.plain(5, self.region(ny, self.core), self.s).wait_send()
        self.plain(6, self.region(nd, self.core), self.s).wait_send()


def forward_kernel(
    layers,
    tok, prm, cosr, sinr, wq, wo, wu, wd,
    result, fq, fo, fu, fd, prm_out,
    h_out, q_out, nkv_out, kv_out, lse_out, ctx_out, mid_out, act_out, dg_out, near_out, all_out, post_out,
    gq, go, gu, gd, prm_buf, par, hid, a, ag, post, q, nkv, kv, bias_c, bias_n,
    lset, ctx, mid, dg, act,
    send, recv, lsem, psend, precv, ksend, krecv, ssem,
):
    n = lax.axis_index("narrow")
    w = lax.axis_index("wide")
    rows, width = tok.shape
    share = rows // 2
    group = share
    pairs = width // 128
    ff = wu.shape[2]
    peers = ((n ^ 1, w), (n ^ 2, w), (n ^ 3, w))

    barrier = pltpu.get_barrier_semaphore()
    for device in peers + ((n, w ^ 1),):
        pl.semaphore_signal(barrier, inc=1, device_id=device, device_id_type=MESH)
    pl.semaphore_wait(barrier, 4)

    tensors = []
    for layer in range(layers):
        for kind, (shard, full) in enumerate(((wq, gq), (wo, go), (wu, gu), (wd, gd))):
            k = layer * 4 + kind
            tensors.append(Gather((n, w), shard.at[layer], full.at[layer], send, recv, 7 * k, lsem.at[k]))

    def params(i):
        return pltpu.make_async_remote_copy(
            src_ref=prm, dst_ref=prm_buf.at[i], send_sem=psend.at[i], recv_sem=precv.at[i],
            device_id=peers[i], device_id_type=MESH)

    def share_a(layer, i):
        region = ag.at[layer, tile_at(n, share)]
        return pltpu.make_async_remote_copy(
            src_ref=region, dst_ref=region, send_sem=ksend.at[3 * layer + i],
            recv_sem=krecv.at[3 * layer + i], device_id=peers[i], device_id_type=MESH)

    def recv_a(layer, i):
        region = ag.at[layer, tile_at(peers[i][0], share)]
        return pltpu.make_async_remote_copy(
            src_ref=region, dst_ref=region, send_sem=ksend.at[3 * layer + i],
            recv_sem=krecv.at[3 * layer + i], device_id=peers[i], device_id_type=MESH)

    gives = (n % 2 == 0, n < 2, n < 2)
    takes = (n % 2 == 1, n >= 2, n >= 2)

    for i in range(3):
        params(i).start()
    tensors[0].issue()

    def saves(layer):
        pieces = [
            (q, q_out.at[layer]), (nkv, nkv_out.at[layer]), (kv, kv_out.at[layer]),
            (lset, lse_out.at[layer]), (ctx, ctx_out.at[layer]), (mid, mid_out.at[layer]), (act, act_out.at[layer]),
            (dg, dg_out.at[layer]), (hid, h_out.at[layer]), (a.at[:share], near_out.at[layer]),
            (ag.at[layer], all_out.at[layer]), (post, post_out.at[layer]),
        ]
        return [pltpu.make_async_copy(s, d, ssem.at[layer * 12 + k]) for k, (s, d) in enumerate(pieces)]

    def weight_saves():
        pieces = ((gq, fq), (go, fo), (gu, fu), (gd, fd))
        out = []
        for layer in range(layers):
            for kind, (s, d) in enumerate(pieces):
                k = layer * 4 + kind
                out.append(pltpu.make_async_copy(s.at[layer], d.at[layer], ssem.at[12 * layers + k]))
        return out

    for i in range(3):
        params(i).wait_recv()
    par[...] = prm[...] + prm_buf[0] + prm_buf[1] + prm_buf[2]
    prm_out[...] = par[...]

    for k in range(2):
        at = slice(k * share, (k + 1) * share)
        bias_c[:, at] = block_bias(blocks_of((share, share), 1), blocks_of((share, share), 0), k == 0)
    same = blocks_of((share, share), 0) == blocks_of((share, share), 1)
    bias_n[...] = jnp.where(same, 0.0, NEG).astype(F32)
    masks = head_masks()
    here = tile_at(n, share)

    full_saves = weight_saves()
    for layer in range(layers):
        t_qkv, t_out, t_up, t_down = tensors[4 * layer:4 * layer + 4]
        later = tensors[4 * layer + 4:]
        gain1, gain2 = par[2 * layer:2 * layer + 1, :], par[2 * layer + 1:2 * layer + 2, :]
        at = 2 * layers + 2 * layer
        bias1, bias2 = par[at:at + 1, :], par[at + 1:at + 2, :]
        saved = saves(layer)
        before = saves(layer - 1) if layer else None
        if before:
            before[9].wait()
        if layer == 0:
            norm_into(tok, a, gain1, bias1, rows)
        else:
            norm_into(hid, a, gain1, bias1, rows)
        ag[layer, here] = a[share:]
        t_qkv.forward()
        for i in range(3):
            @pl.when(gives[i])
            def _():
                share_a(layer, i).start()
        saved[9].start()
        t_out.issue()
        t_up.issue()
        t_qkv.finish()
        t_qkv.use()
        full_saves[4 * layer].start()
        if before:
            before[0].wait()
            before[1].wait()
            before[2].wait()

        wqkv = gq.at[layer]

        def query_tile(j):
            x = dot(a[...], wqkv[:, tile_at(j, 256)])
            for part in range(2):
                v = rotary_halves(x[:, 128 * part:128 * part + 128], cosr[here, :], sinr[here, :])
                q[:, tile_at(2 * j + part, 128)] = (v.astype(BF16).astype(F32) * 0.125).astype(BF16)

        def key_tile(j):
            x = dot(a[...], wqkv[:, tile_at(j + 3, 256)])
            for part in range(2):
                v = rotary_halves(x[:, 128 * part:128 * part + 128], cosr[here, :], sinr[here, :]).astype(BF16)
                nkv[:, tile_at(2 * j + part, 128)] = v[:share]
                kv[here, tile_at(2 * j + part, 128)] = v[share:]

        def value_tile(j):
            v = dot(a[...], wqkv[:, tile_at(j + 6, 256)]).astype(BF16)
            nkv[:, tile_at(j + 3, 256)] = v[:share]
            kv[here, tile_at(j + 3, 256)] = v[share:]

        def far_tiles(g):
            at = tile_at(g, share)

            def far_key(j):
                x = dot(ag[layer, at, :], wqkv[:, tile_at(j + 3, 256)])
                for part in range(2):
                    v = rotary(x[:, 128 * part:128 * part + 128], cosr[at, :], sinr[at, :])
                    kv[at, tile_at(2 * j + part, 128)] = v.astype(BF16)

            def far_value(j):
                kv[at, tile_at(j + 3, 256)] = dot(ag[layer, at, :], wqkv[:, tile_at(j + 6, 256)]).astype(BF16)

            loop(3, far_key)
            loop(3, far_value)

        loop(3, key_tile)
        loop(3, value_tile)
        loop(3, query_tile)
        saved[0].start()
        saved[1].start()
        t_down.issue()
        for i in range(3):
            @pl.when(takes[i])
            def _():
                recv_a(layer, i).wait_recv()
        saved[10].start()
        loop(n, far_tiles)
        saved[2].start()
        if before:
            before[3].wait()
            before[4].wait()

        def fold(v, how):
            v = v.reshape(v.shape[0] // 8, 8, v.shape[1])
            return how(how(v, axis=0), axis=0, keepdims=True)

        def pair_step(pair):
            at_pair = tile_at(pair, 128)
            at_value = tile_at(pair + pairs, 128)
            q2 = q[:, at_pair].astype(F32)
            qm = [(q2 * masks[h]).astype(BF16) for h in range(2)]
            lower = [slice(64 * h, 64 * h + 64) for h in range(2)]

            def absorb(s, v2, carry):
                most, total, out = carry
                peak = jnp.maximum(most, fold(s, jnp.max))
                p = jnp.exp(s - peak)
                shrink = jnp.exp(most - peak)
                total = total * shrink + fold(p, jnp.sum)
                out = out * shrink + dot(v2, p.astype(BF16))
                return peak, total, out

            near_v = nkv[:, at_value].T
            own_v = kv[here, at_value].T
            blank = (jnp.full((1, share), NEG, F32), jnp.zeros((1, share), F32), jnp.zeros((64, share), F32))
            states = []
            for h in range(2):
                s = dot_nt(nkv[:, at_pair], qm[h][:share]) + bias_n[...]
                most = fold(s, jnp.max)
                p = jnp.exp(s - most)
                near = (most, fold(p, jnp.sum), dot(near_v[lower[h]], p.astype(BF16)))
                state = tuple(jnp.concatenate([a, b], axis=1) for a, b in zip(near, blank))
                s = dot_nt(kv[here, at_pair], qm[h]) + bias_c[...]
                states.append(absorb(s, own_v[lower[h]], state))

            def far_step(g, states):
                at = tile_at(g, group)
                far_v = kv[at, at_value].T
                scores = [dot_nt(kv[at, at_pair], qm[h]) for h in range(2)]
                return tuple(absorb(scores[h], far_v[lower[h]], states[h]) for h in range(2))

            states = lax.fori_loop(0, n, far_step, tuple(states))
            outs = []
            for h, (most, total, out) in enumerate(states):
                outs.append(out / total)
                lset[pl.ds(2 * pair + h, 1), :] = most + jnp.log(total)
            ctx[:, at_pair] = jnp.concatenate(outs, axis=0).T.astype(BF16)

        loop(pairs // 2, pair_step)
        t_out.forward()
        t_up.forward()
        loop(pairs - pairs // 2, lambda t: pair_step(t + pairs // 2))
        saved[3].start()
        saved[4].start()
        t_out.finish()
        t_up.finish()
        t_down.forward()
        if later:
            later[0].issue()
        t_out.use()
        full_saves[4 * layer + 1].start()
        if before:
            before[5].wait()
            before[6].wait()
            before[7].wait()
            before[8].wait()

        def out_tile(j):
            at = tile_at(j, 256)
            base = (tok if layer == 0 else hid)[:, at].astype(F32)
            mid[:, at] = base + dot(ctx[...], go[layer, :, at])

        loop(width // 256, out_tile)
        saved[5].start()
        if before:
            before[11].wait()
        norm_into(mid, post, gain2, bias2, rows)
        saved[11].start()
        t_up.use()
        full_saves[4 * layer + 2].start()

        def up_tile(j):
            at = tile_at(j, 256)
            x = dot(post[...], gu[layer, :, at])
            x2 = x * x
            t = jnp.tanh(GELU_C * (x + GELU_A * (x * x2)))
            cdf = 0.5 + 0.5 * t
            act[:, at] = (x * cdf).astype(BF16)
            slope = GELU_C * (1.0 + 3.0 * GELU_A * x2)
            dg[:, at] = (cdf + 0.5 * x * (1.0 - t * t) * slope).astype(BF16)

        loop(ff // 256, up_tile)
        saved[6].start()
        saved[7].start()
        t_down.finish()
        t_down.use()
        full_saves[4 * layer + 3].start()

        def down_tile(j):
            at = tile_at(j, 256)
            out = mid[:, at] + dot(act[...], gd[layer, :, at])
            hid[:, at] = out
            if layer == layers - 1:
                result[:, at] = out.astype(BF16)

        loop(width // 256, down_tile)
        saved[8].start()

    for c in saves(layers - 1):
        c.wait()
    for layer in range(layers - 1):
        saves(layer)[10].wait()
    for c in full_saves:
        c.wait()
    for t in tensors:
        t.drain()
    for i in range(3):
        params(i).wait_send()
        for layer in range(layers):
            @pl.when(gives[i])
            def _():
                share_a(layer, i).wait_send()


def forward(tokens, prm, cosr, sinr, w_qkv, w_out, w_up, w_down):
    rows, width = tokens.shape
    share = rows // 2
    layers = w_qkv.shape[0]
    seq = share * 4
    qw, ff = w_qkv.shape[2], w_up.shape[2]
    full = [
        jax.ShapeDtypeStruct((layers, width, qw), BF16),
        jax.ShapeDtypeStruct((layers, width, width), BF16),
        jax.ShapeDtypeStruct((layers, width, ff), BF16),
        jax.ShapeDtypeStruct((layers, ff, width), BF16),
    ]
    hbm = pl.BlockSpec(memory_space=pltpu.HBM)
    vmem = pl.BlockSpec(memory_space=pltpu.VMEM)
    shape = jax.ShapeDtypeStruct
    kept = [
        shape((layers, rows, width), F32),
        shape((layers, rows, width), BF16),
        shape((layers, share, 2 * width), BF16),
        shape((layers, seq, 2 * width), BF16),
        shape((layers, 16, rows), F32),
        shape((layers, rows, width), BF16),
        shape((layers, rows, width), F32),
        shape((layers, rows, ff), BF16),
        shape((layers, rows, ff), BF16),
        shape((layers, share, width), BF16),
        shape((layers, seq, width), BF16),
        shape((layers, rows, width), BF16),
    ]
    dma, count = pltpu.SemaphoreType.DMA, 7 * 4 * layers
    return pl.pallas_call(
        partial(forward_kernel, layers),
        out_shape=[shape((rows, width), BF16)] + full + [shape(prm.shape, F32)] + kept,
        in_specs=[vmem] * 4 + [hbm] * 4,
        out_specs=[vmem] + [hbm] * 4 + [vmem] + [hbm] * 12,
        scratch_shapes=[pltpu.VMEM(f.shape, BF16) for f in full] + [
            pltpu.VMEM((3,) + prm.shape, F32),
            pltpu.VMEM(prm.shape, F32),
            pltpu.VMEM((rows, width), F32),
            pltpu.VMEM((rows, width), BF16),
            pltpu.VMEM((layers, seq, width), BF16),
            pltpu.VMEM((rows, width), BF16),
            pltpu.VMEM((rows, width), BF16),
            pltpu.VMEM((share, 2 * width), BF16),
            pltpu.VMEM((seq, 2 * width), BF16),
            pltpu.VMEM((share, rows), F32),
            pltpu.VMEM((share, share), F32),
            pltpu.VMEM((16, rows), F32),
            pltpu.VMEM((rows, width), BF16),
            pltpu.VMEM((rows, width), F32),
            pltpu.VMEM((rows, ff), BF16),
            pltpu.VMEM((rows, ff), BF16),
            dma((count,)), dma((count,)), dma((4 * layers,)),
            dma((3,)), dma((3,)), dma((3 * layers,)), dma((3 * layers,)),
            dma((16 * layers,)),
        ],
        compiler_params=pltpu.CompilerParams(
            collective_id=0, has_side_effects=True, vmem_limit_bytes=62 * 2**20),
        cost_estimate=pl.CostEstimate(flops=20 * 10**9, bytes_accessed=10**8, transcendentals=10**7),
        name="forward",
    )(tokens, prm, cosr, sinr, w_qkv, w_out, w_up, w_down)


def add_rows(dst, at, left, left_at, right, right_at, rows):
    size = 48 if rows % 48 == 0 else 16

    def body(i):
        step = lambda base: pl.ds(pl.multiple_of(base + size * i, 16), size)
        dst[step(at), :] = left[step(left_at), :] + right[step(right_at), :]

    loop(rows // size, body)


class Reduce:
    def __init__(self, here, turn, turns, kind, grad, bufs, out, send, recv, base, credit, cbase, lend, lsem):
        self.n, self.w = here
        self.turn, self.turns, self.kind = turn, turns, kind
        self.lend = lend
        self.grad, self.out = grad, out
        self.s1, self.r2, self.r3, self.r4, self.r5, self.zb = bufs
        self.send, self.recv, self.base = send, recv, base
        self.credit, self.cbase, self.lsem = credit, cbase, lsem
        self.core = lax.rem(self.w, 2)
        self.rows = grad.shape[0] // 4
        self.half, self.quarter = self.rows // 2, self.rows // 4
        n, w = here
        self.x, self.y, self.d, self.s = (n ^ 1, w), (n ^ 2, w), (n ^ 3, w), (n, w ^ 1)
        chips = lax.axis_size("wide") // 2
        z = w // 2
        left = z < chips // 2
        step = jnp.where(left, 2, -2)
        self.inner, self.outer = (n, w + step), (n, w - step)
        self.has_outer = jnp.logical_and(z > 0, z < chips - 1)
        self.is_mid = jnp.logical_or(z == chips // 2 - 1, z == chips // 2)
        self.mine = jnp.where(left, 0, 1)

    def at(self, owner, core, quarter=0):
        return pl.multiple_of(owner * self.rows + core * self.half + quarter * self.quarter, 16)

    def part(self, ref, start, count):
        return ref.at[pl.ds(pl.multiple_of(start, 16), count)]

    def copy(self, slot, src, dst, device):
        k = self.base + slot
        return pltpu.make_async_remote_copy(
            src_ref=src, dst_ref=dst, send_sem=self.send.at[k], recv_sem=self.recv.at[k],
            device_id=device, device_id_type=MESH)

    def take(self, slot):
        if self.turn > 0:
            pl.semaphore_wait(self.credit.at[self.cbase + slot], 1)

    def give(self, slot, device):
        if self.turn < self.turns - 1:
            pl.semaphore_signal(
                self.credit.at[self.cbase + slot], inc=1, device_id=device, device_id_type=MESH)

    def to_sibling(self):
        out = []
        for m in range(4):
            src = self.part(self.grad, self.at(m, 1 - self.core), self.half)
            out.append(self.copy(m, src, self.part(self.s1, m * self.half, self.half), self.s))
        return out

    def first_hop(self):
        q, g, c = self.quarter, self.grad, self.core
        nx, ny, nd = self.x[0], self.y[0], self.d[0]
        plan = ((4, nx, 0, 0, self.x), (5, nd, 0, 1, self.x), (6, ny, 1, 2, self.y), (7, nd, 1, 3, self.y))
        return [
            self.copy(slot, self.part(g, self.at(owner, c, quarter), q), self.part(self.r2, place * q, q), device)
            for slot, owner, quarter, place, device in plan]

    def second_hop(self):
        q, g, c = self.quarter, self.grad, self.core
        return [
            self.copy(8, self.part(g, self.at(self.y[0], c, 0), q), self.part(self.r3, 0, q), self.y),
            self.copy(9, self.part(g, self.at(self.x[0], c, 1), q), self.part(self.r3, q, q), self.x)]

    def inward(self):
        return self.copy(10, self.zb, self.r4, self.inner)

    def across(self):
        src = self.part(self.zb, (1 - self.mine) * self.quarter, self.quarter)
        return self.copy(11, src, self.r5, self.inner)

    def done_at(self, core, quarter):
        start = core * self.half + quarter * self.quarter
        return self.part(self.out, start, self.quarter)

    def final(self, quarter, device, slot, from_zb):
        dst = self.done_at(self.core, quarter)
        src = self.part(self.zb, quarter * self.quarter, self.quarter) if from_zb else dst
        return self.copy(slot, src, dst, device)

    def keep(self):
        src = self.part(self.zb, self.mine * self.quarter, self.quarter)
        return pltpu.make_async_copy(src, self.done_at(self.core, self.mine), self.lsem)

    def p1(self):
        if self.kind == "d":
            self.take(0)
        elif self.kind == "u":
            for k in range(4 if self.turn else 0):
                pl.semaphore_wait(self.lend.at[k + 4], 1)
        else:
            pl.semaphore_wait(self.lend.at["qkvo".index(self.kind)], 1)
        for c in self.to_sibling():
            c.start()

    def p2(self):
        g = self.grad
        for m, c in enumerate(self.to_sibling()):
            c.wait_recv()
            add_rows(g, self.at(m, self.core), g, self.at(m, self.core), self.s1, m * self.half, self.half)
        if self.kind == "d":
            self.give(0, self.s)
        elif self.kind == "u":
            for k in range(4):
                pl.semaphore_signal(self.lend.at[k], inc=1, device_id=self.s, device_id_type=MESH)
        elif self.turn < self.turns - 1:
            k = "qkvo".index(self.kind) + 4
            pl.semaphore_signal(self.lend.at[k], inc=1, device_id=self.s, device_id_type=MESH)

    def p2s(self):
        self.take(1)
        self.take(2)
        for c in self.first_hop():
            c.start()

    def p3(self):
        g, q = self.grad, self.quarter
        hops = self.first_hop()
        hops[1].wait_recv()
        at = self.at(self.y[0], self.core, 0)
        add_rows(g, at, g, at, self.r2, q, q)
        self.take(3)
        self.second_hop()[0].start()
        hops[3].wait_recv()
        at = self.at(self.x[0], self.core, 1)
        add_rows(g, at, g, at, self.r2, 3 * q, q)
        self.take(4)
        self.second_hop()[1].start()
        for k in range(2):
            hops[2 * k].wait_recv()
            at = self.at(self.n, self.core, k)
            add_rows(self.zb, k * q, g, at, self.r2, 2 * k * q, q)
        self.give(1, self.x)
        self.give(2, self.y)

    def p4(self):
        q = self.quarter
        for k, c in enumerate(self.second_hop()):
            c.wait_recv()
            add_rows(self.zb, k * q, self.zb, k * q, self.r3, k * q, q)
        self.give(3, self.y)
        self.give(4, self.x)

        @pl.when(jnp.logical_not(jnp.logical_or(self.has_outer, self.is_mid)))
        def _():
            self.take(5)
            self.inward().start()

    def p5(self):
        @pl.when(self.has_outer)
        def _():
            self.inward().wait_recv()
            add_rows(self.zb, 0, self.zb, 0, self.r4, 0, self.half)
            self.give(5, self.outer)

        @pl.when(self.is_mid)
        def _():
            self.take(6)
            self.across().start()

        @pl.when(jnp.logical_and(self.has_outer, jnp.logical_not(self.is_mid)))
        def _():
            self.take(5)
            self.inward().start()

    def p6(self):
        @pl.when(self.is_mid)
        def _():
            self.across().wait_recv()
            at = self.mine * self.quarter
            add_rows(self.zb, at, self.zb, at, self.r5, 0, self.quarter)
            self.give(6, self.inner)
            self.keep().start()
            self.final(self.mine, self.inner, 12, True).start()
            self.final(self.mine, self.s, 13, True).start()

        @pl.when(jnp.logical_and(self.is_mid, self.has_outer))
        def _():
            self.final(self.mine, self.outer, 15, True).start()

    def p7(self):
        other = 1 - self.mine

        @pl.when(self.is_mid)
        def _():
            self.final(other, self.inner, 12, False).wait_recv()
            self.final(other, self.s, 14, False).start()

        @pl.when(jnp.logical_and(self.is_mid, self.has_outer))
        def _():
            self.final(other, self.outer, 16, False).start()

        @pl.when(jnp.logical_not(self.is_mid))
        def _():
            self.final(self.mine, self.inner, 15, False).wait_recv()
            self.final(self.mine, self.s, 13, False).start()
            self.final(other, self.inner, 16, False).wait_recv()
            self.final(other, self.s, 14, False).start()

        @pl.when(jnp.logical_and(jnp.logical_not(self.is_mid), self.has_outer))
        def _():
            self.final(self.mine, self.outer, 15, False).start()
            self.final(other, self.outer, 16, False).start()

    def p8(self):
        for k, quarter in ((13, self.mine), (14, 1 - self.mine)):
            region = self.done_at(1 - self.core, quarter)
            self.copy(k, region, region, self.s).wait_recv()

    def free_grad(self):
        for c in self.to_sibling() + self.first_hop() + self.second_hop():
            c.wait_send()

    def free_zb(self):
        @pl.when(jnp.logical_not(self.is_mid))
        def _():
            self.inward().wait_send()

        @pl.when(self.is_mid)
        def _():
            self.across().wait_send()
            self.final(self.mine, self.inner, 12, True).wait_send()
            self.keep().wait()

        other = 1 - self.mine
        self.final(self.mine, self.s, 13, False).wait_send()
        self.final(other, self.s, 14, False).wait_send()

        @pl.when(self.has_outer)
        def _():
            self.final(self.mine, self.outer, 15, False).wait_send()
            self.final(other, self.outer, 16, False).wait_send()


SLOTS = 17


class SmallSum:
    def __init__(self, here, acc, buf, send, recv):
        n, w = here
        self.acc, self.buf, self.send, self.recv = acc, buf, send, recv
        chips = lax.axis_size("wide") // 2
        z = w // 2
        left = z < chips // 2
        step = jnp.where(left, 2, -2)
        self.inner, self.outer = (n, w + step), (n, w - step)
        self.has_outer = jnp.logical_and(z > 0, z < chips - 1)
        self.is_mid = jnp.logical_or(z == chips // 2 - 1, z == chips // 2)
        self.others = ((n, w ^ 1), (n ^ 1, w), (n ^ 2, w))

    def copy(self, slot, device):
        return pltpu.make_async_remote_copy(
            src_ref=self.buf.at[0, slot], dst_ref=self.buf.at[1, slot], send_sem=self.send.at[slot],
            recv_sem=self.recv.at[slot], device_id=device, device_id_type=MESH)

    def begin(self):
        self.buf[0, 0] = self.acc[...]
        self.copy(0, self.others[0]).start()

    def swap(self, slot):
        self.copy(slot, self.others[slot]).wait_recv()
        self.buf[0, slot + 1] = self.buf[0, slot] + self.buf[1, slot]
        if slot < 2:
            self.copy(slot + 1, self.others[slot + 1]).start()

    def chain(self):
        @pl.when(self.has_outer)
        def _():
            self.copy(3, self.outer).wait_recv()
            self.buf[0, 3] = self.buf[0, 3] + self.buf[1, 3]

        @pl.when(jnp.logical_not(self.is_mid))
        def _():
            self.copy(3, self.inner).start()

        @pl.when(self.is_mid)
        def _():
            self.buf[0, 4] = self.buf[0, 3]
            self.copy(4, self.inner).start()

    def settle(self):
        @pl.when(self.is_mid)
        def _():
            self.copy(4, self.inner).wait_recv()
            self.buf[0, 5] = self.buf[0, 4] + self.buf[1, 4]

        @pl.when(jnp.logical_not(self.is_mid))
        def _():
            self.copy(5, self.inner).wait_recv()
            self.buf[0, 5] = self.buf[1, 5]

        @pl.when(self.has_outer)
        def _():
            self.copy(5, self.outer).start()

    def finish(self):
        for k in range(3):
            self.copy(k, self.others[k]).wait_send()

        @pl.when(jnp.logical_not(self.is_mid))
        def _():
            self.copy(3, self.inner).wait_send()

        @pl.when(self.is_mid)
        def _():
            self.copy(4, self.inner).wait_send()

        @pl.when(self.has_outer)
        def _():
            self.copy(5, self.outer).wait_send()


PLAN = {
    (0, "ffn2"): ("0u1",),
    (0, "out"): ("0u2", "0us",),
    (0, "send2"): ("0o1",),
    (0, "send1"): ("0d1",),
    (0, "rem0"): ("0u3",),
    (0, "q"): ("0d2", "0ds",),
    (0, "gk"): ("0q1", "0u4",),
    (0, "da"): ("0k1",),
    (0, "lna"): ("0v1", "0o2", "0k2", "0ks", "0d3", "0os",),
    (1, "ffn2"): ("0d4", "0o3",),
    (1, "lnb"): ("0k3", "0u5",),
    (1, "out"): ("0v2", "0vs", "0q2", "0qs", "0k4",),
    (1, "delta"): ("1d1",),
    (1, "rem2"): ("0v3", "0d5", "0k5",),
    (1, "send2"): ("0q3", "1u1",),
    (1, "rem1"): ("1d2", "0u6", "0v4", "1u2", "1us",),
    (1, "send1"): ("0q4", "0d6",),
    (1, "own0"): ("0u7",),
    (1, "own1"): ("1u3", "0q5",),
    (1, "tr"): ("0d7",),
    (1, "q"): ("1ds",),
    (1, "gq"): ("0k6",),
    (1, "gk"): ("0q6", "1q1", "1k1", "1u4", "0v5",),
    (1, "da"): ("0o4",),
    (9, "tot0"): ("1d3", "1v1", "0v6", "0v7", "0q7", "1k2", "1ks", "1o1",),
    (9, "tot1"): ("1d4", "1u5", "1o2", "0k7",),
    (9, "tot2"): ("0o5", "1u6", "1v2", "1vs", "1q2", "1qs",),
    (9, "tot3"): ("1k3", "0o6",),
    (9, "tot4"): ("1v3", "1os", "0o7", "1u7", "1d5", "1k4", "1o3", "1q3", "1v4", "1d6", "1k5", "1o4", "1q4", "1v5", "1d7", "1k6", "1o5", "1q5", "1v6", "1k7", "1o6", "1q6", "1v7", "1o7", "1q7",),
}
TILE = 512


def backward_kernel(
    layers,
    lens, cot, tok, par, cosr, sinr,
    fq, fo, fu, fd, h_in, q_in, nkv_in, kv_in, lse_in, ctx_in, mid_in, act_in, dg_in, near_in, all_in, post_in,
    grad_tok, oq, oo, ou, od, out_gain, out_first, out_second,
    *rest,
):
    width = cot.shape[1]
    grads, big, small_s1 = dict(zip("qkvoud", rest[:6])), rest[6], rest[7]
    bufs = {kind: rest[8 + 5 * k:13 + 5 * k] for k, kind in enumerate("qkvoud")}
    rest = rest[38:]
    (wd_s, wu_s, act_s, dg_s, wo, wq, dh, mid, da, at_, db, q, kv, nkv, ctx, dctx, lset, delta, dqkv, dkv, xda, far, acc,
     gacc, sbuf, send, recv, credit, lend, lsem, ksend, krecv, kcredit, stsem, ldsem, ssend, srecv) = rest
    n = lax.axis_index("narrow")
    w = lax.axis_index("wide")
    here = (n, w)
    rows, width = cot.shape
    share = rows // 2
    group = share
    pairs = width // 128
    ff = act_in.shape[2]
    tiles = ff // TILE
    peers = ((n ^ 1, w), (n ^ 2, w), (n ^ 3, w))
    gives = (n % 2 == 0, n < 2, n < 2)
    takes = (n % 2 == 1, n >= 2, n >= 2)
    order = list(reversed(range(layers)))

    def reducers(turn):
        layer = order[turn]
        made = {}
        for kind, name in enumerate("qkvoud"):
            if name in "qkv":
                out = oq.at[layer, :, kind * width:(kind + 1) * width]
            else:
                out = {"o": oo, "u": ou, "d": od}[name].at[layer]
            s1 = {"u": big, "d": small_s1}.get(name)
            if s1 is None:
                s1 = big.at[:, kind * width:(kind + 1) * width]
            k = turn * 6 + kind
            made[name] = Reduce(here, turn, layers, name, grads[name], (s1,) + tuple(bufs[name]), out, send, recv,
                                SLOTS * k, credit, 7 * kind, lend, lsem.at[k])
        return made

    every = [reducers(turn) for turn in range(layers)]

    barrier = pltpu.get_barrier_semaphore()
    zdev = every[0]["q"]
    hello = peers + ((n, w ^ 1), zdev.inner)
    for device in hello:
        pl.semaphore_signal(barrier, inc=1, device_id=device, device_id_type=MESH)

    @pl.when(zdev.has_outer)
    def _():
        pl.semaphore_signal(barrier, inc=1, device_id=zdev.outer, device_id_type=MESH)

    def stream(layer, j, slot):
        cols = tile_at(j, TILE)
        return [
            pltpu.make_async_copy(fd.at[layer, cols], wd_s.at[slot], stsem.at[slot, 0]),
            pltpu.make_async_copy(fu.at[layer, :, cols], wu_s.at[slot], stsem.at[slot, 1]),
            pltpu.make_async_copy(act_in.at[layer, :, cols], act_s.at[slot], stsem.at[slot, 2]),
            pltpu.make_async_copy(dg_in.at[layer, :, cols], dg_s.at[slot], stsem.at[slot, 3]),
        ]

    def loads(layer):
        pieces = ((mid_in, mid), (ctx_in, ctx), (q_in, q), (nkv_in, nkv), (kv_in, kv), (lse_in, lset), (fo, wo), (fq, wq),
                  (post_in, dctx))
        return [pltpu.make_async_copy(s.at[layer], d, ldsem.at[k]) for k, (s, d) in enumerate(pieces)]

    def load_h(layer):
        if layer == 0:
            return pltpu.make_async_copy(tok, db, ldsem.at[10])
        return pltpu.make_async_copy(h_in.at[layer - 1], mid, ldsem.at[10])

    def load_first(layer):
        own = all_in.at[layer, tile_at(n, share)]
        return [pltpu.make_async_copy(near_in.at[layer], ctx.at[:share], ldsem.at[11]),
                pltpu.make_async_copy(own, ctx.at[share:], ldsem.at[12])]

    def load_far(layer, i):
        return pltpu.make_async_copy(all_in.at[layer, tile_at(peers[i][0], share)], far.at[i], ldsem.at[13 + i])

    for c in stream(order[0], 0, 0):
        c.start()
    for c in loads(order[0]):
        c.start()

    local = lax.broadcasted_iota(jnp.int32, (share, 1), 0) + n * share
    valid = (local < lens[0]).astype(F32)
    first_load = pltpu.make_async_copy(cot, db, ldsem.at[9])
    first_load.start()
    first_load.wait()
    for k in range(2):
        dh[k * share:(k + 1) * share] = db[k * share:(k + 1) * share, :].astype(F32) * valid
    gacc[...] = jnp.zeros_like(gacc)
    go, gu, gd = grads["o"], grads["u"], grads["d"]
    masks = head_masks()
    mine = tile_at(n, share)

    def to_bf16(dst):
        def body(i):
            at = tile_at(i, 256)
            dst[at, :] = dh[at, :].astype(BF16)

        loop(rows // 256, body)

    def norm_of(src, at):
        x = src[at, :].astype(F32)
        c = x - jnp.mean(x, axis=-1, keepdims=True)
        inv = lax.rsqrt(jnp.mean(c * c, axis=-1, keepdims=True) + EPS)
        return c * inv, inv

    def transposed(src):
        for i in range(rows // 128):
            at_[:, 128 * i:128 * i + 128] = src[128 * i:128 * i + 128, :].T

    def norm_back(src, gain, row_gain, row_bias):
        step = 256

        def body(i, carry):
            at = tile_at(i, step)
            normed, inv = norm_of(src, at)
            g = da[at, :]
            e = g * gain
            dv = inv * (e - jnp.mean(e, axis=-1, keepdims=True)
                        - normed * jnp.mean(e * normed, axis=-1, keepdims=True))
            dh[at, :] = dh[at, :] + dv
            fold = lambda v: v.reshape(step // 8, 8, width).sum(axis=0)
            return carry[0] + fold(g * normed), carry[1] + fold(g)

        zero = jnp.zeros((8, width), F32)
        one, two = lax.fori_loop(0, rows // step, body, (zero, zero))
        gacc[row_gain:row_gain + 1, :] = jnp.sum(one, axis=0, keepdims=True)
        gacc[row_bias:row_bias + 1, :] = jnp.sum(two, axis=0, keepdims=True)

    def block(pair, k2, v2, at, bias):
        at_pair = tile_at(pair, 128)
        q2 = q[at, at_pair].astype(F32)
        d2 = dctx[at, at_pair].astype(F32)
        k2f = k2.astype(F32)
        dk = dv = dq = None
        for h in range(2):
            row = pl.ds(2 * pair + h, 1)
            qm = (q2 * masks[h]).astype(BF16)
            dm = (d2 * masks[h]).astype(BF16)
            km = (k2f * masks[h]).astype(BF16)
            s = dot_nt(k2, qm)
            if bias is not None:
                s = s + bias()
            p = jnp.exp(s - lset[row, at])
            dp = dot_nt(v2, dm)
            ds = (p * (dp - delta[row, at])).astype(BF16)
            ak, av, aq = dot(ds, qm), dot(p.astype(BF16), dm), dot_tn(ds, km)
            dk, dv, dq = (ak, av, aq) if dk is None else (dk + ak, dv + av, dq + aq)
        return dk, dv, dq

    everyone = slice(0, rows)

    def kv_copy(i):
        region = xda.at[i]
        return pltpu.make_async_remote_copy(
            src_ref=region, dst_ref=region, send_sem=ksend.at[i], recv_sem=krecv.at[i],
            device_id=peers[i], device_id_type=MESH)

    def attend_remote(i):
        @pl.when(takes[i])
        def _():
            rows_of = tile_at(peers[i][0], group)

            def pair_step(pair):
                at_k, at_v = tile_at(pair, 128), tile_at(pair + pairs, 128)
                dk, dv, dq = block(pair, kv[rows_of, at_k], kv[rows_of, at_v], everyone, None)
                dkv[i, :, at_k] = rotary(dk, cosr[rows_of, :], -sinr[rows_of, :]).astype(BF16)
                dkv[i, :, at_v] = dv.astype(BF16)
                da[:, at_k] = da[:, at_k] + dq

            def away_tile(j):
                at = tile_at(j, 256)
                xda[i, :, at] = dot_nt(dkv[i], wq[at, width:3 * width]).astype(BF16)

            loop(pairs, pair_step)
            loop(width // 256, away_tile)

    def own_bias():
        key = blocks_of((group, share), 0)
        query = blocks_of((group, share), 1)
        return jnp.concatenate([block_bias(query, key, True), block_bias(query, key, False)], axis=1)

    def near_bias():
        same = blocks_of((share, share), 0) == blocks_of((share, share), 1)
        return jnp.where(same, 0.0, NEG).astype(F32)

    def attend_own(low, high):
        rows_of = tile_at(n, group)

        def pair_step(pair):
            at_k, at_v = tile_at(pair, 128), tile_at(pair + pairs, 128)
            dk, dv, dq = block(pair, kv[rows_of, at_k], kv[rows_of, at_v], everyone, own_bias)
            dqkv[share:, tile_at(pair + pairs, 128)] = rotary(dk, cosr[mine, :], -sinr[mine, :]).astype(BF16)
            dqkv[share:, tile_at(pair + 2 * pairs, 128)] = dv.astype(BF16)
            da[:, at_k] = da[:, at_k] + dq
            dk, dv, dq = block(pair, nkv[:, at_k], nkv[:, at_v], slice(0, share), near_bias)
            dqkv[:share, tile_at(pair + pairs, 128)] = rotary(dk, cosr[mine, :], -sinr[mine, :]).astype(BF16)
            dqkv[:share, tile_at(pair + 2 * pairs, 128)] = dv.astype(BF16)
            da[:share, at_k] = da[:share, at_k] + dq

        loop(high - low, lambda t: pair_step(t + low))

    pl.semaphore_wait(barrier, jnp.where(zdev.has_outer, 6, 5))

    def run(turn, slot):
        for word in PLAN.get((turn, slot), ()):
            r, act = every[int(word[0])][word[1]], word[2]
            if act == "3" and r.turn:
                every[r.turn - 1][word[1]].free_zb()
            {"1": r.p1, "2": r.p2, "s": r.p2s, "3": r.p3, "4": r.p4, "5": r.p5, "6": r.p6, "7": r.p7}[act]()

    for turn, layer in enumerate(order):
        last = turn == layers - 1
        after = lambda slot: run(turn, slot)

        def reuse(*names):
            if turn:
                for name in names:
                    every[turn - 1][name].free_grad()

        gain1, gain2 = par[2 * layer:2 * layer + 1, :], par[2 * layer + 1:2 * layer + 2, :]
        load = loads(layer)
        load[8].wait()
        transposed(dctx)
        to_bf16(db)
        da[...] = jnp.zeros_like(da)
        reuse("u", "d")

        def ff_step(j):
            slot = lax.rem(j, 2)
            for c in stream(layer, j, slot):
                c.wait()

            @pl.when(j + 1 < tiles)
            def _():
                for c in stream(layer, j + 1, 1 - slot):
                    c.start()

            dact = dot_nt(db[...], wd_s[slot])
            gd[tile_at(j, TILE), :] = dot_tn(act_s[slot], db[...]).astype(BF16)
            du = (dact * dg_s[slot].astype(F32)).astype(BF16)
            dg_s[slot] = du
            gu[:, tile_at(j, TILE)] = dot(at_[...], dg_s[slot]).astype(BF16)
            da[...] = da[...] + dot_nt(dg_s[slot], wu_s[slot])

        for k in range(3):
            low, high = tiles * k // 3, tiles * (k + 1) // 3
            loop(high - low, lambda j: ff_step(j + low))
            after("ffn%d" % k)
        load[0].wait()
        norm_back(mid, gain2, 2 * layer + 1, 2 * layers + 2 * layer + 1)
        if layer:
            load_h(layer).start()
        after("lnb")
        to_bf16(db)
        after("bf")
        load[1].wait()
        load[6].wait()
        reuse("o")

        def out_tile(j):
            at = tile_at(j, 256)
            go[:, at] = dot_tn(ctx[...], db[:, at]).astype(BF16)
            dctx[:, at] = dot_nt(db[...], wo[at, :]).astype(BF16)

        loop(width // 256, out_tile)
        after("out")
        if layer == 0:
            load_h(layer).start()
        load[5].wait()

        def delta_step(pair):
            at = tile_at(pair, 128)
            both = (dctx[:, at].astype(F32) * ctx[:, at].astype(F32)).T
            for h in range(2):
                delta[pl.ds(2 * pair + h, 1), :] = jnp.sum(both[64 * h:64 * h + 64], axis=0, keepdims=True)

        loop(pairs, delta_step)
        for c in load_first(layer):
            c.start()
        for i in range(3):
            @pl.when(takes[i])
            def _():
                load_far(layer, i).start()
        da[...] = jnp.zeros_like(da)
        after("delta")
        for k in (2, 3, 4, 7):
            load[k].wait()
        for i in (2, 1, 0):
            if turn:
                @pl.when(takes[i])
                def _():
                    kv_copy(i).wait_send()
            attend_remote(i)
            after("rem%d" % i)

            @pl.when(takes[i])
            def _():
                if turn:
                    pl.semaphore_wait(kcredit.at[i], 1)
                kv_copy(i).start()
            after("send%d" % i)
        attend_own(0, pairs // 2)
        after("own0")
        attend_own(pairs // 2, pairs)
        after("own1")
        for c in load_first(layer):
            c.wait()
        transposed(ctx)
        after("tr")

        def query_tile(t):
            v = da[:, tile_at(t, 128)] * 0.125
            dqkv[:, tile_at(t, 128)] = rotary_halves(v, cosr[mine, :], -sinr[mine, :]).astype(BF16)

        loop(pairs, query_tile)
        after("q")
        reuse("q")

        def grad_tile(j):
            at = tile_at(j, 256)
            grads["q"][:, at] = dot(at_[...], dqkv[:, at]).astype(BF16)

        loop(width // 256, grad_tile)
        after("gq")
        for i in range(3):
            @pl.when(takes[i])
            def _():
                load_far(layer, i).wait()

        def grad_tile_kv(j, skip, out):
            acc[...] = dot(at_[...], dqkv[:, tile_at(j + (1 + skip) * (width // 256), 256)])
            for i in range(3):
                @pl.when(takes[i])
                def _():
                    acc[...] = acc[...] + dot_tn(far[i], dkv[i, :, tile_at(j + skip * (width // 256), 256)])
            out[:, tile_at(j, 256)] = acc[...].astype(BF16)

        for k, name in enumerate("kv"):
            reuse(name)
            loop(width // 256, lambda j: grad_tile_kv(j, k, grads[name]))
            after("g" + name)

        def first_tile(j):
            at = tile_at(j, 256)
            da[:, at] = dot_nt(dqkv[...], wq[at, :])

        loop(width // 256, first_tile)
        after("da")
        load_h(layer).wait()
        entry = mid if layer else db
        for i in range(3):
            @pl.when(gives[i])
            def _():
                kv_copy(i).wait_recv()
                da[share:, :] = da[share:, :] + xda[i].astype(F32)
                if not last:
                    pl.semaphore_signal(kcredit.at[i], inc=1, device_id=peers[i], device_id_type=MESH)
        after("kvwait")
        norm_back(entry, gain1, 2 * layer, 2 * layers + 2 * layer)
        if not last:
            for c in stream(order[turn + 1], 0, 0):
                c.start()
            for c in loads(order[turn + 1]):
                c.start()
        after("lna")

    tot = SmallSum(here, gacc, sbuf, ssend, srecv)
    tot.begin()
    to_bf16(grad_tok)
    run(9, "tot0")
    tot.swap(0)
    run(9, "tot1")
    tot.swap(1)
    run(9, "tot2")
    tot.swap(2)
    run(9, "tot3")
    tot.chain()
    run(9, "tot4")
    tot.settle()
    tot.finish()
    part = width // 4
    for owner in range(4):
        @pl.when(n == owner)
        def _():
            cut = sbuf[0, 5, :, owner * part:(owner + 1) * part]
            for layer in range(layers):
                out_gain[layer] = cut[2 * layer:2 * layer + 2]
                row = 2 * layers + 2 * layer
                out_first[layer:layer + 1] = cut[row:row + 1]
                out_second[layer:layer + 1] = cut[row + 1:row + 2]
    for turn in every:
        for r in turn.values():
            r.p8()
    for r in every[-1].values():
        r.free_grad()
        r.free_zb()
    for i in range(3):
        @pl.when(takes[i])
        def _():
            kv_copy(i).wait_send()


def backward(lengths, cot, tok, par, tabs, full, kept):
    cosr, sinr = tabs
    rows, width = cot.shape
    share = rows // 2
    layers = full[0].shape[0]
    ff = full[2].shape[2]
    hbm = pl.BlockSpec(memory_space=pltpu.HBM)
    vmem = pl.BlockSpec(memory_space=pltpu.VMEM)
    shape = jax.ShapeDtypeStruct
    v = pltpu.VMEM
    dma, regular = pltpu.SemaphoreType.DMA, pltpu.SemaphoreType.REGULAR
    outs = [shape((layers, f.shape[1] // 4, f.shape[2]), BF16) for f in full]
    part = width // 4
    small = [shape((layers, 2, part), F32), shape((layers, part), F32), shape((layers, part), F32)]
    kinds = [(width, width)] * 4 + [(width, ff), (ff, width)]
    scratch = [v(k, BF16) for k in kinds] + [v((width // 2, ff), BF16), v((ff // 2, width), BF16)]
    for total, cols in kinds:
        quarter = total // 16
        scratch += [v((4 * quarter, cols), BF16), v((2 * quarter, cols), BF16),
                    v((2 * quarter, cols), BF16), v((quarter, cols), BF16), v((2 * quarter, cols), BF16)]
    scratch += [
        v((2, TILE, width), BF16), v((2, width, TILE), BF16), v((2, rows, TILE), BF16), v((2, rows, TILE), BF16),
        v((width, width), BF16), v((width, 3 * width), BF16),
        v((rows, width), F32), v((rows, width), F32), v((rows, width), F32),
        v((width, rows), BF16), v((rows, width), BF16),
        v((rows, width), BF16), v((4 * share, 2 * width), BF16), v((share, 2 * width), BF16),
        v((rows, width), BF16), v((rows, width), BF16),
        v((16, rows), F32), v((16, rows), F32),
        v((rows, 3 * width), BF16), v((3, share, 2 * width), BF16), v((3, share, width), BF16),
        v((3, share, width), BF16), v((width, 256), F32),
        v(par.shape, F32), v((2, 6) + par.shape, F32),
        dma((SLOTS * 6 * layers,)), dma((SLOTS * 6 * layers,)), regular((7 * 6,)), regular((8,)), dma((6 * layers,)),
        dma((3,)), dma((3,)), regular((3,)), dma((2, 4)), dma((16,)), dma((6,)), dma((6,)),
    ]
    return pl.pallas_call(
        partial(backward_kernel, layers),
        out_shape=[shape((rows, width), BF16)] + outs + small,
        in_specs=[pl.BlockSpec(memory_space=pltpu.SMEM)] + [hbm] * 2 + [vmem] * 3 + [hbm] * 16,
        out_specs=[vmem] + [hbm] * 4 + [vmem] * 3,
        scratch_shapes=scratch,
        compiler_params=pltpu.CompilerParams(
            collective_id=1, has_side_effects=True, vmem_limit_bytes=63 * 2**20),
        cost_estimate=pl.CostEstimate(flops=40 * 10**9, bytes_accessed=10**8, transcendentals=10**7),
        name="backward",
    )(lengths, cot, tok, par, cosr, sinr, *full, *kept)


def shared_params(norm_gains, norm_biases):
    layers, _, part = norm_gains.shape
    mine = jnp.concatenate([norm_gains.reshape(2 * layers, part), norm_biases.reshape(2 * layers, part)]).astype(F32)
    parts = lax.axis_size("narrow")
    owner = jnp.arange(parts) == lax.axis_index("narrow")
    return jnp.where(owner[None, :, None], mine[:, None, :], 0.0).reshape(4 * layers, parts * part)


def rotary_tables(seq, head_dim):
    half = head_dim // 2
    freq = np.exp(-np.log(np.float32(10000.0)) * np.arange(half, dtype=np.float32) * np.float32(2.0) / np.float32(head_dim))
    angle = np.arange(seq, dtype=np.float32)[:, None] * freq.astype(np.float32)[None, :]
    cosine, sine = np.cos(angle), np.sin(angle)
    return (jnp.asarray(np.tile(cosine, (1, 4)), F32),
            jnp.asarray(np.tile(np.concatenate([-sine, sine], axis=1), (1, 2)), F32))


def settle_kernel(*refs):
    half = len(refs) // 2
    for src, dst in zip(refs[:half], refs[half:]):
        dst[...] = src[...].astype(dst.dtype)


def settle(grads, rows, small):
    layers = grads[0].shape[0]
    halves = 4
    cut = lambda a: pl.BlockSpec((1, a.shape[1] // halves, a.shape[2]), lambda i, j: (i, j, 0))
    strip = lambda a: pl.BlockSpec((a.shape[0] // (layers * halves), a.shape[1]), lambda i, j: (i * halves + j, 0))
    whole = lambda a: pl.BlockSpec(a.shape, lambda i, j: (0,) * a.ndim)
    specs = [cut(a) for a in grads] + [strip(a) for a in rows] + [whole(a) for a in small]
    shape = jax.ShapeDtypeStruct
    outs = [shape(a.shape, F32) for a in grads] + [shape(a.shape, a.dtype) for a in (*rows, *small)]
    return pl.pallas_call(
        settle_kernel,
        grid=(layers, halves),
        out_shape=outs,
        in_specs=specs,
        out_specs=specs,
        compiler_params=pltpu.CompilerParams(vmem_limit_bytes=62 * 2**20),
        name="settle",
    )(*grads, *rows, *small)


def on_device(tokens, lengths, w_qkv, w_out, w_up, w_down, norm_gains, norm_biases, cotangent):
    _, _, share, width = tokens.shape
    tok = tokens.reshape(2 * share, width)
    tabs = rotary_tables(4 * share, width // H)
    outs = forward(tok, shared_params(norm_gains, norm_biases), *tabs, w_qkv, w_out, w_up, w_down)
    result, full, par, kept = outs[0], outs[1:5], outs[5], outs[6:]
    grad_tok, gq, go, gu, gd, gains, first, second = backward(
        lengths, cotangent.reshape(2 * share, width), tok, par, tabs, full, kept)
    gq, go, gu, gd, result, grad_tok, gains, first, second = settle(
        (gq, go, gu, gd), (result, grad_tok), (gains, first, second))
    return (
        result.reshape(tokens.shape), grad_tok.reshape(tokens.shape), gq, go, gu, gd, gains, first, second)


def solution(mesh):
    return jax.shard_map(
        on_device,
        mesh=mesh,
        in_specs=(
            P("wide", None, "narrow", None),
            P("wide"),
            P(None, "narrow", None),
            P(None, "narrow", None),
            P(None, "narrow", None),
            P(None, "narrow", None),
            P(None, None, "narrow"),
            P(None, None, "narrow"),
            P("wide", None, "narrow", None),
        ),
        out_specs=(
            P("wide", None, "narrow", None),
            P("wide", None, "narrow", None),
            P(None, "narrow", None),
            P(None, "narrow", None),
            P(None, "narrow", None),
            P(None, "narrow", None),
            P(None, None, "narrow"),
            P(None, "narrow"),
            P(None, "narrow"),
        ),
        check_vma=False,
    )
```
